32 devices in a mesh: gz: 8 (over z, y), gy: 4 (over x, core).
Axes of the slice: x: 2, y: 2, z: 4, core: 2. Of those that a mesh axis runs over, the one named last changes fastest.
Arguments:
- level_input: bfloat16 [8, 32, 64, 128], P('gz', 'gy'), may hold values from -6 to 6
- pre_activation: bfloat16 [8, 32, 64, 128], P('gz', 'gy'), may hold values from -6 to 6
- conv_weight: bfloat16 [3, 3, 3, 128, 128], replicated, may hold values from -0.109375 to 0.109375
- down_weight: bfloat16 [2, 2, 2, 128, 256], replicated, may hold values from -0.1875 to 0.1875
- skip_cotangent: bfloat16 [8, 32, 64, 128], P('gz', 'gy'), may hold values from -12 to 12
- deep_cotangent: bfloat16 [4, 16, 32, 256], P(None, 'gy', None, 'gz'), may hold values from -12 to 12
Outputs:
- input_grad: bfloat16 [8, 32, 64, 128], P('gz', 'gy')
- conv_weight_grad: bfloat16 [3, 3, 3, 128, 128], replicated
- down_weight_grad: bfloat16 [2, 2, 2, 128, 256], replicated
The draws below stay inside these ranges and needn't reach their ends.
All inputs are finite; a program needn't handle non-finite values.
Results may differ from the reference program's by a relative error of at most 0.0054.
Values may be sent and summed in bfloat16 or wider, within the bound.
No kernel may reach another device: no remote copies, remote signals or barrier semaphores. Data moves between devices by JAX's collectives and lax.ppermute only.
A program may use at most 64 MiB of HBM per device.

```python
import math
import jax
import jax.numpy as jnp
from jax import lax

C2 = 128
C3 = 256
X2 = 64
Z2 = 8
Y2 = 32
Z3 = 4
Y3 = 16
X3 = 32


def rising(count):
    return jnp.exp(jnp.log(3.0) * jnp.arange(count, dtype=jnp.float32) / max(count - 1, 1))


def scaled_draw(key, shape):
    values = jnp.clip(jax.random.normal(key, shape, jnp.float32), -4.0, 4.0)
    return values * rising(shape[0])[:, None, None, None]


def draw_skip_cotangent(key, part):
    return scaled_draw(key, (Z2, Y2, X2, C2)).astype(jnp.bfloat16)


def draw_deep_cotangent(key, part):
    return scaled_draw(jax.random.fold_in(key, 3), (Z3, Y3, X3, C3)).astype(jnp.bfloat16)


def block_scale(stream_key, dims, pieces, least, largest):
    def one(dim, blocks):
        steps = jax.random.uniform(jax.random.fold_in(jax.random.fold_in(stream_key, 6), dim), (blocks,), jnp.float32, least / len(pieces), largest / len(pieces))
        return jnp.repeat(jnp.exp(steps), dims[dim] // blocks).reshape((-1,) + (1,) * (len(dims) - dim - 1))

    gain = one(*pieces[0])
    for cut in pieces[1:]:
        gain = gain * one(*cut)
    return gain


def noise(stream_key, shape, deviation, bound, cuts=(), kind=jnp.bfloat16):
    values = deviation * jax.random.normal(stream_key, shape, jnp.float32)
    if cuts:
        values = values * block_scale(stream_key, shape, cuts, -0.22, 0.18)
    return jnp.clip(values, -bound, bound).astype(kind)


def setup_inputs(seed: int = 0) -> dict:
    keys = jax.random.split(jax.random.key(seed), 7)
    return {
        "level_input": noise(keys[0], (Z2, Y2, X2, C2), 1.0, 6.0, ((0, 8), (1, 4))),
        "pre_activation": noise(keys[1], (Z2, Y2, X2, C2), 1.0, 6.0, ((0, 8), (1, 4))),
        "conv_weight": noise(keys[2], (3, 3, 3, C2, C2), (27 * C2) ** -0.5, 0.109375),
        "down_weight": noise(keys[3], (2, 2, 2, C2, C3), (8 * C2) ** -0.5, 0.1875),
        "skip_cotangent": draw_skip_cotangent(jax.random.fold_in(keys[6], 71), 0),
        "deep_cotangent": draw_deep_cotangent(jax.random.fold_in(keys[6], 71), 0),
    }


def convolve(batched, kernel):
    return lax.conv_general_dilated(batched, kernel, (1, 1, 1), [(1, 1), (1, 1), (1, 1)], dimension_numbers=('NDHWC', 'DHWIO', 'NDHWC'), precision=lax.Precision.HIGHEST)

def reference(level_input, pre_activation, conv_weight, down_weight, skip_cotangent, deep_cotangent):
    weight_down = down_weight.astype(jnp.float32)

    def spread_plane(plane):
        result = jnp.einsum('yxo,abcio->aybxci', plane.astype(jnp.float32), weight_down)
        return result.reshape(2, Y2, X2, C2)
    down_part = lax.map(spread_plane, deep_cotangent).reshape(Z2, Y2, X2, C2)
    hidden_grad = down_part + skip_cotangent.astype(jnp.float32)
    masked_grad = jnp.where(pre_activation > 0, hidden_grad, jnp.zeros_like(hidden_grad)).astype(jnp.bfloat16)
    hidden = jnp.maximum(pre_activation, jnp.zeros_like(pre_activation))
    blocks = hidden.astype(jnp.float32).reshape(Z3, 2, Y3, 2, X3, 2, C2)
    down_sum = jnp.einsum('zaybxci,zyxo->abcio', blocks, deep_cotangent.astype(jnp.float32))
    down_weight_grad = (down_sum / math.sqrt(Z3 * Y3 * X3)).astype(jnp.bfloat16)
    batched = level_input.astype(jnp.float32)[None]
    outputs, pullback = jax.vjp(convolve, batched, conv_weight.astype(jnp.float32))
    input_total, conv_total = pullback(masked_grad.astype(jnp.float32)[None])
    input_grad = input_total[0].astype(jnp.bfloat16)
    conv_weight_grad = (conv_total / math.sqrt(Z2 * Y2 * X2)).astype(jnp.bfloat16)
    return (input_grad, conv_weight_grad, down_weight_grad)
```

```python
import math

import jax
import jax.numpy as jnp
from jax import lax
from jax.experimental import pallas as pl
from jax.experimental.pallas import tpu as pltpu
from jax.sharding import PartitionSpec as P

F32 = jnp.float32
BF16 = jnp.bfloat16
VMEM_LIMIT = 40 * 1024 * 1024


def call(kernel, out_shape, *operands, scratch=()):
    return pl.pallas_call(
        kernel,
        out_shape=out_shape,
        scratch_shapes=list(scratch),
        compiler_params=pltpu.CompilerParams(vmem_limit_bytes=VMEM_LIMIT),
    )(*operands)


def shifted(cells, step):
    if step == 0:
        return cells
    cols = cells.shape[1]
    moved = pltpu.roll(cells, step % cols, 1)
    col = lax.broadcasted_iota(jnp.int32, cells.shape, 1)
    keep = col >= step if step > 0 else col < cols + step
    return jnp.where(keep, moved, 0.0)


def fill_padded(padded, own, z_low, z_high, y_low, y_high):
    rows = own.shape[0]
    for plane, ref in enumerate((z_low, own, z_high)):
        padded[plane, pl.ds(1, rows)] = ref[...]
        padded[plane, 0] = y_low[plane]
        padded[plane, rows + 1] = y_high[plane]


def mask_kernel(pre, skip, deep_t, weight, grad, down):
    rows, cols, channels = pre.shape
    half = rows // 2
    deep_cols = cols // 2
    cells = half * cols
    deep_cells = half * deep_cols
    wide = lax.broadcasted_iota(jnp.int32, (deep_cells, cells), 1) // 2
    deep = lax.broadcasted_iota(jnp.int32, (deep_cells, cells), 0)
    repeat = (wide == deep).astype(BF16)
    spread = jnp.dot(deep_t[...], repeat, preferred_element_type=F32).astype(BF16)
    col = lax.broadcasted_iota(jnp.int32, (cells, channels), 0) % 2
    for b in range(2):
        parts = [
            lax.dot_general(
                spread, weight[b, c], (((0,), (1,)), ((), ())), preferred_element_type=F32
            )
            for c in range(2)
        ]
        part = jnp.where(col == 0, parts[0], parts[1]).reshape(half, cols, channels)
        for y in range(half):
            row = 2 * y + b
            pre_row = pre[row].astype(F32)
            total = part[y] + skip[row].astype(F32)
            grad[row] = jnp.where(pre_row > 0, total, 0.0).astype(BF16)
        hidden = jnp.concatenate(
            [jnp.maximum(pre[2 * y + b].astype(F32), 0.0) for y in range(half)], axis=0
        )
        for c in range(2):
            one = jnp.where(col == c, hidden, 0.0).astype(BF16)
            down[b, c] = lax.dot_general(
                one, spread, (((0,), (1,)), ((), ())), preferred_element_type=F32
            ).astype(BF16)


def weight_kernel(n_gy, n_gz, conv_rows, down_rows, own, z_low, z_high, y_low, y_high, grad, down, out, padded):
    rows, cols, channels = own.shape
    fill_padded(padded, own, z_low, z_high, y_low, y_high)
    grads = grad[...].astype(F32)
    shifts = jnp.concatenate(
        [shifted(grads, kx - 1).astype(BF16).reshape(rows * cols, channels) for kx in range(3)],
        axis=1,
    )

    def store(base, piece, row, value):
        done = 0
        while done < value.shape[0]:
            owner, inner = divmod(row + done, piece)
            take = min(piece - inner, value.shape[0] - done)
            out[owner // n_gz, owner % n_gz, pl.ds(base + inner, take)] = value[done : done + take]
            done += take

    for kz in range(3):
        for ky in range(3):
            slab = padded[kz, pl.ds(ky, rows)].reshape(rows * cols, channels)
            total = lax.dot_general(
                slab, shifts, (((0,), (0,)), ((), ())), preferred_element_type=F32
            ).astype(BF16)
            for kx in range(3):
                index = (kz * 3 + ky) * 3 + kx
                store(0, conv_rows, index * channels, total[:, kx * channels : (kx + 1) * channels])
    blank = n_gy * n_gz * conv_rows - 27 * channels
    if blank:
        store(0, conv_rows, 27 * channels, jnp.zeros((blank, channels), BF16))
    wide = down.shape[3] // channels
    count = 4 * channels
    for part in range(wide):
        for b in range(2):
            for c in range(2):
                row = part * count + (b * 2 + c) * channels
                store(conv_rows, down_rows, row, down[b, c, :, part * channels : (part + 1) * channels])
    blank = n_gy * n_gz * down_rows - wide * count
    if blank:
        store(conv_rows, down_rows, wide * count, jnp.zeros((blank, channels), BF16))


def input_kernel(own, z_low, z_high, y_low, y_high, weight, out, padded):
    rows, cols, channels = own.shape
    fill_padded(padded, own, z_low, z_high, y_low, y_high)
    total = None
    for kz in range(3):
        for ky in range(3):
            slab = padded[2 - kz, pl.ds(2 - ky, rows)].reshape(rows * cols, channels)
            term = lax.dot_general(
                slab,
                weight[kz, ky].reshape(3 * channels, channels),
                (((1,), (1,)), ((), ())),
                preferred_element_type=F32,
            )
            total = term if total is None else total + term
    answer = None
    for kx in range(3):
        part = total[:, kx * channels : (kx + 1) * channels].reshape(rows, cols, channels)
        part = shifted(part, kx - 1)
        answer = part if answer is None else answer + part
    out[...] = answer.astype(BF16)


def spread_kernel(n_gy, n_gz, conv_rows, down_rows, gathered, conv, down):
    rows, channels = conv.shape
    wide = down.shape[2] // channels
    for owner in range(n_gy * n_gz):
        piece = gathered.at[owner]
        first = owner * conv_rows
        take = min(conv_rows, rows - first)
        if take > 0:
            conv[pl.ds(first, take)] = piece[pl.ds(0, take)]
        first = owner * down_rows
        count = down.shape[1]
        done = 0
        while done < down_rows and first + done < wide * count:
            part, row = divmod(first + done, count)
            take = min(count - row, down_rows - done)
            for a in range(2):
                down[a, pl.ds(row, take), pl.ds(part * channels, channels)] = piece[
                    pl.ds(conv_rows + a * down_rows + done, take)
                ]
            done += take


def sides(cells, gz, gy):
    def moved(value, axis, count, up):
        pairs = [(i, i + 1) if up else (i + 1, i) for i in range(count - 1)]
        return lax.ppermute(value, axis, pairs)

    z_low = moved(cells, "gz", gz, True)
    z_high = moved(cells, "gz", gz, False)
    planes = (z_low, cells, z_high)
    y_low = moved(jnp.stack([plane[-1] for plane in planes]), "gy", gy, True)
    y_high = moved(jnp.stack([plane[0] for plane in planes]), "gy", gy, False)
    return cells, z_low, z_high, y_low, y_high


def per_device(
    level_input, pre_activation, conv_weight, down_weight, skip_cotangent, deep_cotangent
):
    n_gz = lax.axis_size("gz")
    n_gy = lax.axis_size("gy")
    _, rows, cols, channels = level_input.shape
    planes, deep_rows, deep_cols, share = deep_cotangent.shape
    deep_channels = down_weight.shape[4]
    parity = lax.axis_index("gz") % 2
    devices = n_gz * n_gy
    conv_rows = -(-27 * channels // (devices * 16)) * 16
    down_count = 4 * channels * deep_channels // channels
    down_rows = -(-down_count // (devices * 16)) * 16

    deep_t = jnp.swapaxes(deep_cotangent.reshape(planes, deep_rows * deep_cols, share), 1, 2)
    deep_t = jnp.broadcast_to(deep_t[:, None], (planes, 2) + deep_t.shape[1:])
    deep_t = deep_t.reshape(2 * planes, share, deep_rows * deep_cols)
    deep_t = lax.all_to_all(deep_t, "gz", split_axis=0, concat_axis=0, tiled=True)
    deep_t = deep_t.reshape(deep_channels, deep_rows * deep_cols)
    level = sides(level_input[0], n_gz, n_gy)
    down_slice = lax.dynamic_index_in_dim(down_weight, parity, 0, keepdims=False)

    shape = jax.ShapeDtypeStruct
    grad, down = call(
        mask_kernel,
        (
            shape((rows, cols, channels), BF16),
            shape((2, 2, channels, deep_channels), BF16),
        ),
        pre_activation[0],
        skip_cotangent[0],
        deep_t,
        down_slice,
    )

    piece = conv_rows + down_rows
    parts = call(
        lambda *refs: weight_kernel(n_gy, n_gz, conv_rows, down_rows, *refs),
        shape((n_gy, n_gz, piece, channels), BF16),
        *level,
        grad,
        down,
        scratch=[pltpu.VMEM((3, rows + 2, cols, channels), BF16)],
    )
    parts = lax.all_to_all(parts, "gy", split_axis=0, concat_axis=0, tiled=True)
    parts = jnp.sum(parts.astype(F32), axis=0).astype(BF16)
    parts = lax.all_to_all(parts, "gz", split_axis=0, concat_axis=0, tiled=True)
    parts = parts.astype(F32)
    cell_total = devices * rows * cols
    conv_sum = jnp.sum(parts[:, :conv_rows], axis=0) / math.sqrt(cell_total)
    slots = parts[:, conv_rows:].reshape(n_gz // 2, 2, down_rows, channels)
    down_sum = jnp.sum(slots, axis=0) / math.sqrt(cell_total // 8)
    final = jnp.concatenate([conv_sum, down_sum.reshape(2 * down_rows, channels)], axis=0)
    final = final.astype(BF16)
    gathered = lax.all_gather(final, ("gy", "gz"), axis=0, tiled=False)
    conv_grad, down_grad = call(
        lambda *refs: spread_kernel(n_gy, n_gz, conv_rows, down_rows, *refs),
        (
            shape((27 * channels, channels), BF16),
            shape((2, 4 * channels, deep_channels), BF16),
        ),
        gathered,
    )

    halo = sides(grad, n_gz, n_gy)
    input_grad = call(
        input_kernel,
        shape((rows, cols, channels), BF16),
        *halo,
        conv_weight,
        scratch=[pltpu.VMEM((3, rows + 2, cols, channels), BF16)],
    )
    return (
        input_grad[None],
        conv_grad.reshape(conv_weight.shape),
        down_grad.reshape(down_weight.shape),
    )


def solution(mesh):
    return jax.shard_map(
        per_device,
        mesh=mesh,
        in_specs=(
            P("gz", "gy", None, None),
            P("gz", "gy", None, None),
            P(),
            P(),
            P("gz", "gy", None, None),
            P(None, "gy", None, "gz"),
        ),
        out_specs=(P("gz", "gy", None, None), P(), P()),
        check_vma=False,
    )
```

```python
import math

import jax
import jax.numpy as jnp
from jax import lax
from jax.experimental import pallas as pl
from jax.experimental.pallas import tpu as pltpu
from jax.sharding import PartitionSpec as P

F32 = jnp.float32
BF16 = jnp.bfloat16
VMEM_LIMIT = 40 * 1024 * 1024


def call(kernel, out_shape, *operands, scratch=()):
    return pl.pallas_call(
        kernel,
        out_shape=out_shape,
        scratch_shapes=list(scratch),
        compiler_params=pltpu.CompilerParams(vmem_limit_bytes=VMEM_LIMIT),
    )(*operands)


def shifted(cells, step):
    if step == 0:
        return cells
    cols = cells.shape[1]
    moved = pltpu.roll(cells, step % cols, 1)
    col = lax.broadcasted_iota(jnp.int32, cells.shape, 1)
    keep = col >= step if step > 0 else col < cols + step
    return jnp.where(keep, moved, 0.0)


def mask_kernel(pre, skip, deep_t, weight, grad, down):
    rows, cols, channels = pre.shape
    half = rows // 2
    deep_cols = cols // 2
    cells = half * cols
    deep_cells = half * deep_cols
    wide = lax.broadcasted_iota(jnp.int32, (deep_cells, cells), 1) // 2
    deep = lax.broadcasted_iota(jnp.int32, (deep_cells, cells), 0)
    repeat = (wide == deep).astype(BF16)
    spread = jnp.dot(deep_t[...], repeat, preferred_element_type=F32).astype(BF16)
    col = lax.broadcasted_iota(jnp.int32, (cells, channels), 0) % 2
    for b in range(2):
        parts = [
            lax.dot_general(
                spread, weight[b, c], (((0,), (1,)), ((), ())), preferred_element_type=F32
            )
            for c in range(2)
        ]
        part = jnp.where(col == 0, parts[0], parts[1]).reshape(half, cols, channels)
        for y in range(half):
            row = 2 * y + b
            pre_row = pre[row].astype(F32)
            total = part[y] + skip[row].astype(F32)
            grad[row] = jnp.where(pre_row > 0, total, 0.0).astype(BF16)
        hidden = jnp.concatenate(
            [jnp.maximum(pre[2 * y + b].astype(F32), 0.0) for y in range(half)], axis=0
        )
        for c in range(2):
            one = jnp.where(col == c, hidden, 0.0).astype(BF16)
            down[b, c] = lax.dot_general(
                one, spread, (((0,), (1,)), ((), ())), preferred_element_type=F32
            ).astype(BF16)


def slabs(planes, rows):
    cols, channels = planes[0].shape[1:]
    pieces = [
        planes[2 - kz][pl.ds(2 - ky, rows)].reshape(rows * cols, channels)
        for kz in range(3)
        for ky in range(3)
    ]
    return jnp.concatenate(pieces, axis=1)


def weight_kernel(n_gy, n_gz, conv_rows, down_rows, level, z_low, own, z_high, down, out):
    rows, cols, channels = level.shape
    cells = level[...].astype(F32)
    shifts = jnp.concatenate(
        [shifted(cells, 1 - kx).reshape(rows * cols, channels) for kx in range(3)], axis=1
    ).T.astype(BF16)

    def store(base, piece, row, value):
        done = 0
        while done < value.shape[0]:
            owner, inner = divmod(row + done, piece)
            take = min(piece - inner, value.shape[0] - done)
            out[owner // n_gz, owner % n_gz, pl.ds(base + inner, take)] = value[done : done + take]
            done += take

    total = jnp.dot(shifts, slabs((z_low, own, z_high), rows), preferred_element_type=F32)
    total = total.astype(BF16)
    for index in range(9):
        store(
            0,
            conv_rows,
            index * 3 * channels,
            total[:, index * channels : (index + 1) * channels],
        )
    blank = n_gy * n_gz * conv_rows - 27 * channels
    if blank:
        store(0, conv_rows, 27 * channels, jnp.zeros((blank, channels), BF16))
    wide = down.shape[3] // channels
    count = 4 * channels
    for part in range(wide):
        for b in range(2):
            for c in range(2):
                row = part * count + (b * 2 + c) * channels
                store(conv_rows, down_rows, row, down[b, c, :, part * channels : (part + 1) * channels])
    blank = n_gy * n_gz * down_rows - wide * count
    if blank:
        store(conv_rows, down_rows, wide * count, jnp.zeros((blank, channels), BF16))


def input_kernel(z_low, own, z_high, weight, out):
    rows, cols, channels = out.shape
    stacked = slabs((z_low, own, z_high), rows)
    total = None
    for index in range(9):
        term = lax.dot_general(
            stacked[:, index * channels : (index + 1) * channels],
            weight[index // 3, index % 3].reshape(3 * channels, channels),
            (((1,), (1,)), ((), ())),
            preferred_element_type=F32,
        )
        total = term if total is None else total + term
    answer = None
    for kx in range(3):
        part = total[:, kx * channels : (kx + 1) * channels].reshape(rows, cols, channels)
        part = shifted(part, kx - 1)
        answer = part if answer is None else answer + part
    out[...] = answer.astype(BF16)


def spread_kernel(n_gy, n_gz, conv_rows, down_rows, gathered, conv, down):
    rows, channels = conv.shape
    wide = down.shape[2] // channels
    for owner in range(n_gy * n_gz):
        piece = gathered.at[owner]
        first = owner * conv_rows
        take = min(conv_rows, rows - first)
        if take > 0:
            conv[pl.ds(first, take)] = piece[pl.ds(0, take)]
        first = owner * down_rows
        count = down.shape[1]
        done = 0
        while done < down_rows and first + done < wide * count:
            part, row = divmod(first + done, count)
            take = min(count - row, down_rows - done)
            for a in range(2):
                down[a, pl.ds(row, take), pl.ds(part * channels, channels)] = piece[
                    pl.ds(conv_rows + a * down_rows + done, take)
                ]
            done += take


def padded(cells, gz, gy):
    def moved(value, axis, count, up):
        pairs = [(i, i + 1) if up else (i + 1, i) for i in range(count - 1)]
        return lax.ppermute(value, axis, pairs)

    y_low = moved(cells[-1:], "gy", gy, True)
    y_high = moved(cells[:1], "gy", gy, False)
    own = jnp.concatenate([y_low, cells, y_high], axis=0)
    return moved(own, "gz", gz, True), own, moved(own, "gz", gz, False)


def per_device(
    level_input, pre_activation, conv_weight, down_weight, skip_cotangent, deep_cotangent
):
    n_gz = lax.axis_size("gz")
    n_gy = lax.axis_size("gy")
    _, rows, cols, channels = level_input.shape
    planes, deep_rows, deep_cols, share = deep_cotangent.shape
    deep_channels = down_weight.shape[4]
    parity = lax.axis_index("gz") % 2
    devices = n_gz * n_gy
    conv_rows = -(-27 * channels // (devices * 16)) * 16
    down_count = 4 * channels * deep_channels // channels
    down_rows = -(-down_count // (devices * 16)) * 16

    deep_t = jnp.swapaxes(deep_cotangent.reshape(planes, deep_rows * deep_cols, share), 1, 2)
    deep_t = jnp.broadcast_to(deep_t[:, None], (planes, 2) + deep_t.shape[1:])
    deep_t = deep_t.reshape(2 * planes, share, deep_rows * deep_cols)
    deep_t = lax.all_to_all(deep_t, "gz", split_axis=0, concat_axis=0, tiled=True)
    deep_t = deep_t.reshape(deep_channels, deep_rows * deep_cols)
    down_slice = lax.dynamic_index_in_dim(down_weight, parity, 0, keepdims=False)

    shape = jax.ShapeDtypeStruct
    grad, down = call(
        mask_kernel,
        (
            shape((rows, cols, channels), BF16),
            shape((2, 2, channels, deep_channels), BF16),
        ),
        pre_activation[0],
        skip_cotangent[0],
        deep_t,
        down_slice,
    )

    planes_near = padded(grad, n_gz, n_gy)
    piece = conv_rows + down_rows
    parts = call(
        lambda *refs: weight_kernel(n_gy, n_gz, conv_rows, down_rows, *refs),
        shape((n_gy, n_gz, piece, channels), BF16),
        level_input[0],
        *planes_near,
        down,
    )
    parts = lax.all_to_all(parts, "gy", split_axis=0, concat_axis=0, tiled=True)
    parts = jnp.sum(parts.astype(F32), axis=0).astype(BF16)
    parts = lax.all_to_all(parts, "gz", split_axis=0, concat_axis=0, tiled=True)
    parts = parts.astype(F32)
    cell_total = devices * rows * cols
    conv_sum = jnp.sum(parts[:, :conv_rows], axis=0) / math.sqrt(cell_total)
    slots = parts[:, conv_rows:].reshape(n_gz // 2, 2, down_rows, channels)
    down_sum = jnp.sum(slots, axis=0) / math.sqrt(cell_total // 8)
    final = jnp.concatenate([conv_sum, down_sum.reshape(2 * down_rows, channels)], axis=0)
    final = final.astype(BF16)
    gathered = lax.all_gather(final, "gz", axis=0, tiled=False)
    gathered = lax.all_gather(gathered, "gy", axis=0, tiled=False)
    gathered = gathered.reshape((devices,) + final.shape)
    conv_grad, down_grad = call(
        lambda *refs: spread_kernel(n_gy, n_gz, conv_rows, down_rows, *refs),
        (
            shape((27 * channels, channels), BF16),
            shape((2, 4 * channels, deep_channels), BF16),
        ),
        gathered,
    )

    input_grad = call(
        input_kernel,
        shape((rows, cols, channels), BF16),
        *planes_near,
        conv_weight,
    )
    return (
        input_grad[None],
        conv_grad.reshape(conv_weight.shape),
        down_grad.reshape(down_weight.shape),
    )


def solution(mesh):
    return jax.shard_map(
        per_device,
        mesh=mesh,
        in_specs=(
            P("gz", "gy", None, None),
            P("gz", "gy", None, None),
            P(),
            P(),
            P("gz", "gy", None, None),
            P(None, "gy", None, "gz"),
        ),
        out_specs=(P("gz", "gy", None, None), P(), P()),
        check_vma=False,
    )
```

```python
import math

import jax
import jax.numpy as jnp
from jax import lax
from jax.experimental import pallas as pl
from jax.experimental.pallas import tpu as pltpu
from jax.sharding import PartitionSpec as P

F32 = jnp.float32
BF16 = jnp.bfloat16
VMEM_LIMIT = 40 * 1024 * 1024


def call(kernel, out_shape, *operands, scratch=()):
    return pl.pallas_call(
        kernel,
        out_shape=out_shape,
        scratch_shapes=list(scratch),
        compiler_params=pltpu.CompilerParams(vmem_limit_bytes=VMEM_LIMIT),
    )(*operands)


def shifted(cells, step):
    if step == 0:
        return cells
    cols = cells.shape[1]
    moved = pltpu.roll(cells, step % cols, 1)
    col = lax.broadcasted_iota(jnp.int32, cells.shape, 1)
    keep = col >= step if step > 0 else col < cols + step
    return jnp.where(keep, moved, 0.0)


def fill_padded(padded, own, z_low, z_high, y_low, y_high):
    rows = own.shape[0]
    for plane, ref in enumerate((z_low, own, z_high)):
        padded[plane, pl.ds(1, rows)] = ref[...]
        padded[plane, 0] = y_low[plane]
        padded[plane, rows + 1] = y_high[plane]


def mask_kernel(pre, skip, deep_t, weight, grad, down):
    rows, cols, channels = pre.shape
    half = rows // 2
    deep_cols = cols // 2
    cells = half * cols
    deep_cells = half * deep_cols
    wide = lax.broadcasted_iota(jnp.int32, (deep_cells, cells), 1) // 2
    deep = lax.broadcasted_iota(jnp.int32, (deep_cells, cells), 0)
    repeat = (wide == deep).astype(BF16)
    spread = jnp.dot(deep_t[...], repeat, preferred_element_type=F32).astype(BF16)
    col = lax.broadcasted_iota(jnp.int32, (cells, channels), 0) % 2
    for b in range(2):
        parts = [
            lax.dot_general(
                spread, weight[b, c], (((0,), (1,)), ((), ())), preferred_element_type=F32
            )
            for c in range(2)
        ]
        part = jnp.where(col == 0, parts[0], parts[1]).reshape(half, cols, channels)
        for y in range(half):
            row = 2 * y + b
            pre_row = pre[row].astype(F32)
            total = part[y] + skip[row].astype(F32)
            grad[row] = jnp.where(pre_row > 0, total, 0.0).astype(BF16)
        hidden = jnp.concatenate(
            [jnp.maximum(pre[2 * y + b].astype(F32), 0.0) for y in range(half)], axis=0
        )
        for c in range(2):
            one = jnp.where(col == c, hidden, 0.0).astype(BF16)
            down[b, c] = lax.dot_general(
                one, spread, (((0,), (1,)), ((), ())), preferred_element_type=F32
            ).astype(BF16)


def weight_kernel(n_gy, n_gz, conv_rows, down_rows, own, z_low, z_high, y_low, y_high, grad, down, out, padded):
    rows, cols, channels = own.shape
    fill_padded(padded, own, z_low, z_high, y_low, y_high)
    grads = grad[...].astype(F32)
    shifts = jnp.concatenate(
        [shifted(grads, kx - 1).astype(BF16).reshape(rows * cols, channels) for kx in range(3)],
        axis=1,
    )

    def store(base, piece, row, value):
        done = 0
        while done < value.shape[0]:
            owner, inner = divmod(row + done, piece)
            take = min(piece - inner, value.shape[0] - done)
            out[owner // n_gz, owner % n_gz, pl.ds(base + inner, take)] = value[done : done + take]
            done += take

    for kz in range(3):
        for ky in range(3):
            slab = padded[kz, pl.ds(ky, rows)].reshape(rows * cols, channels)
            total = lax.dot_general(
                slab, shifts, (((0,), (0,)), ((), ())), preferred_element_type=F32
            ).astype(BF16)
            for kx in range(3):
                index = (kz * 3 + ky) * 3 + kx
                store(0, conv_rows, index * channels, total[:, kx * channels : (kx + 1) * channels])
    blank = n_gy * n_gz * conv_rows - 27 * channels
    if blank:
        store(0, conv_rows, 27 * channels, jnp.zeros((blank, channels), BF16))
    wide = down.shape[3] // channels
    count = 4 * channels
    for part in range(wide):
        for b in range(2):
            for c in range(2):
                row = part * count + (b * 2 + c) * channels
                store(conv_rows, down_rows, row, down[b, c, :, part * channels : (part + 1) * channels])
    blank = n_gy * n_gz * down_rows - wide * count
    if blank:
        store(conv_rows, down_rows, wide * count, jnp.zeros((blank, channels), BF16))


def input_kernel(own, z_low, z_high, y_low, y_high, weight, out, padded):
    rows, cols, channels = own.shape
    fill_padded(padded, own, z_low, z_high, y_low, y_high)
    total = None
    for kz in range(3):
        for ky in range(3):
            slab = padded[2 - kz, pl.ds(2 - ky, rows)].reshape(rows * cols, channels)
            term = lax.dot_general(
                slab,
                weight[kz, ky].reshape(3 * channels, channels),
                (((1,), (1,)), ((), ())),
                preferred_element_type=F32,
            )
            total = term if total is None else total + term
    answer = None
    for kx in range(3):
        part = total[:, kx * channels : (kx + 1) * channels].reshape(rows, cols, channels)
        part = shifted(part, kx - 1)
        answer = part if answer is None else answer + part
    out[...] = answer.astype(BF16)


def spread_kernel(n_gy, n_gz, conv_rows, down_rows, gathered, conv, down):
    rows, channels = conv.shape
    wide = down.shape[2] // channels
    for owner in range(n_gy * n_gz):
        piece = gathered.at[owner]
        first = owner * conv_rows
        take = min(conv_rows, rows - first)
        if take > 0:
            conv[pl.ds(first, take)] = piece[pl.ds(0, take)]
        first = owner * down_rows
        count = down.shape[1]
        done = 0
        while done < down_rows and first + done < wide * count:
            part, row = divmod(first + done, count)
            take = min(count - row, down_rows - done)
            for a in range(2):
                down[a, pl.ds(row, take), pl.ds(part * channels, channels)] = piece[
                    pl.ds(conv_rows + a * down_rows + done, take)
                ]
            done += take


def sides(cells, gz, gy):
    def moved(value, axis, count, up):
        pairs = [(i, i + 1) if up else (i + 1, i) for i in range(count - 1)]
        return lax.ppermute(value, axis, pairs)

    z_low = moved(cells, "gz", gz, True)
    z_high = moved(cells, "gz", gz, False)
    planes = (z_low, cells, z_high)
    y_low = moved(jnp.stack([plane[-1] for plane in planes]), "gy", gy, True)
    y_high = moved(jnp.stack([plane[0] for plane in planes]), "gy", gy, False)
    return cells, z_low, z_high, y_low, y_high


def everywhere(value, axis):
    copies = jnp.broadcast_to(value[None], (lax.axis_size(axis),) + value.shape)
    return lax.all_to_all(copies, axis, split_axis=0, concat_axis=0, tiled=True)


def per_device(
    level_input, pre_activation, conv_weight, down_weight, skip_cotangent, deep_cotangent
):
    n_gz = lax.axis_size("gz")
    n_gy = lax.axis_size("gy")
    _, rows, cols, channels = level_input.shape
    planes, deep_rows, deep_cols, share = deep_cotangent.shape
    deep_channels = down_weight.shape[4]
    parity = lax.axis_index("gz") % 2
    devices = n_gz * n_gy
    conv_rows = -(-27 * channels // (devices * 16)) * 16
    down_count = 4 * channels * deep_channels // channels
    down_rows = -(-down_count // (devices * 16)) * 16

    deep_t = jnp.swapaxes(deep_cotangent.reshape(planes, deep_rows * deep_cols, share), 1, 2)
    deep_t = jnp.broadcast_to(deep_t[:, None], (planes, 2) + deep_t.shape[1:])
    deep_t = deep_t.reshape(2 * planes, share, deep_rows * deep_cols)
    deep_t = lax.all_to_all(deep_t, "gz", split_axis=0, concat_axis=0, tiled=True)
    deep_t = deep_t.reshape(deep_channels, deep_rows * deep_cols)
    level = sides(level_input[0], n_gz, n_gy)
    down_slice = lax.dynamic_index_in_dim(down_weight, parity, 0, keepdims=False)

    shape = jax.ShapeDtypeStruct
    grad, down = call(
        mask_kernel,
        (
            shape((rows, cols, channels), BF16),
            shape((2, 2, channels, deep_channels), BF16),
        ),
        pre_activation[0],
        skip_cotangent[0],
        deep_t,
        down_slice,
    )

    piece = conv_rows + down_rows
    parts = call(
        lambda *refs: weight_kernel(n_gy, n_gz, conv_rows, down_rows, *refs),
        shape((n_gy, n_gz, piece, channels), BF16),
        *level,
        grad,
        down,
        scratch=[pltpu.VMEM((3, rows + 2, cols, channels), BF16)],
    )
    parts = lax.all_to_all(parts, "gy", split_axis=0, concat_axis=0, tiled=True)
    parts = jnp.sum(parts.astype(F32), axis=0).astype(BF16)
    parts = lax.all_to_all(parts, "gz", split_axis=0, concat_axis=0, tiled=True)
    parts = parts.astype(F32)
    cell_total = devices * rows * cols
    conv_sum = jnp.sum(parts[:, :conv_rows], axis=0) / math.sqrt(cell_total)
    slots = parts[:, conv_rows:].reshape(n_gz // 2, 2, down_rows, channels)
    down_sum = jnp.sum(slots, axis=0) / math.sqrt(cell_total // 8)
    final = jnp.concatenate([conv_sum, down_sum.reshape(2 * down_rows, channels)], axis=0)
    final = final.astype(BF16)
    gathered = everywhere(everywhere(final, "gz"), "gy").reshape((devices,) + final.shape)
    conv_grad, down_grad = call(
        lambda *refs: spread_kernel(n_gy, n_gz, conv_rows, down_rows, *refs),
        (
            shape((27 * channels, channels), BF16),
            shape((2, 4 * channels, deep_channels), BF16),
        ),
        gathered,
    )

    halo = sides(grad, n_gz, n_gy)
    input_grad = call(
        input_kernel,
        shape((rows, cols, channels), BF16),
        *halo,
        conv_weight,
        scratch=[pltpu.VMEM((3, rows + 2, cols, channels), BF16)],
    )
    return (
        input_grad[None],
        conv_grad.reshape(conv_weight.shape),
        down_grad.reshape(down_weight.shape),
    )


def solution(mesh):
    return jax.shard_map(
        per_device,
        mesh=mesh,
        in_specs=(
            P("gz", "gy", None, None),
            P("gz", "gy", None, None),
            P(),
            P(),
            P("gz", "gy", None, None),
            P(None, "gy", None, "gz"),
        ),
        out_specs=(P("gz", "gy", None, None), P(), P()),
        check_vma=False,
    )
```

```python
import math

import jax
import jax.numpy as jnp
from jax import lax
from jax.experimental import pallas as pl
from jax.experimental.pallas import tpu as pltpu
from jax.sharding import PartitionSpec as P

F32 = jnp.float32
BF16 = jnp.bfloat16
VMEM_LIMIT = 40 * 1024 * 1024


def call(kernel, out_shape, *operands, scratch=()):
    return pl.pallas_call(
        kernel,
        out_shape=out_shape,
        scratch_shapes=list(scratch),
        compiler_params=pltpu.CompilerParams(vmem_limit_bytes=VMEM_LIMIT),
    )(*operands)


def shifted(cells, step):
    if step == 0:
        return cells
    cols = cells.shape[1]
    moved = pltpu.roll(cells, step % cols, 1)
    col = lax.broadcasted_iota(jnp.int32, cells.shape, 1)
    keep = col >= step if step > 0 else col < cols + step
    return jnp.where(keep, moved, 0.0)


def pack_kernel(n_gy, deep, level, deep_out, level_out):
    planes, cells, share = deep.shape
    for plane in range(planes):
        turned = deep[plane].astype(F32).T.astype(BF16)
        deep_out[2 * plane] = turned
        deep_out[2 * plane + 1] = turned
    turned = level[...].astype(F32).T.astype(BF16)
    part = turned.shape[0] // n_gy
    for owner in range(n_gy):
        level_out[owner] = turned[owner * part : (owner + 1) * part]


def mask_kernel(n_gy, pre, skip, deep_t, weight, out):
    rows, cols, channels = pre.shape
    half = rows // 2
    deep_cols = cols // 2
    cells = half * cols
    deep_cells = half * deep_cols
    wide = lax.broadcasted_iota(jnp.int32, (deep_cells, cells), 1) // 2
    deep = lax.broadcasted_iota(jnp.int32, (deep_cells, cells), 0)
    repeat = (wide == deep).astype(BF16)
    spread = jnp.dot(deep_t[...], repeat, preferred_element_type=F32).astype(BF16)
    col = lax.broadcasted_iota(jnp.int32, (cells, channels), 0) % 2
    down = []
    for b in range(2):
        parts = [
            lax.dot_general(
                spread, weight[b, c], (((0,), (1,)), ((), ())), preferred_element_type=F32
            )
            for c in range(2)
        ]
        part = jnp.where(col == 0, parts[0], parts[1]).reshape(half, cols, channels)
        for y in range(half):
            row = 2 * y + b
            pre_row = pre[row].astype(F32)
            total = part[y] + skip[row].astype(F32)
            grad = jnp.where(pre_row > 0, total, 0.0).astype(BF16)
            for owner in range(n_gy):
                out[owner, pl.ds(row * cols, cols)] = grad
        hidden = jnp.concatenate(
            [jnp.maximum(pre[2 * y + b].astype(F32), 0.0) for y in range(half)], axis=0
        )
        for c in range(2):
            one = jnp.where(col == c, hidden, 0.0).astype(BF16)
            down.append(
                lax.dot_general(
                    one, spread, (((0,), (1,)), ((), ())), preferred_element_type=F32
                ).astype(BF16)
            )
    down = jnp.concatenate(down, axis=0)
    count = down.shape[0] // n_gy
    for owner in range(n_gy):
        for half_part in range(down.shape[1] // channels):
            out[owner, pl.ds(rows * cols + half_part * count, count)] = down[
                owner * count : (owner + 1) * count,
                half_part * channels : (half_part + 1) * channels,
            ]


def segments(rows, piece, unit):
    row = 0
    while row < rows:
        take = min(rows - row, unit - row % unit, piece - row % piece)
        yield row, row // piece, row % piece, take
        row += take


def weight_kernel(conv_rows, down_rows, shape, z_low, own, z_high, shared, out, near, wide):
    rows, cols, channels = shape
    n_gy, part, cells = own.shape
    n_gz = out.shape[0]
    rows_all = n_gy * rows
    for edge in (0, rows_all + 1):
        wide[edge] = jnp.zeros(wide.shape[1:], BF16)
    for owner in range(n_gy):
        grads = shared[owner, pl.ds(0, cells)].reshape(rows, cols, channels)
        grads = grads.astype(F32)
        for kx in range(3):
            wide[pl.ds(1 + owner * rows, rows), :, pl.ds(kx * channels, channels)] = shifted(
                grads, kx - 1
            ).astype(BF16)
    mine = lax.axis_index("gy") * rows
    near[...] = wide[pl.ds(mine, rows + 2), :, pl.ds(channels, channels)]
    level = jnp.concatenate(
        [
            jnp.concatenate([ref[owner] for owner in range(n_gy)], axis=1)
            for ref in (z_low, own, z_high)
        ],
        axis=0,
    )
    for ky in range(3):
        slab = wide[pl.ds(2 - ky, rows_all)].reshape(rows_all * cols, 3 * channels)
        total = jnp.dot(level, slab, preferred_element_type=F32).astype(BF16)
        for kz in range(3):
            for kx in range(3):
                first = ((kz * 3 + ky) * 3 + kx) * part
                value = total[kz * part : (kz + 1) * part, kx * channels : (kx + 1) * channels]
                for row in range(0, part, 16):
                    owner, inner = divmod(first + row, conv_rows)
                    out[owner, pl.ds(inner, 16)] = value[row : row + 16]
    for row in range(27 * part, n_gz * conv_rows, 16):
        owner, inner = divmod(row, conv_rows)
        out[owner, pl.ds(inner, 16)] = jnp.zeros((16, channels), BF16)
    down = shared[0, pl.ds(cells, shared.shape[1] - cells)].astype(F32)
    for owner in range(1, n_gy):
        down = down + shared[owner, pl.ds(cells, shared.shape[1] - cells)].astype(F32)
    down = down.astype(BF16)
    for row in range(0, n_gz * down_rows, 16):
        owner, inner = divmod(row, down_rows)
        value = down[row : row + 16] if row < down.shape[0] else jnp.zeros((16, channels), BF16)
        out[owner, pl.ds(conv_rows + inner, 16)] = value


def input_kernel(z_low, own, z_high, weight, out):
    rows, cols, channels = out.shape
    planes = (z_low, own, z_high)
    total = None
    for kz in range(3):
        for ky in range(3):
            slab = planes[2 - kz][pl.ds(2 - ky, rows)].reshape(rows * cols, channels)
            term = lax.dot_general(
                slab,
                weight[kz, ky].reshape(3 * channels, channels),
                (((1,), (1,)), ((), ())),
                preferred_element_type=F32,
            )
            total = term if total is None else total + term
    answer = None
    for kx in range(3):
        part = total[:, kx * channels : (kx + 1) * channels].reshape(rows, cols, channels)
        part = shifted(part, kx - 1)
        answer = part if answer is None else answer + part
    out[...] = answer.astype(BF16)


def place_kernel(conv_rows, down_rows, blocks, conv, down):
    me = lax.axis_index("gy")
    part = conv.shape[2]
    count, deep_channels = down.shape[2:]
    channels = conv.shape[3]
    for code, block in blocks:
        column = jnp.bitwise_xor(me, code)
        for row, owner, inner, take in segments(27 * part, conv_rows, part):
            conv[row // part, column, pl.ds(row % part, take)] = block[owner, pl.ds(inner, take)]
        for a in range(2):
            base = conv_rows + a * down_rows
            for half in range(deep_channels // channels):
                for row, _, _, take in segments(count, down_rows, down_rows):
                    owner, inner = divmod(half * count + row, down_rows)
                    down[a, column, pl.ds(row, take), pl.ds(half * channels, channels)] = block[
                        owner, pl.ds(base + inner, take)
                    ]


def along(value, axis, up):
    pairs = [(i, i + 1) if up else (i + 1, i) for i in range(lax.axis_size(axis) - 1)]
    return lax.ppermute(value, axis, pairs)


def swapped(value, axis, code):
    return lax.ppermute(value, axis, [(i, i ^ code) for i in range(lax.axis_size(axis))])


def everywhere(value, axis):
    copies = jnp.broadcast_to(value[None], (lax.axis_size(axis),) + value.shape)
    return exchanged(copies, axis)


def exchanged(value, axis):
    return lax.all_to_all(value, axis, split_axis=0, concat_axis=0, tiled=True)


def per_device(
    level_input, pre_activation, conv_weight, down_weight, skip_cotangent, deep_cotangent
):
    n_gz = lax.axis_size("gz")
    n_gy = lax.axis_size("gy")
    _, rows, cols, channels = level_input.shape
    planes, deep_rows, deep_cols, share = deep_cotangent.shape
    deep_channels = down_weight.shape[4]
    parity = lax.axis_index("gz") % 2
    devices = n_gz * n_gy
    part = channels // n_gy
    cells = rows * cols
    deep_cells = deep_rows * deep_cols
    conv_rows = -(-27 * part // (n_gz * 16)) * 16
    down_count = 4 * deep_channels // n_gy
    down_rows = -(-down_count // (n_gz * 16)) * 16
    shape = jax.ShapeDtypeStruct

    level = level_input.reshape(cells, channels)
    deep = deep_cotangent.reshape(planes, deep_cells, share)
    if share % 16 == 0:
        deep_t, level_t = call(
            lambda *refs: pack_kernel(n_gy, *refs),
            (
                shape((2 * planes, share, deep_cells), BF16),
                shape((n_gy, part, cells), BF16),
            ),
            deep,
            level,
        )
    else:
        deep_t = jnp.repeat(jnp.swapaxes(deep, 1, 2), 2, axis=0)
        level_t = level.T.reshape(n_gy, part, cells)
    deep_t = exchanged(deep_t, "gz").reshape(deep_channels, deep_cells)
    level_t = exchanged(level_t, "gy")
    down_slice = lax.dynamic_index_in_dim(down_weight, parity, 0, keepdims=False)
    shared = call(
        lambda *refs: mask_kernel(n_gy, *refs),
        shape((n_gy, cells + down_count, channels), BF16),
        pre_activation[0],
        skip_cotangent[0],
        deep_t,
        down_slice,
    )
    shared = exchanged(shared, "gy")
    parts, near = call(
        lambda *refs: weight_kernel(conv_rows, down_rows, (rows, cols, channels), *refs),
        (
            shape((n_gz, conv_rows + down_rows, channels), BF16),
            shape((rows + 2, cols, channels), BF16),
        ),
        along(level_t, "gz", True),
        level_t,
        along(level_t, "gz", False),
        shared,
        scratch=[pltpu.VMEM((n_gy * rows + 2, cols, 3 * channels), BF16)],
    )
    parts = exchanged(parts, "gz").astype(F32)
    cell_total = devices * cells
    conv_sum = jnp.sum(parts[:, :conv_rows], axis=0) / math.sqrt(cell_total)
    slots = parts[:, conv_rows:].reshape(n_gz // 2, 2, down_rows, channels)
    down_sum = jnp.sum(slots, axis=0) / math.sqrt(cell_total // 8)
    final = jnp.concatenate([conv_sum, down_sum.reshape(2 * down_rows, channels)], axis=0)
    block = everywhere(final.astype(BF16), "gz")
    if n_gy == 4:
        across = swapped(block, "gy", 2)
        blocks = {0: block, 1: swapped(block, "gy", 1), 2: across, 3: swapped(across, "gy", 1)}
    else:
        blocks = {code: swapped(block, "gy", code) for code in range(n_gy)}
    conv_grad, down_grad = call(
        lambda *refs: place_kernel(conv_rows, down_rows, list(zip(blocks, refs)), *refs[n_gy:]),
        (
            shape((27, n_gy, part, channels), BF16),
            shape((2, n_gy, 4 * channels // n_gy, deep_channels), BF16),
        ),
        *blocks.values(),
    )
    input_grad = call(
        input_kernel,
        shape((rows, cols, channels), BF16),
        along(near, "gz", True),
        near,
        along(near, "gz", False),
        conv_weight,
    )
    return (
        input_grad[None],
        conv_grad.reshape(conv_weight.shape),
        down_grad.reshape(down_weight.shape),
    )


def solution(mesh):
    return jax.shard_map(
        per_device,
        mesh=mesh,
        in_specs=(
            P("gz", "gy", None, None),
            P("gz", "gy", None, None),
            P(),
            P(),
            P("gz", "gy", None, None),
            P(None, "gy", None, "gz"),
        ),
        out_specs=(P("gz", "gy", None, None), P(), P()),
        check_vma=False,
    )
```

```python
import math

import jax
import jax.numpy as jnp
from jax import lax
from jax.experimental import pallas as pl
from jax.experimental.pallas import tpu as pltpu
from jax.sharding import PartitionSpec as P

F32 = jnp.float32
BF16 = jnp.bfloat16
VMEM_LIMIT = 40 * 1024 * 1024


def call(kernel, out_shape, *operands, scratch=()):
    return pl.pallas_call(
        kernel,
        out_shape=out_shape,
        scratch_shapes=list(scratch),
        compiler_params=pltpu.CompilerParams(vmem_limit_bytes=VMEM_LIMIT),
    )(*operands)


def shifted(cells, step):
    if step == 0:
        return cells
    cols = cells.shape[1]
    moved = pltpu.roll(cells, step % cols, 1)
    col = lax.broadcasted_iota(jnp.int32, cells.shape, 1)
    keep = col >= step if step > 0 else col < cols + step
    return jnp.where(keep, moved, 0.0)


def pack_kernel(n_gy, turn_deep, deep, level, *rest):
    level_outs, rest = rest[:n_gy], rest[n_gy:]
    turned = level[...].astype(F32).T.astype(BF16)
    part = turned.shape[0] // n_gy
    level_t = rest[-1]
    for owner in range(n_gy):
        level_t[owner] = turned[owner * part : (owner + 1) * part]
    me = lax.axis_index("gy")
    for code in range(n_gy):
        level_outs[code][...] = level_t[jnp.bitwise_xor(me, code)]
    if turn_deep:
        deep_outs, deep_t = rest[:-2], rest[-2]
        for plane in range(deep.shape[0]):
            deep_t[plane] = deep[plane].astype(F32).T.astype(BF16)
        me = lax.axis_index("gz")
        for code in range(len(deep_outs)):
            deep_outs[code][...] = deep_t[jnp.bitwise_xor(me, code) // 2]


def mask_kernel(n_gy, pre, skip, weight, *rest):
    deeps, outs = rest[: -n_gy - 2], rest[-n_gy - 2 : -2]
    deep_t, down_all = rest[-2:]
    share = deeps[0].shape[0]
    if len(deeps) > 1:
        source = lax.axis_index("gz")
        for code, ref in enumerate(deeps):
            first = pl.multiple_of(jnp.bitwise_xor(source, code) * share, share)
            deep_t[pl.ds(first, share)] = ref[...]
    else:
        deep_t[...] = deeps[0][...]
    rows, cols, channels = pre.shape
    half = rows // 2
    deep_cols = cols // 2
    cells = half * cols
    deep_cells = half * deep_cols
    wide = lax.broadcasted_iota(jnp.int32, (deep_cells, cells), 1) // 2
    deep = lax.broadcasted_iota(jnp.int32, (deep_cells, cells), 0)
    repeat = (wide == deep).astype(BF16)
    spread = jnp.dot(deep_t[...], repeat, preferred_element_type=F32).astype(BF16)
    col = lax.broadcasted_iota(jnp.int32, (cells, channels), 0) % 2
    count = down_all.shape[1]
    for b in range(2):
        parts = [
            lax.dot_general(
                spread, weight[b, c], (((0,), (1,)), ((), ())), preferred_element_type=F32
            )
            for c in range(2)
        ]
        part = jnp.where(col == 0, parts[0], parts[1]).reshape(half, cols, channels)
        for y in range(half):
            row = 2 * y + b
            pre_row = pre[row].astype(F32)
            total = part[y] + skip[row].astype(F32)
            grad = jnp.where(pre_row > 0, total, 0.0).astype(BF16)
            for out in outs:
                out[pl.ds(row * cols, cols)] = grad
        hidden = jnp.concatenate(
            [jnp.maximum(pre[2 * y + b].astype(F32), 0.0) for y in range(half)], axis=0
        )
        for c in range(2):
            one = jnp.where(col == c, hidden, 0.0).astype(BF16)
            down = lax.dot_general(
                one, spread, (((0,), (1,)), ((), ())), preferred_element_type=F32
            ).astype(BF16)
            for first, owner, inner, take in segments(channels, count, channels, (b * 2 + c) * channels):
                down_all[owner, pl.ds(inner, take)] = down[first : first + take]
    me = lax.axis_index("gy")
    for code, out in enumerate(outs):
        owner = jnp.bitwise_xor(me, code)
        for side in range(down_all.shape[2] // channels):
            out[pl.ds(rows * cols + side * count, count)] = down_all[
                owner, :, pl.ds(side * channels, channels)
            ]


def segments(rows, piece, unit, base=0):
    row = 0
    while row < rows:
        take = min(rows - row, unit - row % unit, piece - (base + row) % piece)
        yield row, (base + row) // piece, (base + row) % piece, take
        row += take


def sides(even, odd):
    upper = lax.axis_index("gz") % 2 == 0
    low = jnp.where(upper, odd[...].astype(F32), even[...].astype(F32)).astype(BF16)
    high = jnp.where(upper, even[...].astype(F32), odd[...].astype(F32)).astype(BF16)
    return low, high


def weight_kernel(n_gy, conv_rows, down_rows, shape, *refs):
    even, own, odd = refs[:3]
    shared = refs[3 : 3 + n_gy]
    near, wide, level, parts = refs[-4:]
    outs = refs[3 + n_gy : -4]
    rows, cols, channels = shape
    part = own.shape[1]
    cells = rows * cols
    n_gz = parts.shape[0]
    rows_all = n_gy * rows
    me = lax.axis_index("gy")
    low, high = sides(even, odd)
    for edge in (0, rows_all + 1):
        wide[edge] = jnp.zeros(wide.shape[1:], BF16)
    for code in range(n_gy):
        owner = jnp.bitwise_xor(me, code)
        grads = shared[code][pl.ds(0, cells)].reshape(rows, cols, channels).astype(F32)
        for kx in range(3):
            wide[pl.ds(1 + owner * rows, rows), :, pl.ds(kx * channels, channels)] = shifted(
                grads, kx - 1
            ).astype(BF16)
        for kz, plane in enumerate((low[code], own[code], high[code])):
            level[owner, pl.ds(kz * part, part)] = plane
    near[...] = wide[pl.ds(me * rows, rows + 2), :, pl.ds(channels, channels)]
    for ky in range(3):
        total = None
        for owner in range(n_gy):
            slab = wide[pl.ds(2 - ky + owner * rows, rows)].reshape(cells, 3 * channels)
            term = jnp.dot(level[owner], slab, preferred_element_type=F32)
            total = term if total is None else total + term
        total = total.astype(BF16)
        for kz in range(3):
            for kx in range(3):
                value = total[kz * part : (kz + 1) * part, kx * channels : (kx + 1) * channels]
                first = ((kz * 3 + ky) * 3 + kx) * part
                for row, owner, inner, take in segments(part, conv_rows, part, first):
                    parts[owner, pl.ds(inner, take)] = value[row : row + take]
    blank = n_gz * conv_rows - 27 * part
    for row, owner, inner, take in segments(blank, conv_rows, conv_rows, 27 * part):
        parts[owner, pl.ds(inner, take)] = jnp.zeros((take, channels), BF16)
    count = shared[0].shape[0] - cells
    down = shared[0][pl.ds(cells, count)].astype(F32)
    for code in range(1, n_gy):
        down = down + shared[code][pl.ds(cells, count)].astype(F32)
    down = down.astype(BF16)
    for row, owner, inner, take in segments(count, down_rows, count):
        parts[owner, pl.ds(conv_rows + inner, take)] = down[row : row + take]
    blank = n_gz * down_rows - count
    for row, owner, inner, take in segments(blank, down_rows, down_rows, count):
        parts[owner, pl.ds(conv_rows + inner, take)] = jnp.zeros((take, channels), BF16)
    if len(outs) > 1:
        me = lax.axis_index("gz")
        for code, out in enumerate(outs):
            out[...] = parts[jnp.bitwise_xor(me, code)]
    else:
        outs[0][...] = parts[...]


def input_kernel(even, own, odd, weight, out):
    rows, cols, channels = out.shape
    low, high = sides(even, odd)
    planes = (low, own, high)
    total = None
    for kz in range(3):
        for ky in range(3):
            slab = planes[2 - kz][2 - ky : 2 - ky + rows].reshape(rows * cols, channels)
            term = lax.dot_general(
                slab,
                weight[kz, ky].reshape(3 * channels, channels),
                (((1,), (1,)), ((), ())),
                preferred_element_type=F32,
            )
            total = term if total is None else total + term
    answer = None
    for kx in range(3):
        part = total[:, kx * channels : (kx + 1) * channels].reshape(rows, cols, channels)
        part = shifted(part, kx - 1)
        answer = part if answer is None else answer + part
    out[...] = answer.astype(BF16)


def reversed_bits(code, count):
    place, bit = 0, 1
    while bit < count:
        place = place * 2 + code // bit % 2
        bit *= 2
    return place


def place_kernel(n_gy, conv_rows, down_rows, *refs):
    blocks, (conv, down) = refs[:n_gy], refs[n_gy:]
    me = lax.axis_index("gy")
    line = lax.axis_index("gz")
    part = conv.shape[2]
    count, deep_channels = down.shape[2:]
    channels = conv.shape[3]
    n_gz = blocks[0].shape[0]
    places = [reversed_bits(jnp.bitwise_xor(line, owner), n_gz) for owner in range(n_gz)]
    for code, block in enumerate(blocks):
        column = jnp.bitwise_xor(me, code)
        for row, owner, inner, take in segments(27 * part, conv_rows, part):
            conv[row // part, column, pl.ds(row % part, take)] = block[
                places[owner], pl.ds(inner, take)
            ]
        for a in range(2):
            base = conv_rows + a * down_rows
            for side in range(deep_channels // channels):
                for row, owner, inner, take in segments(count, down_rows, count, side * count):
                    down[a, column, pl.ds(row, take), pl.ds(side * channels, channels)] = block[
                        places[owner], pl.ds(base + inner, take)
                    ]


def swapped(value, axis, code):
    return lax.ppermute(value, axis, [(i, i ^ code) for i in range(lax.axis_size(axis))])


def neighbours(value):
    last = lax.axis_size("gz") - 1
    odd = [(i + d, i + 1 - d) for i in range(1, last, 2) for d in range(2)]
    return swapped(value, "gz", 1), lax.ppermute(value, "gz", odd)


def exchanged(value, axis):
    return lax.all_to_all(value, axis, split_axis=0, concat_axis=0, tiled=True)


def per_device(
    level_input, pre_activation, conv_weight, down_weight, skip_cotangent, deep_cotangent
):
    n_gz = lax.axis_size("gz")
    n_gy = lax.axis_size("gy")
    _, rows, cols, channels = level_input.shape
    planes, deep_rows, deep_cols, share = deep_cotangent.shape
    deep_channels = down_weight.shape[4]
    parity = lax.axis_index("gz") % 2
    devices = n_gz * n_gy
    part = channels // n_gy
    cells = rows * cols
    deep_cells = deep_rows * deep_cols
    conv_rows = -(-27 * part // (n_gz * 16)) * 16
    down_count = 4 * deep_channels // n_gy
    down_rows = -(-down_count // (n_gz * 16)) * 16
    piece = conv_rows + down_rows
    direct = n_gz <= 8
    shape = jax.ShapeDtypeStruct

    level = level_input.reshape(cells, channels)
    deep = deep_cotangent.reshape(planes, deep_cells, share)
    packed = call(
        lambda *refs: pack_kernel(n_gy, direct, *refs),
        [shape((part, cells), BF16)] * n_gy
        + ([shape((share, deep_cells), BF16)] * n_gz if direct else []),
        deep,
        level,
        scratch=([pltpu.VMEM((planes, share, deep_cells), BF16)] if direct else [])
        + [pltpu.VMEM((n_gy, part, cells), BF16)],
    )
    level_t, deep_t = packed[:n_gy], packed[n_gy:]
    if direct:
        deep_t = [swapped(value, "gz", code) if code else value for code, value in enumerate(deep_t)]
    else:
        turned = jnp.repeat(jnp.swapaxes(deep, 1, 2), 2, axis=0)
        deep_t = [exchanged(turned, "gz").reshape(deep_channels, deep_cells)]
    level_t = jnp.stack(
        [swapped(value, "gy", code) if code else value for code, value in enumerate(level_t)]
    )
    down_slice = lax.dynamic_index_in_dim(down_weight, parity, 0, keepdims=False)
    shared = call(
        lambda *refs: mask_kernel(n_gy, *refs),
        [shape((cells + down_count, channels), BF16)] * n_gy,
        pre_activation[0],
        skip_cotangent[0],
        down_slice,
        *deep_t,
        scratch=[
            pltpu.VMEM((deep_channels, deep_cells), BF16),
            pltpu.VMEM((n_gy, 4 * channels // n_gy, deep_channels), BF16),
        ],
    )
    shared = [swapped(value, "gy", code) if code else value for code, value in enumerate(shared)]
    even, odd = neighbours(level_t)
    *parts, near = call(
        lambda *refs: weight_kernel(n_gy, conv_rows, down_rows, (rows, cols, channels), *refs),
        (
            [shape((piece, channels), BF16)] * n_gz
            if direct
            else [shape((n_gz, piece, channels), BF16)]
        )
        + [shape((rows + 2, cols, channels), BF16)],
        even,
        level_t,
        odd,
        *shared,
        scratch=[
            pltpu.VMEM((n_gy * rows + 2, cols, 3 * channels), BF16),
            pltpu.VMEM((n_gy, 3 * part, cells), BF16),
            pltpu.VMEM((n_gz, piece, channels), BF16),
        ],
    )
    cell_total = devices * cells
    if direct:
        parts = [swapped(value, "gz", code) if code else value for code, value in enumerate(parts)]
        same = sum(value.astype(F32) for value in parts[0::2])
        other = sum(value.astype(F32) for value in parts[1::2])
        first = jnp.where(parity == 0, same[conv_rows:], other[conv_rows:])
        second = jnp.where(parity == 0, other[conv_rows:], same[conv_rows:])
    else:
        parts = exchanged(parts[0], "gz").astype(F32)
        same, other = jnp.sum(parts[0::2], axis=0), jnp.sum(parts[1::2], axis=0)
        first, second = same[conv_rows:], other[conv_rows:]
    conv_sum = (same[:conv_rows] + other[:conv_rows]) / math.sqrt(cell_total)
    down_sum = jnp.concatenate([first, second], axis=0) / math.sqrt(cell_total // 8)
    block = jnp.concatenate([conv_sum, down_sum], axis=0).astype(BF16)[None]
    code = n_gz // 2
    while code:
        block = jnp.concatenate([block, swapped(block, "gz", code)], axis=0)
        code //= 2
    blocks = [block]
    code = n_gy // 2
    while code:
        blocks = blocks + [swapped(value, "gy", code) for value in blocks]
        code //= 2
    order = [reversed_bits(place, n_gy) for place in range(n_gy)]
    blocks = [blocks[order[place]] for place in range(n_gy)]
    conv_grad, down_grad = call(
        lambda *refs: place_kernel(n_gy, conv_rows, down_rows, *refs),
        (
            shape((27, n_gy, part, channels), BF16),
            shape((2, n_gy, 4 * channels // n_gy, deep_channels), BF16),
        ),
        *blocks,
    )
    even, odd = neighbours(near)
    input_grad = call(
        input_kernel,
        shape((rows, cols, channels), BF16),
        even,
        near,
        odd,
        conv_weight,
    )
    return (
        input_grad[None],
        conv_grad.reshape(conv_weight.shape),
        down_grad.reshape(down_weight.shape),
    )


def solution(mesh):
    return jax.shard_map(
        per_device,
        mesh=mesh,
        in_specs=(
            P("gz", "gy", None, None),
            P("gz", "gy", None, None),
            P(),
            P(),
            P("gz", "gy", None, None),
            P(None, "gy", None, "gz"),
        ),
        out_specs=(P("gz", "gy", None, None), P(), P()),
        check_vma=False,
    )
```

```python
import math

import jax
import jax.numpy as jnp
from jax import lax
from jax.experimental import pallas as pl
from jax.experimental.pallas import tpu as pltpu
from jax.sharding import PartitionSpec as P

F32 = jnp.float32
BF16 = jnp.bfloat16
VMEM_LIMIT = 40 * 1024 * 1024


def call(kernel, out_shape, *operands, scratch=()):
    return pl.pallas_call(
        kernel,
        out_shape=out_shape,
        scratch_shapes=list(scratch),
        compiler_params=pltpu.CompilerParams(vmem_limit_bytes=VMEM_LIMIT),
    )(*operands)


def shifted(cells, step):
    if step == 0:
        return cells
    cols = cells.shape[1]
    moved = pltpu.roll(cells, step % cols, 1)
    col = lax.broadcasted_iota(jnp.int32, cells.shape, 1)
    keep = col >= step if step > 0 else col < cols + step
    return jnp.where(keep, moved, 0.0)


def pack_kernel(n_gy, turn_deep, deep, level, *rest):
    level_outs, level_t = rest[:n_gy], rest[-1]
    turned = level[...].astype(F32).T.astype(BF16)
    part = turned.shape[0] // n_gy
    for owner in range(n_gy):
        level_t[owner] = turned[owner * part : (owner + 1) * part]
    me = lax.axis_index("gy")
    for code in range(n_gy):
        level_outs[code][...] = level_t[jnp.bitwise_xor(me, code)]
    if turn_deep:
        deep_out = rest[n_gy]
        for plane in range(deep.shape[0]):
            turned = deep[plane].astype(F32).T.astype(BF16)
            deep_out[2 * plane] = turned
            deep_out[2 * plane + 1] = turned


def mask_kernel(n_gy, pre, skip, weight, deep_t, *rest):
    outs, down_all = rest[:-1], rest[-1]
    rows, cols, channels = pre.shape
    half = rows // 2
    deep_cols = cols // 2
    cells = half * cols
    deep_cells = half * deep_cols
    wide = lax.broadcasted_iota(jnp.int32, (deep_cells, cells), 1) // 2
    deep = lax.broadcasted_iota(jnp.int32, (deep_cells, cells), 0)
    repeat = (wide == deep).astype(BF16)
    spread = jnp.dot(deep_t[...], repeat, preferred_element_type=F32).astype(BF16)
    col = lax.broadcasted_iota(jnp.int32, (cells, channels), 0) % 2
    count = down_all.shape[1]
    for b in range(2):
        parts = [
            lax.dot_general(
                spread, weight[b, c], (((0,), (1,)), ((), ())), preferred_element_type=F32
            )
            for c in range(2)
        ]
        part = jnp.where(col == 0, parts[0], parts[1]).reshape(half, cols, channels)
        for y in range(half):
            row = 2 * y + b
            pre_row = pre[row].astype(F32)
            total = part[y] + skip[row].astype(F32)
            grad = jnp.where(pre_row > 0, total, 0.0).astype(BF16)
            for out in outs:
                out[pl.ds(row * cols, cols)] = grad
        hidden = jnp.concatenate(
            [jnp.maximum(pre[2 * y + b].astype(F32), 0.0) for y in range(half)], axis=0
        )
        for c in range(2):
            one = jnp.where(col == c, hidden, 0.0).astype(BF16)
            down = lax.dot_general(
                one, spread, (((0,), (1,)), ((), ())), preferred_element_type=F32
            ).astype(BF16)
            for first, owner, inner, take in segments(channels, count, channels, (b * 2 + c) * channels):
                down_all[owner, pl.ds(inner, take)] = down[first : first + take]
    me = lax.axis_index("gy")
    for code, out in enumerate(outs):
        owner = jnp.bitwise_xor(me, code)
        for side in range(down_all.shape[2] // channels):
            out[pl.ds(rows * cols + side * count, count)] = down_all[
                owner, :, pl.ds(side * channels, channels)
            ]


def segments(rows, piece, unit, base=0):
    row = 0
    while row < rows:
        take = min(rows - row, unit - row % unit, piece - (base + row) % piece)
        yield row, (base + row) // piece, (base + row) % piece, take
        row += take


def sides(even, odd):
    upper = lax.axis_index("gz") % 2 == 0
    low = jnp.where(upper, odd[...].astype(F32), even[...].astype(F32)).astype(BF16)
    high = jnp.where(upper, even[...].astype(F32), odd[...].astype(F32)).astype(BF16)
    return low, high


def weight_kernel(n_gy, conv_rows, down_rows, shape, *refs):
    even, own, odd = refs[:3]
    shared = refs[3 : 3 + n_gy]
    parts, near, wide, level = refs[3 + n_gy :]
    rows, cols, channels = shape
    part = own.shape[1]
    cells = rows * cols
    n_gz = parts.shape[0]
    rows_all = n_gy * rows
    me = lax.axis_index("gy")
    low, high = sides(even, odd)
    for edge in (0, rows_all + 1):
        wide[edge] = jnp.zeros(wide.shape[1:], BF16)
    for code in range(n_gy):
        owner = jnp.bitwise_xor(me, code)
        grads = shared[code][pl.ds(0, cells)].reshape(rows, cols, channels).astype(F32)
        for kx in range(3):
            wide[pl.ds(1 + owner * rows, rows), :, pl.ds(kx * channels, channels)] = shifted(
                grads, kx - 1
            ).astype(BF16)
        for kz, plane in enumerate((low[code], own[code], high[code])):
            level[owner, pl.ds(kz * part, part)] = plane
    near[...] = wide[pl.ds(me * rows, rows + 2), :, pl.ds(channels, channels)]
    for ky in range(3):
        total = None
        for owner in range(n_gy):
            slab = wide[pl.ds(2 - ky + owner * rows, rows)].reshape(cells, 3 * channels)
            term = jnp.dot(level[owner], slab, preferred_element_type=F32)
            total = term if total is None else total + term
        total = total.astype(BF16)
        for kz in range(3):
            for kx in range(3):
                value = total[kz * part : (kz + 1) * part, kx * channels : (kx + 1) * channels]
                first = ((kz * 3 + ky) * 3 + kx) * part
                for row, owner, inner, take in segments(part, conv_rows, part, first):
                    parts[owner, pl.ds(inner, take)] = value[row : row + take]
    blank = n_gz * conv_rows - 27 * part
    for row, owner, inner, take in segments(blank, conv_rows, conv_rows, 27 * part):
        parts[owner, pl.ds(inner, take)] = jnp.zeros((take, channels), BF16)
    count = shared[0].shape[0] - cells
    down = shared[0][pl.ds(cells, count)].astype(F32)
    for code in range(1, n_gy):
        down = down + shared[code][pl.ds(cells, count)].astype(F32)
    down = down.astype(BF16)
    for row, owner, inner, take in segments(count, down_rows, count):
        parts[owner, pl.ds(conv_rows + inner, take)] = down[row : row + take]
    blank = n_gz * down_rows - count
    for row, owner, inner, take in segments(blank, down_rows, down_rows, count):
        parts[owner, pl.ds(conv_rows + inner, take)] = jnp.zeros((take, channels), BF16)


def input_kernel(even, own, odd, weight, out):
    rows, cols, channels = out.shape
    low, high = sides(even, odd)
    planes = (low, own, high)
    total = None
    for kz in range(3):
        for ky in range(3):
            slab = planes[2 - kz][2 - ky : 2 - ky + rows].reshape(rows * cols, channels)
            term = lax.dot_general(
                slab,
                weight[kz, ky].reshape(3 * channels, channels),
                (((1,), (1,)), ((), ())),
                preferred_element_type=F32,
            )
            total = term if total is None else total + term
    answer = None
    for kx in range(3):
        part = total[:, kx * channels : (kx + 1) * channels].reshape(rows, cols, channels)
        part = shifted(part, kx - 1)
        answer = part if answer is None else answer + part
    out[...] = answer.astype(BF16)


def reversed_bits(code, count):
    place, bit = 0, 1
    while bit < count:
        place = place * 2 + code // bit % 2
        bit *= 2
    return place


def place_kernel(n_gy, conv_rows, down_rows, *refs):
    blocks, (conv, down) = refs[:n_gy], refs[n_gy:]
    me = lax.axis_index("gy")
    part = conv.shape[2]
    count, deep_channels = down.shape[2:]
    channels = conv.shape[3]
    for code, block in enumerate(blocks):
        column = jnp.bitwise_xor(me, code)
        for row, owner, inner, take in segments(27 * part, conv_rows, part):
            conv[row // part, column, pl.ds(row % part, take)] = block[
                owner, pl.ds(inner, take)
            ]
        for a in range(2):
            base = conv_rows + a * down_rows
            for side in range(deep_channels // channels):
                for row, owner, inner, take in segments(count, down_rows, count, side * count):
                    down[a, column, pl.ds(row, take), pl.ds(side * channels, channels)] = block[
                        owner, pl.ds(base + inner, take)
                    ]


def swapped(value, axis, code):
    return lax.ppermute(value, axis, [(i, i ^ code) for i in range(lax.axis_size(axis))])


def neighbours(value):
    last = lax.axis_size("gz") - 1
    odd = [(i + d, i + 1 - d) for i in range(1, last, 2) for d in range(2)]
    return swapped(value, "gz", 1), lax.ppermute(value, "gz", odd)


def exchanged(value, axis):
    return lax.all_to_all(value, axis, split_axis=0, concat_axis=0, tiled=True)


def per_device(
    level_input, pre_activation, conv_weight, down_weight, skip_cotangent, deep_cotangent
):
    n_gz = lax.axis_size("gz")
    n_gy = lax.axis_size("gy")
    _, rows, cols, channels = level_input.shape
    planes, deep_rows, deep_cols, share = deep_cotangent.shape
    deep_channels = down_weight.shape[4]
    parity = lax.axis_index("gz") % 2
    devices = n_gz * n_gy
    part = channels // n_gy
    cells = rows * cols
    deep_cells = deep_rows * deep_cols
    conv_rows = -(-27 * part // (n_gz * 16)) * 16
    down_count = 4 * deep_channels // n_gy
    down_rows = -(-down_count // (n_gz * 16)) * 16
    piece = conv_rows + down_rows
    turn_deep = share % 16 == 0
    shape = jax.ShapeDtypeStruct

    level = level_input.reshape(cells, channels)
    deep = deep_cotangent.reshape(planes, deep_cells, share)
    packed = call(
        lambda *refs: pack_kernel(n_gy, turn_deep, *refs),
        [shape((part, cells), BF16)] * n_gy
        + [shape((2 * planes, share, deep_cells), BF16)] * turn_deep,
        deep,
        level,
        scratch=[pltpu.VMEM((n_gy, part, cells), BF16)],
    )
    level_t = packed[:n_gy]
    deep_t = packed[n_gy] if turn_deep else jnp.repeat(jnp.swapaxes(deep, 1, 2), 2, axis=0)
    deep_t = exchanged(deep_t, "gz").reshape(deep_channels, deep_cells)
    level_t = [swapped(value, "gy", code) if code else value for code, value in enumerate(level_t)]
    deep_t, level_t = lax.optimization_barrier((deep_t, jnp.stack(level_t)))
    down_slice = lax.dynamic_index_in_dim(down_weight, parity, 0, keepdims=False)
    shared = call(
        lambda *refs: mask_kernel(n_gy, *refs),
        [shape((cells + down_count, channels), BF16)] * n_gy,
        pre_activation[0],
        skip_cotangent[0],
        down_slice,
        deep_t,
        scratch=[pltpu.VMEM((n_gy, 4 * channels // n_gy, deep_channels), BF16)],
    )
    shared = [swapped(value, "gy", code) if code else value for code, value in enumerate(shared)]
    even, odd = neighbours(level_t)
    parts, near = call(
        lambda *refs: weight_kernel(n_gy, conv_rows, down_rows, (rows, cols, channels), *refs),
        (
            shape((n_gz, piece, channels), BF16),
            shape((rows + 2, cols, channels), BF16),
        ),
        even,
        level_t,
        odd,
        *shared,
        scratch=[
            pltpu.VMEM((n_gy * rows + 2, cols, 3 * channels), BF16),
            pltpu.VMEM((n_gy, 3 * part, cells), BF16),
        ],
    )
    parts = exchanged(parts, "gz").astype(F32)
    cell_total = devices * cells
    conv_sum = jnp.sum(parts[:, :conv_rows], axis=0) / math.sqrt(cell_total)
    slots = parts[:, conv_rows:].reshape(n_gz // 2, 2, down_rows, channels)
    down_sum = jnp.sum(slots, axis=0) / math.sqrt(cell_total // 8)
    final = jnp.concatenate([conv_sum, down_sum.reshape(2 * down_rows, channels)], axis=0)
    final = final.astype(BF16)[None]
    block = exchanged(jnp.broadcast_to(final, (n_gz,) + final.shape[1:]), "gz")
    even, odd = neighbours(near)
    input_grad = call(
        input_kernel,
        shape((rows, cols, channels), BF16),
        even,
        near,
        odd,
        conv_weight,
    )
    blocks = [block]
    code = n_gy // 2
    while code:
        if code == 1:
            input_grad, *blocks = lax.optimization_barrier((input_grad, *blocks))
        blocks = blocks + [swapped(value, "gy", code) for value in blocks]
        code //= 2
    order = [reversed_bits(place, n_gy) for place in range(n_gy)]
    blocks = [blocks[order[place]] for place in range(n_gy)]
    conv_grad, down_grad = call(
        lambda *refs: place_kernel(n_gy, conv_rows, down_rows, *refs),
        (
            shape((27, n_gy, part, channels), BF16),
            shape((2, n_gy, 4 * channels // n_gy, deep_channels), BF16),
        ),
        *blocks,
    )
    return (
        input_grad[None],
        conv_grad.reshape(conv_weight.shape),
        down_grad.reshape(down_weight.shape),
    )


def solution(mesh):
    return jax.shard_map(
        per_device,
        mesh=mesh,
        in_specs=(
            P("gz", "gy", None, None),
            P("gz", "gy", None, None),
            P(),
            P(),
            P("gz", "gy", None, None),
            P(None, "gy", None, "gz"),
        ),
        out_specs=(P("gz", "gy", None, None), P(), P()),
        check_vma=False,
    )
```

```python
import math

import jax
import jax.numpy as jnp
from jax import lax
from jax.experimental import pallas as pl
from jax.experimental.pallas import tpu as pltpu
from jax.sharding import PartitionSpec as P

F32 = jnp.float32
BF16 = jnp.bfloat16
VMEM_LIMIT = 40 * 1024 * 1024


def call(kernel, out_shape, *operands, scratch=()):
    return pl.pallas_call(
        kernel,
        out_shape=out_shape,
        scratch_shapes=list(scratch),
        compiler_params=pltpu.CompilerParams(vmem_limit_bytes=VMEM_LIMIT),
    )(*operands)


def shifted(cells, step):
    if step == 0:
        return cells
    cols = cells.shape[1]
    moved = pltpu.roll(cells, step % cols, 1)
    col = lax.broadcasted_iota(jnp.int32, cells.shape, 1)
    keep = col >= step if step > 0 else col < cols + step
    return jnp.where(keep, moved, 0.0)


def deep_kernel(deep, out):
    for plane in range(deep.shape[0]):
        turned = deep[plane].astype(F32).T.astype(BF16)
        out[2 * plane] = turned
        out[2 * plane + 1] = turned


def level_kernel(level, *rest):
    outs, level_t = rest[:-1], rest[-1]
    turned = level[...].astype(F32).T.astype(BF16)
    part = level_t.shape[1]
    for owner in range(len(outs)):
        level_t[owner] = turned[owner * part : (owner + 1) * part]
    me = lax.axis_index("gy")
    for code, out in enumerate(outs):
        out[...] = level_t[jnp.bitwise_xor(me, code)]


def mask_kernel(n_gy, pre, skip, weight, deep_t, *rest):
    outs, down_all = rest[:-1], rest[-1]
    rows, cols, channels = pre.shape
    half = rows // 2
    deep_cols = cols // 2
    cells = half * cols
    deep_cells = half * deep_cols
    wide = lax.broadcasted_iota(jnp.int32, (deep_cells, cells), 1) // 2
    deep = lax.broadcasted_iota(jnp.int32, (deep_cells, cells), 0)
    repeat = (wide == deep).astype(BF16)
    spread = jnp.dot(deep_t[...], repeat, preferred_element_type=F32).astype(BF16)
    col = lax.broadcasted_iota(jnp.int32, (cells, channels), 0) % 2
    count = down_all.shape[1]
    for b in range(2):
        parts = [
            lax.dot_general(
                spread, weight[b, c], (((0,), (1,)), ((), ())), preferred_element_type=F32
            )
            for c in range(2)
        ]
        part = jnp.where(col == 0, parts[0], parts[1]).reshape(half, cols, channels)
        for y in range(half):
            row = 2 * y + b
            pre_row = pre[row].astype(F32)
            total = part[y] + skip[row].astype(F32)
            grad = jnp.where(pre_row > 0, total, 0.0).astype(BF16)
            for out in outs:
                out[pl.ds(row * cols, cols)] = grad
        hidden = jnp.concatenate(
            [jnp.maximum(pre[2 * y + b].astype(F32), 0.0) for y in range(half)], axis=0
        )
        for c in range(2):
            one = jnp.where(col == c, hidden, 0.0).astype(BF16)
            down = lax.dot_general(
                one, spread, (((0,), (1,)), ((), ())), preferred_element_type=F32
            ).astype(BF16)
            for first, owner, inner, take in segments(channels, count, channels, (b * 2 + c) * channels):
                down_all[owner, pl.ds(inner, take)] = down[first : first + take]
    me = lax.axis_index("gy")
    for code, out in enumerate(outs):
        owner = jnp.bitwise_xor(me, code)
        for side in range(down_all.shape[2] // channels):
            out[pl.ds(rows * cols + side * count, count)] = down_all[
                owner, :, pl.ds(side * channels, channels)
            ]


def segments(rows, piece, unit, base=0):
    row = 0
    while row < rows:
        take = min(rows - row, unit - row % unit, piece - (base + row) % piece)
        yield row, (base + row) // piece, (base + row) % piece, take
        row += take


def sides(even, odd):
    upper = lax.axis_index("gz") % 2 == 0
    low = jnp.where(upper, odd[...].astype(F32), even[...].astype(F32)).astype(BF16)
    high = jnp.where(upper, even[...].astype(F32), odd[...].astype(F32)).astype(BF16)
    return low, high


def weight_kernel(n_gy, conv_rows, down_rows, shape, *refs):
    even, own, odd = refs[:3]
    shared = refs[3 : 3 + n_gy]
    parts, near, wide, level = refs[3 + n_gy :]
    rows, cols, channels = shape
    part = own.shape[1]
    cells = rows * cols
    n_gz = parts.shape[0]
    rows_all = n_gy * rows
    me = lax.axis_index("gy")
    low, high = sides(even, odd)
    for edge in (0, rows_all + 1):
        wide[edge] = jnp.zeros(wide.shape[1:], BF16)
    for code in range(n_gy):
        owner = jnp.bitwise_xor(me, code)
        grads = shared[code][pl.ds(0, cells)].reshape(rows, cols, channels).astype(F32)
        for kx in range(3):
            wide[pl.ds(1 + owner * rows, rows), :, pl.ds(kx * channels, channels)] = shifted(
                grads, kx - 1
            ).astype(BF16)
        for kz, plane in enumerate((low[code], own[code], high[code])):
            level[owner, pl.ds(kz * part, part)] = plane
    near[...] = wide[pl.ds(me * rows, rows + 2), :, pl.ds(channels, channels)]
    for ky in range(3):
        total = None
        for owner in range(n_gy):
            slab = wide[pl.ds(2 - ky + owner * rows, rows)].reshape(cells, 3 * channels)
            term = jnp.dot(level[owner], slab, preferred_element_type=F32)
            total = term if total is None else total + term
        total = total.astype(BF16)
        for kz in range(3):
            for kx in range(3):
                value = total[kz * part : (kz + 1) * part, kx * channels : (kx + 1) * channels]
                first = ((kz * 3 + ky) * 3 + kx) * part
                for row, owner, inner, take in segments(part, conv_rows, part, first):
                    parts[owner, pl.ds(inner, take)] = value[row : row + take]
    blank = n_gz * conv_rows - 27 * part
    for row, owner, inner, take in segments(blank, conv_rows, conv_rows, 27 * part):
        parts[owner, pl.ds(inner, take)] = jnp.zeros((take, channels), BF16)
    count = shared[0].shape[0] - cells
    down = shared[0][pl.ds(cells, count)].astype(F32)
    for code in range(1, n_gy):
        down = down + shared[code][pl.ds(cells, count)].astype(F32)
    down = down.astype(BF16)
    for row, owner, inner, take in segments(count, down_rows, count):
        parts[owner, pl.ds(conv_rows + inner, take)] = down[row : row + take]
    blank = n_gz * down_rows - count
    for row, owner, inner, take in segments(blank, down_rows, down_rows, count):
        parts[owner, pl.ds(conv_rows + inner, take)] = jnp.zeros((take, channels), BF16)


def input_kernel(even, own, odd, weight, out):
    rows, cols, channels = out.shape
    low, high = sides(even, odd)
    planes = (low, own, high)
    total = None
    for kz in range(3):
        for ky in range(3):
            slab = planes[2 - kz][2 - ky : 2 - ky + rows].reshape(rows * cols, channels)
            term = lax.dot_general(
                slab,
                weight[kz, ky].reshape(3 * channels, channels),
                (((1,), (1,)), ((), ())),
                preferred_element_type=F32,
            )
            total = term if total is None else total + term
    answer = None
    for kx in range(3):
        part = total[:, kx * channels : (kx + 1) * channels].reshape(rows, cols, channels)
        part = shifted(part, kx - 1)
        answer = part if answer is None else answer + part
    out[...] = answer.astype(BF16)


def reversed_bits(code, count):
    place, bit = 0, 1
    while bit < count:
        place = place * 2 + code // bit % 2
        bit *= 2
    return place


def place_kernel(n_gy, conv_rows, down_rows, *refs):
    blocks, (conv, down) = refs[:n_gy], refs[n_gy:]
    me = lax.axis_index("gy")
    part = conv.shape[2]
    count, deep_channels = down.shape[2:]
    channels = conv.shape[3]
    for code, block in enumerate(blocks):
        column = jnp.bitwise_xor(me, code)
        for row, owner, inner, take in segments(27 * part, conv_rows, part):
            conv[row // part, column, pl.ds(row % part, take)] = block[
                owner, pl.ds(inner, take)
            ]
        for a in range(2):
            base = conv_rows + a * down_rows
            for side in range(deep_channels // channels):
                for row, owner, inner, take in segments(count, down_rows, count, side * count):
                    down[a, column, pl.ds(row, take), pl.ds(side * channels, channels)] = block[
                        owner, pl.ds(base + inner, take)
                    ]


def swapped(value, axis, code):
    return lax.ppermute(value, axis, [(i, i ^ code) for i in range(lax.axis_size(axis))])


def neighbours(value):
    last = lax.axis_size("gz") - 1
    odd = [(i + d, i + 1 - d) for i in range(1, last, 2) for d in range(2)]
    return swapped(value, "gz", 1), lax.ppermute(value, "gz", odd)


def exchanged(value, axis):
    return lax.all_to_all(value, axis, split_axis=0, concat_axis=0, tiled=True)


def per_device(
    level_input, pre_activation, conv_weight, down_weight, skip_cotangent, deep_cotangent
):
    n_gz = lax.axis_size("gz")
    n_gy = lax.axis_size("gy")
    _, rows, cols, channels = level_input.shape
    planes, deep_rows, deep_cols, share = deep_cotangent.shape
    deep_channels = down_weight.shape[4]
    parity = lax.axis_index("gz") % 2
    devices = n_gz * n_gy
    part = channels // n_gy
    cells = rows * cols
    deep_cells = deep_rows * deep_cols
    conv_rows = -(-27 * part // (n_gz * 16)) * 16
    down_count = 4 * deep_channels // n_gy
    down_rows = -(-down_count // (n_gz * 16)) * 16
    piece = conv_rows + down_rows
    shape = jax.ShapeDtypeStruct

    level = level_input.reshape(cells, channels)
    deep = deep_cotangent.reshape(planes, deep_cells, share)
    if share % 16 == 0:
        deep_t = call(deep_kernel, shape((2 * planes, share, deep_cells), BF16), deep)
    else:
        deep_t = jnp.repeat(jnp.swapaxes(deep, 1, 2), 2, axis=0)
    deep_t = exchanged(deep_t, "gz").reshape(deep_channels, deep_cells)
    level_t = call(
        level_kernel,
        [shape((part, cells), BF16)] * n_gy,
        level,
        scratch=[pltpu.VMEM((n_gy, part, cells), BF16)],
    )
    level_t = [swapped(value, "gy", code) if code else value for code, value in enumerate(level_t)]
    level_t = jnp.stack(level_t)
    even, odd = neighbours(level_t)
    deep_t, level_t = lax.optimization_barrier((deep_t, level_t))
    down_slice = lax.dynamic_index_in_dim(down_weight, parity, 0, keepdims=False)
    shared = call(
        lambda *refs: mask_kernel(n_gy, *refs),
        [shape((cells + down_count, channels), BF16)] * n_gy,
        pre_activation[0],
        skip_cotangent[0],
        down_slice,
        deep_t,
        scratch=[pltpu.VMEM((n_gy, 4 * channels // n_gy, deep_channels), BF16)],
    )
    shared = [swapped(value, "gy", code) if code else value for code, value in enumerate(shared)]
    parts, near = call(
        lambda *refs: weight_kernel(n_gy, conv_rows, down_rows, (rows, cols, channels), *refs),
        (
            shape((n_gz, piece, channels), BF16),
            shape((rows + 2, cols, channels), BF16),
        ),
        even,
        level_t,
        odd,
        *shared,
        scratch=[
            pltpu.VMEM((n_gy * rows + 2, cols, 3 * channels), BF16),
            pltpu.VMEM((n_gy, 3 * part, cells), BF16),
        ],
    )
    near_even, near_odd = neighbours(near)
    parts, near_even = lax.optimization_barrier((exchanged(parts, "gz"), near_even))
    parts = parts.astype(F32)
    cell_total = devices * cells
    conv_sum = jnp.sum(parts[:, :conv_rows], axis=0) / math.sqrt(cell_total)
    slots = parts[:, conv_rows:].reshape(n_gz // 2, 2, down_rows, channels)
    down_sum = jnp.sum(slots, axis=0) / math.sqrt(cell_total // 8)
    final = jnp.concatenate([conv_sum, down_sum.reshape(2 * down_rows, channels)], axis=0)
    final = final.astype(BF16)[None]
    block = exchanged(jnp.broadcast_to(final, (n_gz,) + final.shape[1:]), "gz")
    block, near_odd = lax.optimization_barrier((block, near_odd))
    input_grad = call(
        input_kernel,
        shape((rows, cols, channels), BF16),
        near_even,
        near,
        near_odd,
        conv_weight,
    )
    blocks = [block]
    code = n_gy // 2
    while code:
        if code == 1:
            input_grad, *blocks = lax.optimization_barrier((input_grad, *blocks))
        blocks = blocks + [swapped(value, "gy", code) for value in blocks]
        code //= 2
    order = [reversed_bits(place, n_gy) for place in range(n_gy)]
    blocks = [blocks[order[place]] for place in range(n_gy)]
    conv_grad, down_grad = call(
        lambda *refs: place_kernel(n_gy, conv_rows, down_rows, *refs),
        (
            shape((27, n_gy, part, channels), BF16),
            shape((2, n_gy, 4 * channels // n_gy, deep_channels), BF16),
        ),
        *blocks,
    )
    return (
        input_grad[None],
        conv_grad.reshape(conv_weight.shape),
        down_grad.reshape(down_weight.shape),
    )


def solution(mesh):
    return jax.shard_map(
        per_device,
        mesh=mesh,
        in_specs=(
            P("gz", "gy", None, None),
            P("gz", "gy", None, None),
            P(),
            P(),
            P("gz", "gy", None, None),
            P(None, "gy", None, "gz"),
        ),
        out_specs=(P("gz", "gy", None, None), P(), P()),
        check_vma=False,
    )
```

```python
import math

import jax
import jax.numpy as jnp
from jax import lax
from jax.experimental import pallas as pl
from jax.experimental.pallas import tpu as pltpu
from jax.sharding import PartitionSpec as P

F32 = jnp.float32
BF16 = jnp.bfloat16
VMEM_LIMIT = 40 * 1024 * 1024


def call(kernel, out_shape, *operands, scratch=()):
    return pl.pallas_call(
        kernel,
        out_shape=out_shape,
        scratch_shapes=list(scratch),
        compiler_params=pltpu.CompilerParams(vmem_limit_bytes=VMEM_LIMIT),
    )(*operands)


def shifted(cells, step):
    if step == 0:
        return cells
    cols = cells.shape[1]
    moved = pltpu.roll(cells, step % cols, 1)
    col = lax.broadcasted_iota(jnp.int32, cells.shape, 1)
    keep = col >= step if step > 0 else col < cols + step
    return jnp.where(keep, moved, 0.0)


def deep_kernel(deep, keep, send, turned):
    planes = deep.shape[0]
    half = planes // 2
    for plane in range(planes):
        turned[plane] = deep[plane].astype(F32).T.astype(BF16)
    upper = lax.axis_index("gz") // planes
    keep[...] = turned[pl.ds(upper * half, half)]
    send[...] = turned[pl.ds((1 - upper) * half, half)]


def level_kernel(level, *rest):
    outs, level_t = rest[:-1], rest[-1]
    turned = level[...].astype(F32).T.astype(BF16)
    part = level_t.shape[1]
    for owner in range(len(outs)):
        level_t[owner] = turned[owner * part : (owner + 1) * part]
    me = lax.axis_index("gy")
    for code, out in enumerate(outs):
        out[...] = level_t[jnp.bitwise_xor(me, code)]


def mask_kernel(n_gy, pre, skip, weight, *rest):
    deeps, outs, (deep_t, down_all) = rest[: -n_gy - 2], rest[-n_gy - 2 : -2], rest[-2:]
    if len(deeps) > 1:
        count, share = deeps[0].shape[:2]
        me = lax.axis_index("gz")
        for place in range(2 * count):
            owner = jnp.bitwise_xor(me, reversed_bits(place, 2 * count))
            first = pl.multiple_of(owner * share, share)
            deep_t[pl.ds(first, share)] = deeps[place // count][place % count]
    else:
        deep_t[...] = deeps[0][...]
    rows, cols, channels = pre.shape
    half = rows // 2
    deep_cols = cols // 2
    cells = half * cols
    deep_cells = half * deep_cols
    wide = lax.broadcasted_iota(jnp.int32, (deep_cells, cells), 1) // 2
    deep = lax.broadcasted_iota(jnp.int32, (deep_cells, cells), 0)
    repeat = (wide == deep).astype(BF16)
    spread = jnp.dot(deep_t[...], repeat, preferred_element_type=F32).astype(BF16)
    col = lax.broadcasted_iota(jnp.int32, (cells, channels), 0) % 2
    count = down_all.shape[1]
    for b in range(2):
        parts = [
            lax.dot_general(
                spread, weight[b, c], (((0,), (1,)), ((), ())), preferred_element_type=F32
            )
            for c in range(2)
        ]
        part = jnp.where(col == 0, parts[0], parts[1]).reshape(half, cols, channels)
        for y in range(half):
            row = 2 * y + b
            pre_row = pre[row].astype(F32)
            total = part[y] + skip[row].astype(F32)
            grad = jnp.where(pre_row > 0, total, 0.0).astype(BF16)
            for out in outs:
                out[pl.ds(row * cols, cols)] = grad
        hidden = jnp.concatenate(
            [jnp.maximum(pre[2 * y + b].astype(F32), 0.0) for y in range(half)], axis=0
        )
        for c in range(2):
            one = jnp.where(col == c, hidden, 0.0).astype(BF16)
            down = lax.dot_general(
                one, spread, (((0,), (1,)), ((), ())), preferred_element_type=F32
            ).astype(BF16)
            for first, owner, inner, take in segments(channels, count, channels, (b * 2 + c) * channels):
                down_all[owner, pl.ds(inner, take)] = down[first : first + take]
    me = lax.axis_index("gy")
    for code, out in enumerate(outs):
        owner = jnp.bitwise_xor(me, code)
        for side in range(down_all.shape[2] // channels):
            out[pl.ds(rows * cols + side * count, count)] = down_all[
                owner, :, pl.ds(side * channels, channels)
            ]


def segments(rows, piece, unit, base=0):
    row = 0
    while row < rows:
        take = min(rows - row, unit - row % unit, piece - (base + row) % piece)
        yield row, (base + row) // piece, (base + row) % piece, take
        row += take


def sides(even, odd):
    upper = lax.axis_index("gz") % 2 == 0
    low = jnp.where(upper, odd[...].astype(F32), even[...].astype(F32)).astype(BF16)
    high = jnp.where(upper, even[...].astype(F32), odd[...].astype(F32)).astype(BF16)
    return low, high


def weight_kernel(n_gy, shape, *refs):
    even, own, odd = refs[:3]
    shared = refs[3 : 3 + n_gy]
    keep, send, down_out, near, wide, level, halves = refs[3 + n_gy :]
    rows, cols, channels = shape
    part = own.shape[1]
    cells = rows * cols
    half = part // 2
    rows_all = n_gy * rows
    me = lax.axis_index("gy")
    low, high = sides(even, odd)
    for edge in (0, rows_all + 1):
        wide[edge] = jnp.zeros(wide.shape[1:], BF16)
    for code in range(n_gy):
        owner = jnp.bitwise_xor(me, code)
        grads = shared[code][pl.ds(0, cells)].reshape(rows, cols, channels).astype(F32)
        for kx in range(3):
            wide[pl.ds(1 + owner * rows, rows), :, pl.ds(kx * channels, channels)] = shifted(
                grads, kx - 1
            ).astype(BF16)
        for kz, plane in enumerate((low[code], own[code], high[code])):
            level[owner, pl.ds(kz * part, part)] = plane
    near[...] = wide[pl.ds(me * rows, rows + 2), :, pl.ds(channels, channels)]
    for ky in range(3):
        total = None
        for owner in range(n_gy):
            slab = wide[pl.ds(2 - ky + owner * rows, rows)].reshape(cells, 3 * channels)
            term = jnp.dot(level[owner], slab, preferred_element_type=F32)
            total = term if total is None else total + term
        for kz in range(3):
            for kx in range(3):
                value = total[kz * part : (kz + 1) * part, kx * channels : (kx + 1) * channels]
                index = (kz * 3 + ky) * 3 + kx
                for side in range(2):
                    halves[side, pl.ds(index * half, half)] = value[side * half : (side + 1) * half]
    side = lax.axis_index("gz") % 2
    keep[...] = halves[side]
    send[...] = halves[1 - side].astype(send.dtype)
    count = shared[0].shape[0] - cells
    down = shared[0][pl.ds(cells, count)].astype(F32)
    for code in range(1, n_gy):
        down = down + shared[code][pl.ds(cells, count)].astype(F32)
    down_out[...] = down.astype(down_out.dtype)


def input_kernel(even, own, odd, weight, out):
    rows, cols, channels = out.shape
    low, high = sides(even, odd)
    planes = (low, own, high)
    total = None
    for kz in range(3):
        for ky in range(3):
            slab = planes[2 - kz][2 - ky : 2 - ky + rows].reshape(rows * cols, channels)
            term = lax.dot_general(
                slab,
                weight[kz, ky].reshape(3 * channels, channels),
                (((1,), (1,)), ((), ())),
                preferred_element_type=F32,
            )
            total = term if total is None else total + term
    answer = None
    for kx in range(3):
        part = total[:, kx * channels : (kx + 1) * channels].reshape(rows, cols, channels)
        part = shifted(part, kx - 1)
        answer = part if answer is None else answer + part
    out[...] = answer.astype(BF16)


def reversed_bits(code, count):
    place, bit = 0, 1
    while bit < count:
        place = place * 2 + code // bit % 2
        bit *= 2
    return place


def place_kernel(n_gy, *refs):
    blocks, (conv, down) = refs[: 2 * n_gy], refs[2 * n_gy :]
    me = lax.axis_index("gy")
    parity = lax.axis_index("gz") % 2
    half, channels = conv.shape[3:]
    count, deep_channels = down.shape[2:]
    for index, block in enumerate(blocks):
        side = jnp.bitwise_xor(parity, index // n_gy)
        column = jnp.bitwise_xor(me, index % n_gy)
        for k in range(27):
            conv[k, column, side] = block[pl.ds(k * half, half)]
        for wide in range(deep_channels // channels):
            down[side, column, :, pl.ds(wide * channels, channels)] = block[
                pl.ds(27 * half + wide * count, count)
            ]


def swapped(value, axis, code):
    return lax.ppermute(value, axis, [(i, i ^ code) for i in range(lax.axis_size(axis))])


def neighbours(value):
    last = lax.axis_size("gz") - 1
    odd = [(i + d, i + 1 - d) for i in range(1, last, 2) for d in range(2)]
    return swapped(value, "gz", 1), lax.ppermute(value, "gz", odd)


def exchanged(value, axis):
    return lax.all_to_all(value, axis, split_axis=0, concat_axis=0, tiled=True)


def per_device(
    level_input, pre_activation, conv_weight, down_weight, skip_cotangent, deep_cotangent
):
    n_gz = lax.axis_size("gz")
    n_gy = lax.axis_size("gy")
    _, rows, cols, channels = level_input.shape
    planes, deep_rows, deep_cols, share = deep_cotangent.shape
    deep_channels = down_weight.shape[4]
    parity = lax.axis_index("gz") % 2
    devices = n_gz * n_gy
    part = channels // n_gy
    cells = rows * cols
    deep_cells = deep_rows * deep_cols
    half = part // 2
    down_count = 4 * deep_channels // n_gy
    wire = BF16 if n_gz <= 8 else F32
    shape = jax.ShapeDtypeStruct

    level = level_input.reshape(cells, channels)
    deep = deep_cotangent.reshape(planes, deep_cells, share)
    if share % 16 == 0:
        keep, send = call(
            deep_kernel,
            [shape((planes // 2, share, deep_cells), BF16)] * 2,
            deep,
            scratch=[pltpu.VMEM((planes, share, deep_cells), BF16)],
        )
        code = planes
        held = jnp.stack([keep, swapped(send, "gz", code)], axis=1)
        while code > 2:
            code //= 2
            count = code // 2
            upper = lax.axis_index("gz") // code % 2
            keep = lax.dynamic_slice_in_dim(held, upper * count, count, axis=0)
            send = lax.dynamic_slice_in_dim(held, (1 - upper) * count, count, axis=0)
            held = jnp.concatenate([keep, swapped(send, "gz", code)], axis=1)
        deep_t = [held[0], swapped(held[0], "gz", 1)]
    else:
        deep_t = jnp.repeat(jnp.swapaxes(deep, 1, 2), 2, axis=0)
        deep_t = [exchanged(deep_t, "gz").reshape(deep_channels, deep_cells)]
    level_t = call(
        level_kernel,
        [shape((part, cells), BF16)] * n_gy,
        level,
        scratch=[pltpu.VMEM((n_gy, part, cells), BF16)],
    )
    level_t = [swapped(value, "gy", code) if code else value for code, value in enumerate(level_t)]
    level_t = jnp.stack(level_t)
    even, odd = neighbours(level_t)
    *deep_t, level_t = lax.optimization_barrier((*deep_t, level_t))
    down_slice = lax.dynamic_index_in_dim(down_weight, parity, 0, keepdims=False)
    shared = call(
        lambda *refs: mask_kernel(n_gy, *refs),
        [shape((cells + down_count, channels), BF16)] * n_gy,
        pre_activation[0],
        skip_cotangent[0],
        down_slice,
        *deep_t,
        scratch=[
            pltpu.VMEM((deep_channels, deep_cells), BF16),
            pltpu.VMEM((n_gy, 4 * channels // n_gy, deep_channels), BF16),
        ],
    )
    shared = [swapped(value, "gy", code) if code else value for code, value in enumerate(shared)]
    keep, send, down, near = call(
        lambda *refs: weight_kernel(n_gy, (rows, cols, channels), *refs),
        (
            shape((27 * half, channels), F32),
            shape((27 * half, channels), wire),
            shape((down_count, channels), wire),
            shape((rows + 2, cols, channels), BF16),
        ),
        even,
        level_t,
        odd,
        *shared,
        scratch=[
            pltpu.VMEM((n_gy * rows + 2, cols, 3 * channels), BF16),
            pltpu.VMEM((n_gy, 3 * part, cells), BF16),
            pltpu.VMEM((2, 27 * half, channels), F32),
        ],
    )
    near_even, near_odd = neighbours(near)
    conv = (keep + swapped(send, "gz", 1).astype(F32)).astype(wire)
    total = lax.optimization_barrier(jnp.concatenate([conv, down], axis=0))
    code = n_gz // 2
    while code > 1:
        other = swapped(total, "gz", code)
        if code == 4:
            other, near_even = lax.optimization_barrier((other, near_even))
        total = total.astype(F32) + other.astype(F32)
        if code > 2:
            total = lax.optimization_barrier(total.astype(wire))
        code //= 2
    cell_total = devices * cells
    row = lax.broadcasted_iota(jnp.int32, total.shape, 0)
    scale = jnp.where(
        row < 27 * half, 1 / math.sqrt(cell_total), 1 / math.sqrt(cell_total // 8)
    )
    total = (total * scale).astype(BF16)
    pair = [total, swapped(total, "gz", 1)]
    input_grad = call(
        input_kernel,
        shape((rows, cols, channels), BF16),
        near_even,
        near,
        near_odd,
        conv_weight,
    )
    blocks = []
    for index, block in enumerate(pair):
        line = [block]
        code = n_gy // 2
        while code:
            if code == 1 and index == 1:
                input_grad, *line = lax.optimization_barrier((input_grad, *line))
            line = line + [swapped(value, "gy", code) for value in line]
            code //= 2
        blocks += [line[reversed_bits(place, n_gy)] for place in range(n_gy)]
    conv_grad, down_grad = call(
        lambda *refs: place_kernel(n_gy, *refs),
        (
            shape((27, n_gy, 2, half, channels), BF16),
            shape((2, n_gy, 4 * channels // n_gy, deep_channels), BF16),
        ),
        *blocks,
    )
    return (
        input_grad[None],
        conv_grad.reshape(conv_weight.shape),
        down_grad.reshape(down_weight.shape),
    )


def solution(mesh):
    return jax.shard_map(
        per_device,
        mesh=mesh,
        in_specs=(
            P("gz", "gy", None, None),
            P("gz", "gy", None, None),
            P(),
            P(),
            P("gz", "gy", None, None),
            P(None, "gy", None, "gz"),
        ),
        out_specs=(P("gz", "gy", None, None), P(), P()),
        check_vma=False,
    )
```

```python
import math

import jax
import jax.numpy as jnp
from jax import lax
from jax.experimental import pallas as pl
from jax.experimental.pallas import tpu as pltpu
from jax.sharding import PartitionSpec as P

F32 = jnp.float32
BF16 = jnp.bfloat16
VMEM_LIMIT = 40 * 1024 * 1024


def call(kernel, out_shape, *operands, scratch=()):
    return pl.pallas_call(
        kernel,
        out_shape=out_shape,
        scratch_shapes=list(scratch),
        compiler_params=pltpu.CompilerParams(vmem_limit_bytes=VMEM_LIMIT),
    )(*operands)


def shifted(cells, step):
    if step == 0:
        return cells
    cols = cells.shape[1]
    moved = pltpu.roll(cells, step % cols, 1)
    col = lax.broadcasted_iota(jnp.int32, cells.shape, 1)
    keep = col >= step if step > 0 else col < cols + step
    return jnp.where(keep, moved, 0.0)


def deep_kernel(deep, keep, send, turned):
    planes = deep.shape[0]
    half = planes // 2
    for plane in range(planes):
        turned[plane] = deep[plane].astype(F32).T.astype(BF16)
    upper = lax.axis_index("gz") // planes
    keep[...] = turned[pl.ds(upper * half, half)]
    send[...] = turned[pl.ds((1 - upper) * half, half)]


def level_kernel(even, level, odd, *rest):
    outs, level_t = rest[:-1], rest[-1]
    low, high = sides(even, odd)
    part = level.shape[1] // len(outs)
    for kz, plane in enumerate((low, level[...], high)):
        turned = plane.astype(F32).T.astype(BF16)
        for owner in range(len(outs)):
            level_t[owner, pl.ds(kz * part, part)] = turned[owner * part : (owner + 1) * part]
    me = lax.axis_index("gy")
    for code, out in enumerate(outs):
        out[...] = level_t[jnp.bitwise_xor(me, code)]


def mask_kernel(pre, skip, weight, *rest):
    deeps, (grad_out, pair_out, kept, deep_t, down_all) = rest[:-5], rest[-5:]
    if len(deeps) > 1:
        count, share = deeps[0].shape[:2]
        me = lax.axis_index("gz")
        for place in range(2 * count):
            owner = jnp.bitwise_xor(me, reversed_bits(place, 2 * count))
            first = pl.multiple_of(owner * share, share)
            deep_t[pl.ds(first, share)] = deeps[place // count][place % count]
    else:
        deep_t[...] = deeps[0][...]
    rows, cols, channels = pre.shape
    half = rows // 2
    deep_cols = cols // 2
    cells = half * cols
    deep_cells = half * deep_cols
    wide = lax.broadcasted_iota(jnp.int32, (deep_cells, cells), 1) // 2
    deep = lax.broadcasted_iota(jnp.int32, (deep_cells, cells), 0)
    repeat = (wide == deep).astype(BF16)
    spread = jnp.dot(deep_t[...], repeat, preferred_element_type=F32).astype(BF16)
    col = lax.broadcasted_iota(jnp.int32, (cells, channels), 0) % 2
    count = down_all.shape[1]
    for b in range(2):
        parts = [
            lax.dot_general(
                spread, weight[b, c], (((0,), (1,)), ((), ())), preferred_element_type=F32
            )
            for c in range(2)
        ]
        part = jnp.where(col == 0, parts[0], parts[1]).reshape(half, cols, channels)
        for y in range(half):
            row = 2 * y + b
            pre_row = pre[row].astype(F32)
            total = part[y] + skip[row].astype(F32)
            grad = jnp.where(pre_row > 0, total, 0.0).astype(BF16)
            for out in (grad_out, pair_out):
                out[pl.ds(row * cols, cols)] = grad
        hidden = jnp.concatenate(
            [jnp.maximum(pre[2 * y + b].astype(F32), 0.0) for y in range(half)], axis=0
        )
        for c in range(2):
            one = jnp.where(col == c, hidden, 0.0).astype(BF16)
            down = lax.dot_general(
                one, spread, (((0,), (1,)), ((), ())), preferred_element_type=F32
            )
            for first, owner, inner, take in segments(channels, count, channels, (b * 2 + c) * channels):
                down_all[owner, pl.ds(inner, take)] = down[first : first + take]
    me = lax.axis_index("gy")
    for side in range(down_all.shape[2] // channels):
        for far in range(2):
            kept[far, pl.ds(side * count, count)] = down_all[
                jnp.bitwise_xor(me, 2 * far), :, pl.ds(side * channels, channels)
            ]
            first = rows * cols + far * kept.shape[1] + side * count
            pair_out[pl.ds(first, count)] = down_all[
                jnp.bitwise_xor(me, 2 * far + 1), :, pl.ds(side * channels, channels)
            ].astype(BF16)


def segments(rows, piece, unit, base=0):
    row = 0
    while row < rows:
        take = min(rows - row, unit - row % unit, piece - (base + row) % piece)
        yield row, (base + row) // piece, (base + row) % piece, take
        row += take


def sides(even, odd):
    upper = lax.axis_index("gz") % 2 == 0
    low = jnp.where(upper, odd[...].astype(F32), even[...].astype(F32)).astype(BF16)
    high = jnp.where(upper, even[...].astype(F32), odd[...].astype(F32)).astype(BF16)
    return low, high


def weight_kernel(n_gy, shape, *refs):
    levels, shared = refs[:n_gy], refs[n_gy : 2 * n_gy]
    kept, other, keep, send, down_out, near, wide, level, halves = refs[2 * n_gy :]
    rows, cols, channels = shape
    part = levels[0].shape[0] // 3
    cells = rows * cols
    half = part // 2
    rows_all = n_gy * rows
    me = lax.axis_index("gy")
    for edge in (0, rows_all + 1):
        wide[edge] = jnp.zeros(wide.shape[1:], BF16)
    for code in range(n_gy):
        owner = jnp.bitwise_xor(me, code)
        grads = shared[code][pl.ds(0, cells)].reshape(rows, cols, channels).astype(F32)
        for kx in range(3):
            wide[pl.ds(1 + owner * rows, rows), :, pl.ds(kx * channels, channels)] = shifted(
                grads, kx - 1
            ).astype(BF16)
        level[owner] = levels[code][...]
    near[...] = wide[pl.ds(me * rows, rows + 2), :, pl.ds(channels, channels)]
    for ky in range(3):
        total = None
        for owner in range(n_gy):
            slab = wide[pl.ds(2 - ky + owner * rows, rows)].reshape(cells, 3 * channels)
            term = jnp.dot(level[owner], slab, preferred_element_type=F32)
            total = term if total is None else total + term
        for kz in range(3):
            for kx in range(3):
                value = total[kz * part : (kz + 1) * part, kx * channels : (kx + 1) * channels]
                index = (kz * 3 + ky) * 3 + kx
                for side in range(2):
                    halves[side, pl.ds(index * half, half)] = value[side * half : (side + 1) * half]
    side = lax.axis_index("gz") % 2
    keep[...] = halves[side]
    send[...] = halves[1 - side].astype(send.dtype)
    count = other.shape[0]
    down = kept[0] + shared[1][pl.ds(cells, count)].astype(F32) + other[...].astype(F32)
    down_out[...] = down.astype(down_out.dtype)


def input_kernel(even, own, odd, weight, out):
    rows, cols, channels = out.shape
    low, high = sides(even, odd)
    planes = (low, own, high)
    total = None
    for kz in range(3):
        for ky in range(3):
            slab = planes[2 - kz][2 - ky : 2 - ky + rows].reshape(rows * cols, channels)
            term = lax.dot_general(
                slab,
                weight[kz, ky].reshape(3 * channels, channels),
                (((1,), (1,)), ((), ())),
                preferred_element_type=F32,
            )
            total = term if total is None else total + term
    answer = None
    for kx in range(3):
        part = total[:, kx * channels : (kx + 1) * channels].reshape(rows, cols, channels)
        part = shifted(part, kx - 1)
        answer = part if answer is None else answer + part
    out[...] = answer.astype(BF16)


def reversed_bits(code, count):
    place, bit = 0, 1
    while bit < count:
        place = place * 2 + code // bit % 2
        bit *= 2
    return place


def place_kernel(n_gy, *refs):
    blocks, (conv, down) = refs[: 2 * n_gy], refs[2 * n_gy :]
    me = lax.axis_index("gy")
    parity = lax.axis_index("gz") % 2
    half, channels = conv.shape[3:]
    count, deep_channels = down.shape[2:]
    for index, block in enumerate(blocks):
        side = jnp.bitwise_xor(parity, index // n_gy)
        column = jnp.bitwise_xor(me, index % n_gy)
        for k in range(27):
            conv[k, column, side] = block[pl.ds(k * half, half)]
        for wide in range(deep_channels // channels):
            down[side, column, :, pl.ds(wide * channels, channels)] = block[
                pl.ds(27 * half + wide * count, count)
            ]


def swapped(value, axis, code):
    return lax.ppermute(value, axis, [(i, i ^ code) for i in range(lax.axis_size(axis))])


def neighbours(value):
    last = lax.axis_size("gz") - 1
    odd = [(i + d, i + 1 - d) for i in range(1, last, 2) for d in range(2)]
    return swapped(value, "gz", 1), lax.ppermute(value, "gz", odd)


def exchanged(value, axis):
    return lax.all_to_all(value, axis, split_axis=0, concat_axis=0, tiled=True)


def per_device(
    level_input, pre_activation, conv_weight, down_weight, skip_cotangent, deep_cotangent
):
    n_gz = lax.axis_size("gz")
    n_gy = lax.axis_size("gy")
    _, rows, cols, channels = level_input.shape
    planes, deep_rows, deep_cols, share = deep_cotangent.shape
    deep_channels = down_weight.shape[4]
    parity = lax.axis_index("gz") % 2
    devices = n_gz * n_gy
    part = channels // n_gy
    cells = rows * cols
    deep_cells = deep_rows * deep_cols
    half = part // 2
    down_count = 4 * deep_channels // n_gy
    wire = BF16 if n_gz <= 8 else F32
    shape = jax.ShapeDtypeStruct

    level = level_input.reshape(cells, channels)
    deep = deep_cotangent.reshape(planes, deep_cells, share)
    if share % 16 == 0:
        keep, send = call(
            deep_kernel,
            [shape((planes // 2, share, deep_cells), BF16)] * 2,
            deep,
            scratch=[pltpu.VMEM((planes, share, deep_cells), BF16)],
        )
        code = planes
        held = jnp.stack([keep, swapped(send, "gz", code)], axis=1)
        while code > 2:
            code //= 2
            count = code // 2
            upper = lax.axis_index("gz") // code % 2
            keep = lax.dynamic_slice_in_dim(held, upper * count, count, axis=0)
            send = lax.dynamic_slice_in_dim(held, (1 - upper) * count, count, axis=0)
            held = jnp.concatenate([keep, swapped(send, "gz", code)], axis=1)
        deep_t = [held[0], swapped(held[0], "gz", 1)]
    else:
        deep_t = jnp.repeat(jnp.swapaxes(deep, 1, 2), 2, axis=0)
        deep_t = [exchanged(deep_t, "gz").reshape(deep_channels, deep_cells)]
    even, odd = neighbours(level)
    level_t = call(
        level_kernel,
        [shape((3 * part, cells), BF16)] * n_gy,
        even,
        level,
        odd,
        scratch=[pltpu.VMEM((n_gy, 3 * part, cells), BF16)],
    )
    level_t = [swapped(value, "gy", code) if code else value for code, value in enumerate(level_t)]
    tied = lax.optimization_barrier((*deep_t, *level_t))
    deep_t, level_t = tied[:-n_gy], tied[-n_gy:]
    down_slice = lax.dynamic_index_in_dim(down_weight, parity, 0, keepdims=False)
    grad, pair, kept = call(
        mask_kernel,
        [
            shape((cells, channels), BF16),
            shape((cells + 2 * down_count, channels), BF16),
            shape((2, down_count, channels), F32),
        ],
        pre_activation[0],
        skip_cotangent[0],
        down_slice,
        *deep_t,
        scratch=[
            pltpu.VMEM((deep_channels, deep_cells), BF16),
            pltpu.VMEM((n_gy, 4 * channels // n_gy, deep_channels), F32),
        ],
    )
    across = swapped(grad, "gy", 2)
    pair = swapped(pair, "gy", 1)
    other = (kept[1] + pair[cells + down_count :].astype(F32)).astype(BF16)
    other = swapped(other, "gy", 2)
    shared = [grad, pair, across, swapped(across, "gy", 1)]
    keep, send, down, near = call(
        lambda *refs: weight_kernel(n_gy, (rows, cols, channels), *refs),
        (
            shape((27 * half, channels), F32),
            shape((27 * half, channels), wire),
            shape((down_count, channels), wire),
            shape((rows + 2, cols, channels), BF16),
        ),
        *level_t,
        *shared,
        kept,
        other,
        scratch=[
            pltpu.VMEM((n_gy * rows + 2, cols, 3 * channels), BF16),
            pltpu.VMEM((n_gy, 3 * part, cells), BF16),
            pltpu.VMEM((2, 27 * half, channels), F32),
        ],
    )
    near_even, near_odd = neighbours(near)
    conv = (keep + swapped(send, "gz", 1).astype(F32)).astype(wire)
    total = lax.optimization_barrier(jnp.concatenate([conv, down], axis=0))
    code = n_gz // 2
    while code > 1:
        other = swapped(total, "gz", code)
        if code == 4:
            other, near_even = lax.optimization_barrier((other, near_even))
        if code == 2:
            other, near_odd = lax.optimization_barrier((other, near_odd))
        total = total.astype(F32) + other.astype(F32)
        if code > 2:
            total = lax.optimization_barrier(total.astype(wire))
        code //= 2
    cell_total = devices * cells
    row = lax.broadcasted_iota(jnp.int32, total.shape, 0)
    scale = jnp.where(
        row < 27 * half, 1 / math.sqrt(cell_total), 1 / math.sqrt(cell_total // 8)
    )
    total = (total * scale).astype(BF16)
    pair = [total, swapped(total, "gz", 1)]
    input_grad = call(
        input_kernel,
        shape((rows, cols, channels), BF16),
        near_even,
        near,
        near_odd,
        conv_weight,
    )
    blocks = []
    for index, block in enumerate(pair):
        line = [block]
        code = n_gy // 2
        while code:
            if code == 1 and index == 1:
                input_grad, *line = lax.optimization_barrier((input_grad, *line))
            line = line + [swapped(value, "gy", code) for value in line]
            code //= 2
        blocks += [line[reversed_bits(place, n_gy)] for place in range(n_gy)]
    conv_grad, down_grad = call(
        lambda *refs: place_kernel(n_gy, *refs),
        (
            shape((27, n_gy, 2, half, channels), BF16),
            shape((2, n_gy, 4 * channels // n_gy, deep_channels), BF16),
        ),
        *blocks,
    )
    return (
        input_grad[None],
        conv_grad.reshape(conv_weight.shape),
        down_grad.reshape(down_weight.shape),
    )


def solution(mesh):
    return jax.shard_map(
        per_device,
        mesh=mesh,
        in_specs=(
            P("gz", "gy", None, None),
            P("gz", "gy", None, None),
            P(),
            P(),
            P("gz", "gy", None, None),
            P(None, "gy", None, "gz"),
        ),
        out_specs=(P("gz", "gy", None, None), P(), P()),
        check_vma=False,
    )
```

```python
import math

import jax
import jax.numpy as jnp
from jax import lax
from jax.experimental import pallas as pl
from jax.experimental.pallas import tpu as pltpu
from jax.sharding import PartitionSpec as P

F32 = jnp.float32
BF16 = jnp.bfloat16
VMEM_LIMIT = 40 * 1024 * 1024


def call(kernel, out_shape, *operands, scratch=()):
    return pl.pallas_call(
        kernel,
        out_shape=out_shape,
        scratch_shapes=list(scratch),
        compiler_params=pltpu.CompilerParams(vmem_limit_bytes=VMEM_LIMIT),
    )(*operands)


def shifted(cells, step):
    if step == 0:
        return cells
    cols = cells.shape[1]
    moved = pltpu.roll(cells, step % cols, 1)
    col = lax.broadcasted_iota(jnp.int32, cells.shape, 1)
    keep = col >= step if step > 0 else col < cols + step
    return jnp.where(keep, moved, 0.0)


def deep_kernel(deep, keep, send, turned):
    planes = deep.shape[0]
    half = planes // 2
    for plane in range(planes):
        turned[plane] = deep[plane].astype(F32).T.astype(BF16)
    upper = lax.axis_index("gz") // planes
    keep[...] = turned[pl.ds(upper * half, half)]
    send[...] = turned[pl.ds((1 - upper) * half, half)]


def level_kernel(level, *rest):
    outs, level_t = rest[:-1], rest[-1]
    turned = level[...].astype(F32).T.astype(BF16)
    part = level_t.shape[1]
    for owner in range(len(outs)):
        level_t[owner] = turned[owner * part : (owner + 1) * part]
    me = lax.axis_index("gy")
    for code, out in enumerate(outs):
        out[...] = level_t[jnp.bitwise_xor(me, code)]


def mask_kernel(n_gy, pre, skip, weight, *rest):
    deeps, rest = rest[: -n_gy - 3], rest[-n_gy - 3 :]
    grad_out, kept, *outs, deep_t, down_all = rest
    if len(deeps) > 1:
        count, share = deeps[0].shape[:2]
        me = lax.axis_index("gz")
        for place in range(2 * count):
            owner = jnp.bitwise_xor(me, reversed_bits(place, 2 * count))
            first = pl.multiple_of(owner * share, share)
            deep_t[pl.ds(first, share)] = deeps[place // count][place % count]
    else:
        deep_t[...] = deeps[0][...]
    rows, cols, channels = pre.shape
    half = rows // 2
    deep_cols = cols // 2
    cells = half * cols
    deep_cells = half * deep_cols
    wide = lax.broadcasted_iota(jnp.int32, (deep_cells, cells), 1) // 2
    deep = lax.broadcasted_iota(jnp.int32, (deep_cells, cells), 0)
    repeat = (wide == deep).astype(BF16)
    spread = jnp.dot(deep_t[...], repeat, preferred_element_type=F32).astype(BF16)
    col = lax.broadcasted_iota(jnp.int32, (cells, channels), 0) % 2
    count = down_all.shape[1]
    for b in range(2):
        parts = [
            lax.dot_general(
                spread, weight[b, c], (((0,), (1,)), ((), ())), preferred_element_type=F32
            )
            for c in range(2)
        ]
        part = jnp.where(col == 0, parts[0], parts[1]).reshape(half, cols, channels)
        for y in range(half):
            row = 2 * y + b
            pre_row = pre[row].astype(F32)
            total = part[y] + skip[row].astype(F32)
            grad = jnp.where(pre_row > 0, total, 0.0).astype(BF16)
            grad_out[pl.ds(row * cols, cols)] = grad
        hidden = jnp.concatenate(
            [jnp.maximum(pre[2 * y + b].astype(F32), 0.0) for y in range(half)], axis=0
        )
        for c in range(2):
            one = jnp.where(col == c, hidden, 0.0).astype(BF16)
            down = lax.dot_general(
                one, spread, (((0,), (1,)), ((), ())), preferred_element_type=F32
            )
            for first, owner, inner, take in segments(channels, count, channels, (b * 2 + c) * channels):
                down_all[owner, pl.ds(inner, take)] = down[first : first + take]
    me = lax.axis_index("gy")
    for code, out in enumerate([kept, *outs]):
        owner = jnp.bitwise_xor(me, code)
        for side in range(down_all.shape[2] // channels):
            out[pl.ds(side * count, count)] = down_all[
                owner, :, pl.ds(side * channels, channels)
            ].astype(out.dtype)


def segments(rows, piece, unit, base=0):
    row = 0
    while row < rows:
        take = min(rows - row, unit - row % unit, piece - (base + row) % piece)
        yield row, (base + row) // piece, (base + row) % piece, take
        row += take


def sides(even, odd):
    upper = lax.axis_index("gz") % 2 == 0
    low = jnp.where(upper, odd[...].astype(F32), even[...].astype(F32)).astype(BF16)
    high = jnp.where(upper, even[...].astype(F32), odd[...].astype(F32)).astype(BF16)
    return low, high


def weight_kernel(n_gy, shape, *refs):
    even, own, odd = refs[:3]
    shared = refs[3 : 3 + n_gy]
    keep, send, near, wide, level, halves = refs[3 + n_gy :]
    rows, cols, channels = shape
    part = own.shape[1]
    cells = rows * cols
    half = part // 2
    rows_all = n_gy * rows
    me = lax.axis_index("gy")
    low, high = sides(even, odd)
    for edge in (0, rows_all + 1):
        wide[edge] = jnp.zeros(wide.shape[1:], BF16)
    for code in range(n_gy):
        owner = jnp.bitwise_xor(me, code)
        grads = shared[code][pl.ds(0, cells)].reshape(rows, cols, channels).astype(F32)
        for kx in range(3):
            wide[pl.ds(1 + owner * rows, rows), :, pl.ds(kx * channels, channels)] = shifted(
                grads, kx - 1
            ).astype(BF16)
        for kz, plane in enumerate((low[code], own[code], high[code])):
            level[owner, pl.ds(kz * part, part)] = plane
    near[...] = wide[pl.ds(me * rows, rows + 2), :, pl.ds(channels, channels)]
    for ky in range(3):
        total = None
        for owner in range(n_gy):
            slab = wide[pl.ds(2 - ky + owner * rows, rows)].reshape(cells, 3 * channels)
            term = jnp.dot(level[owner], slab, preferred_element_type=F32)
            total = term if total is None else total + term
        for kz in range(3):
            for kx in range(3):
                value = total[kz * part : (kz + 1) * part, kx * channels : (kx + 1) * channels]
                index = (kz * 3 + ky) * 3 + kx
                for side in range(2):
                    halves[side, pl.ds(index * half, half)] = value[side * half : (side + 1) * half]
    side = lax.axis_index("gz") % 2
    keep[...] = halves[side]
    send[...] = halves[1 - side].astype(send.dtype)


def input_kernel(even, own, odd, weight, out):
    rows, cols, channels = out.shape
    low, high = sides(even, odd)
    planes = (low, own, high)
    total = None
    for kz in range(3):
        for ky in range(3):
            slab = planes[2 - kz][2 - ky : 2 - ky + rows].reshape(rows * cols, channels)
            term = lax.dot_general(
                slab,
                weight[kz, ky].reshape(3 * channels, channels),
                (((1,), (1,)), ((), ())),
                preferred_element_type=F32,
            )
            total = term if total is None else total + term
    answer = None
    for kx in range(3):
        part = total[:, kx * channels : (kx + 1) * channels].reshape(rows, cols, channels)
        part = shifted(part, kx - 1)
        answer = part if answer is None else answer + part
    out[...] = answer.astype(BF16)


def reversed_bits(code, count):
    place, bit = 0, 1
    while bit < count:
        place = place * 2 + code // bit % 2
        bit *= 2
    return place


def place_kernel(n_gy, *refs):
    blocks, (conv, down) = refs[: 2 * n_gy], refs[2 * n_gy :]
    me = lax.axis_index("gy")
    parity = lax.axis_index("gz") % 2
    half, channels = conv.shape[3:]
    count, deep_channels = down.shape[2:]
    for index, block in enumerate(blocks):
        side = jnp.bitwise_xor(parity, index // n_gy)
        column = jnp.bitwise_xor(me, index % n_gy)
        for k in range(27):
            conv[k, column, side] = block[pl.ds(k * half, half)]
        for wide in range(deep_channels // channels):
            down[side, column, :, pl.ds(wide * channels, channels)] = block[
                pl.ds(27 * half + wide * count, count)
            ]


def swapped(value, axis, code):
    return lax.ppermute(value, axis, [(i, i ^ code) for i in range(lax.axis_size(axis))])


def neighbours(value):
    last = lax.axis_size("gz") - 1
    odd = [(i + d, i + 1 - d) for i in range(1, last, 2) for d in range(2)]
    return swapped(value, "gz", 1), lax.ppermute(value, "gz", odd)


def exchanged(value, axis):
    return lax.all_to_all(value, axis, split_axis=0, concat_axis=0, tiled=True)


def per_device(
    level_input, pre_activation, conv_weight, down_weight, skip_cotangent, deep_cotangent
):
    n_gz = lax.axis_size("gz")
    n_gy = lax.axis_size("gy")
    _, rows, cols, channels = level_input.shape
    planes, deep_rows, deep_cols, share = deep_cotangent.shape
    deep_channels = down_weight.shape[4]
    parity = lax.axis_index("gz") % 2
    devices = n_gz * n_gy
    part = channels // n_gy
    cells = rows * cols
    deep_cells = deep_rows * deep_cols
    half = part // 2
    down_count = 4 * deep_channels // n_gy
    wire = BF16 if n_gz <= 8 else F32
    shape = jax.ShapeDtypeStruct

    level = level_input.reshape(cells, channels)
    deep = deep_cotangent.reshape(planes, deep_cells, share)
    if share % 16 == 0:
        keep, send = call(
            deep_kernel,
            [shape((planes // 2, share, deep_cells), BF16)] * 2,
            deep,
            scratch=[pltpu.VMEM((planes, share, deep_cells), BF16)],
        )
        code = planes
        held = jnp.stack([keep, swapped(send, "gz", code)], axis=1)
        while code > 2:
            code //= 2
            count = code // 2
            upper = lax.axis_index("gz") // code % 2
            keep = lax.dynamic_slice_in_dim(held, upper * count, count, axis=0)
            send = lax.dynamic_slice_in_dim(held, (1 - upper) * count, count, axis=0)
            held = jnp.concatenate([keep, swapped(send, "gz", code)], axis=1)
        deep_t = [held[0], swapped(held[0], "gz", 1)]
    else:
        deep_t = jnp.repeat(jnp.swapaxes(deep, 1, 2), 2, axis=0)
        deep_t = [exchanged(deep_t, "gz").reshape(deep_channels, deep_cells)]
    level_t = call(
        level_kernel,
        [shape((part, cells), BF16)] * n_gy,
        level,
        scratch=[pltpu.VMEM((n_gy, part, cells), BF16)],
    )
    level_t = [swapped(value, "gy", code) if code else value for code, value in enumerate(level_t)]
    level_t = jnp.stack(level_t)
    even, odd = neighbours(level_t)
    *deep_t, even, odd = lax.optimization_barrier((*deep_t, even, odd))
    down_slice = lax.dynamic_index_in_dim(down_weight, parity, 0, keepdims=False)
    grad, down, *others = call(
        lambda *refs: mask_kernel(n_gy, *refs),
        [shape((cells, channels), BF16), shape((down_count, channels), F32)]
        + [shape((down_count, channels), BF16)] * (n_gy - 1),
        pre_activation[0],
        skip_cotangent[0],
        down_slice,
        *deep_t,
        scratch=[
            pltpu.VMEM((deep_channels, deep_cells), BF16),
            pltpu.VMEM((n_gy, 4 * channels // n_gy, deep_channels), F32),
        ],
    )
    shared = [swapped(grad, "gy", code) if code else grad for code in range(n_gy)]
    for code, value in enumerate(others):
        down = down + swapped(value, "gy", code + 1).astype(F32)
    keep, send, near = call(
        lambda *refs: weight_kernel(n_gy, (rows, cols, channels), *refs),
        (
            shape((27 * half, channels), F32),
            shape((27 * half, channels), wire),
            shape((rows + 2, cols, channels), BF16),
        ),
        even,
        level_t,
        odd,
        *shared,
        scratch=[
            pltpu.VMEM((n_gy * rows + 2, cols, 3 * channels), BF16),
            pltpu.VMEM((n_gy, 3 * part, cells), BF16),
            pltpu.VMEM((2, 27 * half, channels), F32),
        ],
    )
    near_even, near_odd = neighbours(near)
    conv = (keep + swapped(send, "gz", 1).astype(F32)).astype(wire)
    total = jnp.concatenate([conv, down.astype(wire)], axis=0)
    total = lax.optimization_barrier(total)
    code = n_gz // 2
    while code > 1:
        other = swapped(total, "gz", code)
        if code == 4:
            other, near_even = lax.optimization_barrier((other, near_even))
        total = total.astype(F32) + other.astype(F32)
        if code > 2:
            total = lax.optimization_barrier(total.astype(wire))
        code //= 2
    cell_total = devices * cells
    row = lax.broadcasted_iota(jnp.int32, total.shape, 0)
    scale = jnp.where(
        row < 27 * half, 1 / math.sqrt(cell_total), 1 / math.sqrt(cell_total // 8)
    )
    total = (total * scale).astype(BF16)
    pair = [total, swapped(total, "gz", 1)]
    pair[1], near_odd = lax.optimization_barrier((pair[1], near_odd))
    input_grad = call(
        input_kernel,
        shape((rows, cols, channels), BF16),
        near_even,
        near,
        near_odd,
        conv_weight,
    )
    blocks = []
    for index, block in enumerate(pair):
        line = [block]
        code = n_gy // 2
        while code:
            if code == 1 and index == 1:
                input_grad, *line = lax.optimization_barrier((input_grad, *line))
            line = line + [swapped(value, "gy", code) for value in line]
            code //= 2
        blocks += [line[reversed_bits(place, n_gy)] for place in range(n_gy)]
    conv_grad, down_grad = call(
        lambda *refs: place_kernel(n_gy, *refs),
        (
            shape((27, n_gy, 2, half, channels), BF16),
            shape((2, n_gy, 4 * channels // n_gy, deep_channels), BF16),
        ),
        *blocks,
    )
    return (
        input_grad[None],
        conv_grad.reshape(conv_weight.shape),
        down_grad.reshape(down_weight.shape),
    )


def solution(mesh):
    return jax.shard_map(
        per_device,
        mesh=mesh,
        in_specs=(
            P("gz", "gy", None, None),
            P("gz", "gy", None, None),
            P(),
            P(),
            P("gz", "gy", None, None),
            P(None, "gy", None, "gz"),
        ),
        out_specs=(P("gz", "gy", None, None), P(), P()),
        check_vma=False,
    )
```

```python
import math

import jax
import jax.numpy as jnp
from jax import lax
from jax.experimental import pallas as pl
from jax.experimental.pallas import tpu as pltpu
from jax.sharding import PartitionSpec as P

F32 = jnp.float32
BF16 = jnp.bfloat16
VMEM_LIMIT = 40 * 1024 * 1024


def call(kernel, out_shape, *operands, scratch=()):
    return pl.pallas_call(
        kernel,
        out_shape=out_shape,
        scratch_shapes=list(scratch),
        compiler_params=pltpu.CompilerParams(vmem_limit_bytes=VMEM_LIMIT),
    )(*operands)


def shifted(cells, step):
    if step == 0:
        return cells
    cols = cells.shape[1]
    moved = pltpu.roll(cells, step % cols, 1)
    col = lax.broadcasted_iota(jnp.int32, cells.shape, 1)
    keep = col >= step if step > 0 else col < cols + step
    return jnp.where(keep, moved, 0.0)


def deep_kernel(deep, keep, send, turned):
    planes = deep.shape[0]
    half = planes // 2
    for plane in range(planes):
        turned[plane] = deep[plane].astype(F32).T.astype(BF16)
    upper = lax.axis_index("gz") // planes
    keep[...] = turned[pl.ds(upper * half, half)]
    send[...] = turned[pl.ds((1 - upper) * half, half)]


def level_kernel(level, *rest):
    outs, level_t = rest[:-1], rest[-1]
    turned = level[...].astype(F32).T.astype(BF16)
    part = level_t.shape[1]
    for owner in range(len(outs)):
        level_t[owner] = turned[owner * part : (owner + 1) * part]
    me = lax.axis_index("gy")
    for code, out in enumerate(outs):
        out[...] = level_t[jnp.bitwise_xor(me, code)]


def mask_kernel(n_gy, pre, skip, weight, *rest):
    deeps, rest = rest[: -n_gy - 3], rest[-n_gy - 3 :]
    grad_out, kept, *outs, deep_t, down_all = rest
    if len(deeps) > 1:
        count, share = deeps[0].shape[:2]
        me = lax.axis_index("gz")
        for place in range(2 * count):
            owner = jnp.bitwise_xor(me, reversed_bits(place, 2 * count))
            first = pl.multiple_of(owner * share, share)
            deep_t[pl.ds(first, share)] = deeps[place // count][place % count]
    else:
        deep_t[...] = deeps[0][...]
    rows, cols, channels = pre.shape
    half = rows // 2
    deep_cols = cols // 2
    cells = half * cols
    deep_cells = half * deep_cols
    wide = lax.broadcasted_iota(jnp.int32, (deep_cells, cells), 1) // 2
    deep = lax.broadcasted_iota(jnp.int32, (deep_cells, cells), 0)
    repeat = (wide == deep).astype(BF16)
    spread = jnp.dot(deep_t[...], repeat, preferred_element_type=F32).astype(BF16)
    col = lax.broadcasted_iota(jnp.int32, (cells, channels), 0) % 2
    count = down_all.shape[1]
    for b in range(2):
        parts = [
            lax.dot_general(
                spread, weight[b, c], (((0,), (1,)), ((), ())), preferred_element_type=F32
            )
            for c in range(2)
        ]
        part = jnp.where(col == 0, parts[0], parts[1]).reshape(half, cols, channels)
        for y in range(half):
            row = 2 * y + b
            pre_row = pre[row].astype(F32)
            total = part[y] + skip[row].astype(F32)
            grad = jnp.where(pre_row > 0, total, 0.0).astype(BF16)
            grad_out[pl.ds(row * cols, cols)] = grad
        hidden = jnp.concatenate(
            [jnp.maximum(pre[2 * y + b].astype(F32), 0.0) for y in range(half)], axis=0
        )
        for c in range(2):
            one = jnp.where(col == c, hidden, 0.0).astype(BF16)
            down = lax.dot_general(
                one, spread, (((0,), (1,)), ((), ())), preferred_element_type=F32
            )
            for first, owner, inner, take in segments(channels, count, channels, (b * 2 + c) * channels):
                down_all[owner, pl.ds(inner, take)] = down[first : first + take]
    me = lax.axis_index("gy")
    for code, out in enumerate([kept, *outs]):
        owner = jnp.bitwise_xor(me, code)
        for side in range(down_all.shape[2] // channels):
            out[pl.ds(side * count, count)] = down_all[
                owner, :, pl.ds(side * channels, channels)
            ].astype(out.dtype)


def segments(rows, piece, unit, base=0):
    row = 0
    while row < rows:
        take = min(rows - row, unit - row % unit, piece - (base + row) % piece)
        yield row, (base + row) // piece, (base + row) % piece, take
        row += take


def sides(even, odd):
    upper = lax.axis_index("gz") % 2 == 0
    low = jnp.where(upper, odd[...].astype(F32), even[...].astype(F32)).astype(BF16)
    high = jnp.where(upper, even[...].astype(F32), odd[...].astype(F32)).astype(BF16)
    return low, high


def weight_kernel(n_gy, shape, *refs):
    even, own, odd = refs[:3]
    shared = refs[3 : 3 + n_gy]
    keep, send, near, wide, level, halves = refs[3 + n_gy :]
    rows, cols, channels = shape
    part = own.shape[1]
    cells = rows * cols
    half = part // 2
    rows_all = n_gy * rows
    me = lax.axis_index("gy")
    low, high = sides(even, odd)
    for edge in (0, rows_all + 1):
        wide[edge] = jnp.zeros(wide.shape[1:], BF16)
    for code in range(n_gy):
        owner = jnp.bitwise_xor(me, code)
        grads = shared[code][pl.ds(0, cells)].reshape(rows, cols, channels).astype(F32)
        for kx in range(3):
            wide[pl.ds(1 + owner * rows, rows), :, pl.ds(kx * channels, channels)] = shifted(
                grads, kx - 1
            ).astype(BF16)
        for kz, plane in enumerate((low[code], own[code], high[code])):
            level[owner, pl.ds(kz * part, part)] = plane
    near[...] = wide[pl.ds(me * rows, rows + 2), :, pl.ds(channels, channels)]
    for ky in range(3):
        total = None
        for owner in range(n_gy):
            slab = wide[pl.ds(2 - ky + owner * rows, rows)].reshape(cells, 3 * channels)
            term = jnp.dot(level[owner], slab, preferred_element_type=F32)
            total = term if total is None else total + term
        for kz in range(3):
            for kx in range(3):
                value = total[kz * part : (kz + 1) * part, kx * channels : (kx + 1) * channels]
                index = (kz * 3 + ky) * 3 + kx
                for side in range(2):
                    halves[side, pl.ds(index * half, half)] = value[side * half : (side + 1) * half]
    side = lax.axis_index("gz") % 2
    keep[...] = halves[side]
    send[...] = halves[1 - side].astype(send.dtype)


def input_kernel(even, own, odd, weight, out):
    rows, cols, channels = out.shape
    low, high = sides(even, odd)
    planes = (low, own, high)
    total = None
    for kz in range(3):
        for ky in range(3):
            slab = planes[2 - kz][2 - ky : 2 - ky + rows].reshape(rows * cols, channels)
            term = lax.dot_general(
                slab,
                weight[kz, ky].reshape(3 * channels, channels),
                (((1,), (1,)), ((), ())),
                preferred_element_type=F32,
            )
            total = term if total is None else total + term
    answer = None
    for kx in range(3):
        part = total[:, kx * channels : (kx + 1) * channels].reshape(rows, cols, channels)
        part = shifted(part, kx - 1)
        answer = part if answer is None else answer + part
    out[...] = answer.astype(BF16)


def reversed_bits(code, count):
    place, bit = 0, 1
    while bit < count:
        place = place * 2 + code // bit % 2
        bit *= 2
    return place


def place_kernel(n_gy, *refs):
    blocks, (conv, down) = refs[: 2 * n_gy], refs[2 * n_gy :]
    me = lax.axis_index("gy")
    parity = lax.axis_index("gz") % 2
    half, channels = conv.shape[3:]
    count, deep_channels = down.shape[2:]
    for index, block in enumerate(blocks):
        side = jnp.bitwise_xor(parity, index // n_gy)
        column = jnp.bitwise_xor(me, index % n_gy)
        for k in range(27):
            conv[k, column, side] = block[pl.ds(k * half, half)]
        for wide in range(deep_channels // channels):
            down[side, column, :, pl.ds(wide * channels, channels)] = block[
                pl.ds(27 * half + wide * count, count)
            ]


def swapped(value, axis, code):
    return lax.ppermute(value, axis, [(i, i ^ code) for i in range(lax.axis_size(axis))])


def neighbours(value):
    last = lax.axis_size("gz") - 1
    odd = [(i + d, i + 1 - d) for i in range(1, last, 2) for d in range(2)]
    return swapped(value, "gz", 1), lax.ppermute(value, "gz", odd)


def exchanged(value, axis):
    return lax.all_to_all(value, axis, split_axis=0, concat_axis=0, tiled=True)


def per_device(
    level_input, pre_activation, conv_weight, down_weight, skip_cotangent, deep_cotangent
):
    n_gz = lax.axis_size("gz")
    n_gy = lax.axis_size("gy")
    _, rows, cols, channels = level_input.shape
    planes, deep_rows, deep_cols, share = deep_cotangent.shape
    deep_channels = down_weight.shape[4]
    parity = lax.axis_index("gz") % 2
    devices = n_gz * n_gy
    part = channels // n_gy
    cells = rows * cols
    deep_cells = deep_rows * deep_cols
    half = part // 2
    down_count = 4 * deep_channels // n_gy
    wire = BF16 if n_gz <= 8 else F32
    shape = jax.ShapeDtypeStruct

    level = level_input.reshape(cells, channels)
    deep = deep_cotangent.reshape(planes, deep_cells, share)
    if share % 16 == 0:
        keep, send = call(
            deep_kernel,
            [shape((planes // 2, share, deep_cells), BF16)] * 2,
            deep,
            scratch=[pltpu.VMEM((planes, share, deep_cells), BF16)],
        )
        code = planes
        held = jnp.stack([keep, swapped(send, "gz", code)], axis=1)
        while code > 2:
            code //= 2
            count = code // 2
            upper = lax.axis_index("gz") // code % 2
            keep = lax.dynamic_slice_in_dim(held, upper * count, count, axis=0)
            send = lax.dynamic_slice_in_dim(held, (1 - upper) * count, count, axis=0)
            held = jnp.concatenate([keep, swapped(send, "gz", code)], axis=1)
        deep_t = [held[0], swapped(held[0], "gz", 1)]
    else:
        deep_t = jnp.repeat(jnp.swapaxes(deep, 1, 2), 2, axis=0)
        deep_t = [exchanged(deep_t, "gz").reshape(deep_channels, deep_cells)]
    level_t = call(
        level_kernel,
        [shape((part, cells), BF16)] * n_gy,
        level,
        scratch=[pltpu.VMEM((n_gy, part, cells), BF16)],
    )
    level_t = [swapped(value, "gy", code) if code else value for code, value in enumerate(level_t)]
    level_t = jnp.stack(level_t)
    even, odd = neighbours(level_t)
    *deep_t, level_t = lax.optimization_barrier((*deep_t, level_t))
    down_slice = lax.dynamic_index_in_dim(down_weight, parity, 0, keepdims=False)
    grad, down, *others = call(
        lambda *refs: mask_kernel(n_gy, *refs),
        [shape((cells, channels), BF16), shape((down_count, channels), F32)]
        + [shape((down_count, channels), BF16)] * (n_gy - 1),
        pre_activation[0],
        skip_cotangent[0],
        down_slice,
        *deep_t,
        scratch=[
            pltpu.VMEM((deep_channels, deep_cells), BF16),
            pltpu.VMEM((n_gy, 4 * channels // n_gy, deep_channels), F32),
        ],
    )
    shared = [swapped(grad, "gy", code) if code else grad for code in range(n_gy)]
    even, odd, *others = lax.optimization_barrier((even, odd, *others))
    for code, value in enumerate(others):
        down = down + swapped(value, "gy", code + 1).astype(F32)
    keep, send, near = call(
        lambda *refs: weight_kernel(n_gy, (rows, cols, channels), *refs),
        (
            shape((27 * half, channels), F32),
            shape((27 * half, channels), wire),
            shape((rows + 2, cols, channels), BF16),
        ),
        even,
        level_t,
        odd,
        *shared,
        scratch=[
            pltpu.VMEM((n_gy * rows + 2, cols, 3 * channels), BF16),
            pltpu.VMEM((n_gy, 3 * part, cells), BF16),
            pltpu.VMEM((2, 27 * half, channels), F32),
        ],
    )
    near_even, near_odd = neighbours(near)
    conv = (keep + swapped(send, "gz", 1).astype(F32)).astype(wire)
    total = jnp.concatenate([conv, down.astype(wire)], axis=0)
    total = lax.optimization_barrier(total)
    code = n_gz // 2
    while code > 1:
        other = swapped(total, "gz", code)
        if code == 4:
            other, near_even, near_odd = lax.optimization_barrier((other, near_even, near_odd))
        if code == 2:
            input_grad = call(
                input_kernel,
                shape((rows, cols, channels), BF16),
                near_even,
                near,
                near_odd,
                conv_weight,
            )
            other, input_grad = lax.optimization_barrier((other, input_grad))
        total = total.astype(F32) + other.astype(F32)
        if code > 2:
            total = lax.optimization_barrier(total.astype(wire))
        code //= 2
    cell_total = devices * cells
    row = lax.broadcasted_iota(jnp.int32, total.shape, 0)
    scale = jnp.where(
        row < 27 * half, 1 / math.sqrt(cell_total), 1 / math.sqrt(cell_total // 8)
    )
    total = (total * scale).astype(BF16)
    pair = [total, swapped(total, "gz", 1)]
    blocks = []
    for index, block in enumerate(pair):
        line = [block]
        code = n_gy // 2
        while code:
            line = line + [swapped(value, "gy", code) for value in line]
            code //= 2
        blocks += [line[reversed_bits(place, n_gy)] for place in range(n_gy)]
    conv_grad, down_grad = call(
        lambda *refs: place_kernel(n_gy, *refs),
        (
            shape((27, n_gy, 2, half, channels), BF16),
            shape((2, n_gy, 4 * channels // n_gy, deep_channels), BF16),
        ),
        *blocks,
    )
    return (
        input_grad[None],
        conv_grad.reshape(conv_weight.shape),
        down_grad.reshape(down_weight.shape),
    )


def solution(mesh):
    return jax.shard_map(
        per_device,
        mesh=mesh,
        in_specs=(
            P("gz", "gy", None, None),
            P("gz", "gy", None, None),
            P(),
            P(),
            P("gz", "gy", None, None),
            P(None, "gy", None, "gz"),
        ),
        out_specs=(P("gz", "gy", None, None), P(), P()),
        check_vma=False,
    )
```

```python
import math

import jax
import jax.numpy as jnp
from jax import lax
from jax.experimental import pallas as pl
from jax.experimental.pallas import tpu as pltpu
from jax.sharding import PartitionSpec as P

F32 = jnp.float32
BF16 = jnp.bfloat16
VMEM_LIMIT = 40 * 1024 * 1024


def call(kernel, out_shape, *operands, scratch=()):
    return pl.pallas_call(
        kernel,
        out_shape=out_shape,
        scratch_shapes=list(scratch),
        compiler_params=pltpu.CompilerParams(vmem_limit_bytes=VMEM_LIMIT),
    )(*operands)


def shifted(cells, step):
    if step == 0:
        return cells
    cols = cells.shape[1]
    moved = pltpu.roll(cells, step % cols, 1)
    col = lax.broadcasted_iota(jnp.int32, cells.shape, 1)
    keep = col >= step if step > 0 else col < cols + step
    return jnp.where(keep, moved, 0.0)


def deep_kernel(deep, keep, send, turned):
    planes = deep.shape[0]
    half = planes // 2
    for plane in range(planes):
        turned[plane] = deep[plane].astype(F32).T.astype(BF16)
    upper = lax.axis_index("gz") // planes
    keep[...] = turned[pl.ds(upper * half, half)]
    send[...] = turned[pl.ds((1 - upper) * half, half)]


def level_kernel(level, *rest):
    outs, level_t = rest[:-1], rest[-1]
    turned = level[...].astype(F32).T.astype(BF16)
    part = level_t.shape[1]
    for owner in range(len(outs)):
        level_t[owner] = turned[owner * part : (owner + 1) * part]
    me = lax.axis_index("gy")
    for code, out in enumerate(outs):
        out[...] = level_t[jnp.bitwise_xor(me, code)]


def mask_kernel(n_gy, pre, skip, weight, *rest):
    deeps, rest = rest[: -n_gy - 3], rest[-n_gy - 3 :]
    grad_out, kept, *outs, deep_t, down_all = rest
    if len(deeps) > 1:
        count, share = deeps[0].shape[:2]
        me = lax.axis_index("gz")
        for place in range(2 * count):
            owner = jnp.bitwise_xor(me, reversed_bits(place, 2 * count))
            first = pl.multiple_of(owner * share, share)
            deep_t[pl.ds(first, share)] = deeps[place // count][place % count]
    else:
        deep_t[...] = deeps[0][...]
    rows, cols, channels = pre.shape
    half = rows // 2
    deep_cols = cols // 2
    cells = half * cols
    deep_cells = half * deep_cols
    wide = lax.broadcasted_iota(jnp.int32, (deep_cells, cells), 1) // 2
    deep = lax.broadcasted_iota(jnp.int32, (deep_cells, cells), 0)
    repeat = (wide == deep).astype(BF16)
    spread = jnp.dot(deep_t[...], repeat, preferred_element_type=F32).astype(BF16)
    col = lax.broadcasted_iota(jnp.int32, (cells, channels), 0) % 2
    count = down_all.shape[1]
    for b in range(2):
        parts = [
            lax.dot_general(
                spread, weight[b, c], (((0,), (1,)), ((), ())), preferred_element_type=F32
            )
            for c in range(2)
        ]
        part = jnp.where(col == 0, parts[0], parts[1]).reshape(half, cols, channels)
        for y in range(half):
            row = 2 * y + b
            pre_row = pre[row].astype(F32)
            total = part[y] + skip[row].astype(F32)
            grad = jnp.where(pre_row > 0, total, 0.0).astype(BF16)
            grad_out[pl.ds(row * cols, cols)] = grad
        hidden = jnp.concatenate(
            [jnp.maximum(pre[2 * y + b].astype(F32), 0.0) for y in range(half)], axis=0
        )
        for c in range(2):
            one = jnp.where(col == c, hidden, 0.0).astype(BF16)
            down = lax.dot_general(
                one, spread, (((0,), (1,)), ((), ())), preferred_element_type=F32
            )
            for first, owner, inner, take in segments(channels, count, channels, (b * 2 + c) * channels):
                down_all[owner, pl.ds(inner, take)] = down[first : first + take]
    me = lax.axis_index("gy")
    for code, out in enumerate([kept, *outs]):
        owner = jnp.bitwise_xor(me, code)
        for side in range(down_all.shape[2] // channels):
            out[pl.ds(side * count, count)] = down_all[
                owner, :, pl.ds(side * channels, channels)
            ].astype(out.dtype)


def segments(rows, piece, unit, base=0):
    row = 0
    while row < rows:
        take = min(rows - row, unit - row % unit, piece - (base + row) % piece)
        yield row, (base + row) // piece, (base + row) % piece, take
        row += take


def sides(even, odd):
    upper = lax.axis_index("gz") % 2 == 0
    low = jnp.where(upper, odd[...].astype(F32), even[...].astype(F32)).astype(BF16)
    high = jnp.where(upper, even[...].astype(F32), odd[...].astype(F32)).astype(BF16)
    return low, high


def weight_kernel(n_gy, shape, *refs):
    even, own, odd = refs[:3]
    shared = refs[3 : 3 + n_gy]
    keep, send, near, wide, level, halves = refs[3 + n_gy :]
    rows, cols, channels = shape
    part = own.shape[1]
    cells = rows * cols
    half = part // 2
    rows_all = n_gy * rows
    me = lax.axis_index("gy")
    low, high = sides(even, odd)
    for edge in (0, rows_all + 1):
        wide[edge] = jnp.zeros(wide.shape[1:], BF16)
    for code in range(n_gy):
        owner = jnp.bitwise_xor(me, code)
        grads = shared[code][pl.ds(0, cells)].reshape(rows, cols, channels).astype(F32)
        for kx in range(3):
            wide[pl.ds(1 + owner * rows, rows), :, pl.ds(kx * channels, channels)] = shifted(
                grads, kx - 1
            ).astype(BF16)
        for kz, plane in enumerate((low[code], own[code], high[code])):
            level[owner, pl.ds(kz * part, part)] = plane
    near[...] = wide[pl.ds(me * rows, rows + 2), :, pl.ds(channels, channels)]
    for ky in range(3):
        total = None
        for owner in range(n_gy):
            slab = wide[pl.ds(2 - ky + owner * rows, rows)].reshape(cells, 3 * channels)
            term = jnp.dot(level[owner], slab, preferred_element_type=F32)
            total = term if total is None else total + term
        for kz in range(3):
            for kx in range(3):
                value = total[kz * part : (kz + 1) * part, kx * channels : (kx + 1) * channels]
                index = (kz * 3 + ky) * 3 + kx
                for side in range(2):
                    halves[side, pl.ds(index * half, half)] = value[side * half : (side + 1) * half]
    side = lax.axis_index("gz") % 2
    keep[...] = halves[side]
    send[...] = halves[1 - side].astype(send.dtype)


def input_kernel(even, own, odd, weight, out):
    rows, cols, channels = out.shape
    low, high = sides(even, odd)
    planes = (low, own, high)
    total = None
    for kz in range(3):
        for ky in range(3):
            slab = planes[2 - kz][2 - ky : 2 - ky + rows].reshape(rows * cols, channels)
            term = lax.dot_general(
                slab,
                weight[kz, ky].reshape(3 * channels, channels),
                (((1,), (1,)), ((), ())),
                preferred_element_type=F32,
            )
            total = term if total is None else total + term
    answer = None
    for kx in range(3):
        part = total[:, kx * channels : (kx + 1) * channels].reshape(rows, cols, channels)
        part = shifted(part, kx - 1)
        answer = part if answer is None else answer + part
    out[...] = answer.astype(BF16)


def reversed_bits(code, count):
    place, bit = 0, 1
    while bit < count:
        place = place * 2 + code // bit % 2
        bit *= 2
    return place


def cut_kernel(keep, other, *rest):
    downs, (own, *outs, pieces) = rest[: -len(rest) // 2], rest[-len(rest) // 2 :]
    me = lax.axis_index("gz") // 2
    rows = own.shape[0]
    down = sum(ref[...].astype(F32) for ref in downs)
    values = (keep[...] + other[...].astype(F32), down)
    first = 0
    for value in values:
        for row, owner, inner, take in segments(value.shape[0], rows, value.shape[0], first):
            pieces[owner, pl.ds(inner, take)] = value[row : row + take]
        first += value.shape[0]
    blank = pieces.shape[0] * rows - first
    for row, owner, inner, take in segments(blank, rows, rows, first):
        pieces[owner, pl.ds(inner, take)] = jnp.zeros((take, own.shape[1]), F32)
    own[...] = pieces[me]
    for code, out in enumerate(outs):
        out[...] = pieces[jnp.bitwise_xor(me, code + 1)].astype(BF16)


def place_kernel(n_gy, *refs):
    blocks, (conv, down) = refs[: 2 * n_gy], refs[2 * n_gy :]
    me = lax.axis_index("gy")
    line = lax.axis_index("gz") // 2
    parity = lax.axis_index("gz") % 2
    half, channels = conv.shape[3:]
    count, deep_channels = down.shape[2:]
    parts, rows = blocks[0].shape[:2]
    places = [jnp.bitwise_xor(line, owner) if parts > 1 else 0 for owner in range(parts)]
    for index, block in enumerate(blocks):
        side = jnp.bitwise_xor(parity, index // n_gy)
        column = jnp.bitwise_xor(me, index % n_gy)
        for k in range(27):
            for row, owner, inner, take in segments(half, rows, half, k * half):
                conv[k, column, side, pl.ds(row, take)] = block[places[owner], pl.ds(inner, take)]
        for wide in range(deep_channels // channels):
            first = 27 * half + wide * count
            for row, owner, inner, take in segments(count, rows, count, first):
                down[side, column, pl.ds(row, take), pl.ds(wide * channels, channels)] = block[
                    places[owner], pl.ds(inner, take)
                ]


def swapped(value, axis, code):
    return lax.ppermute(value, axis, [(i, i ^ code) for i in range(lax.axis_size(axis))])


def neighbours(value):
    last = lax.axis_size("gz") - 1
    odd = [(i + d, i + 1 - d) for i in range(1, last, 2) for d in range(2)]
    return swapped(value, "gz", 1), lax.ppermute(value, "gz", odd)


def exchanged(value, axis):
    return lax.all_to_all(value, axis, split_axis=0, concat_axis=0, tiled=True)


def per_device(
    level_input, pre_activation, conv_weight, down_weight, skip_cotangent, deep_cotangent
):
    n_gz = lax.axis_size("gz")
    n_gy = lax.axis_size("gy")
    _, rows, cols, channels = level_input.shape
    planes, deep_rows, deep_cols, share = deep_cotangent.shape
    deep_channels = down_weight.shape[4]
    parity = lax.axis_index("gz") % 2
    devices = n_gz * n_gy
    part = channels // n_gy
    cells = rows * cols
    deep_cells = deep_rows * deep_cols
    half = part // 2
    down_count = 4 * deep_channels // n_gy
    wire = BF16 if n_gz <= 8 else F32
    shape = jax.ShapeDtypeStruct

    level = level_input.reshape(cells, channels)
    deep = deep_cotangent.reshape(planes, deep_cells, share)
    if share % 16 == 0:
        keep, send = call(
            deep_kernel,
            [shape((planes // 2, share, deep_cells), BF16)] * 2,
            deep,
            scratch=[pltpu.VMEM((planes, share, deep_cells), BF16)],
        )
        code = planes
        held = jnp.stack([keep, swapped(send, "gz", code)], axis=1)
        while code > 2:
            code //= 2
            count = code // 2
            upper = lax.axis_index("gz") // code % 2
            keep = lax.dynamic_slice_in_dim(held, upper * count, count, axis=0)
            send = lax.dynamic_slice_in_dim(held, (1 - upper) * count, count, axis=0)
            held = jnp.concatenate([keep, swapped(send, "gz", code)], axis=1)
        deep_t = [held[0], swapped(held[0], "gz", 1)]
    else:
        deep_t = jnp.repeat(jnp.swapaxes(deep, 1, 2), 2, axis=0)
        deep_t = [exchanged(deep_t, "gz").reshape(deep_channels, deep_cells)]
    level_t = call(
        level_kernel,
        [shape((part, cells), BF16)] * n_gy,
        level,
        scratch=[pltpu.VMEM((n_gy, part, cells), BF16)],
    )
    level_t = [swapped(value, "gy", code) if code else value for code, value in enumerate(level_t)]
    level_t = jnp.stack(level_t)
    *deep_t, level_t = lax.optimization_barrier((*deep_t, level_t))
    down_slice = lax.dynamic_index_in_dim(down_weight, parity, 0, keepdims=False)
    grad, down, *others = call(
        lambda *refs: mask_kernel(n_gy, *refs),
        [shape((cells, channels), BF16), shape((down_count, channels), F32)]
        + [shape((down_count, channels), BF16)] * (n_gy - 1),
        pre_activation[0],
        skip_cotangent[0],
        down_slice,
        *deep_t,
        scratch=[
            pltpu.VMEM((deep_channels, deep_cells), BF16),
            pltpu.VMEM((n_gy, 4 * channels // n_gy, deep_channels), F32),
        ],
    )
    grad, level_t = lax.optimization_barrier((grad, level_t))
    even, odd = neighbours(level_t)
    shared = [swapped(grad, "gy", code) if code else grad for code in range(n_gy)]
    even, odd, *others = lax.optimization_barrier((even, odd, *others))
    downs = [down] + [swapped(value, "gy", code + 1) for code, value in enumerate(others)]
    keep, send, near = call(
        lambda *refs: weight_kernel(n_gy, (rows, cols, channels), *refs),
        (
            shape((27 * half, channels), F32),
            shape((27 * half, channels), wire),
            shape((rows + 2, cols, channels), BF16),
        ),
        even,
        level_t,
        odd,
        *shared,
        scratch=[
            pltpu.VMEM((n_gy * rows + 2, cols, 3 * channels), BF16),
            pltpu.VMEM((n_gy, 3 * part, cells), BF16),
            pltpu.VMEM((2, 27 * half, channels), F32),
        ],
    )
    near_even, near_odd = neighbours(near)
    send = swapped(send, "gz", 1)

    def input_part(near_even, near_odd):
        return call(
            input_kernel,
            shape((rows, cols, channels), BF16),
            near_even,
            near,
            near_odd,
            conv_weight,
        )

    cell_total = devices * cells
    n_z = n_gz // 2
    total_rows = 27 * half + down_count
    piece = -(-total_rows // (16 * n_z)) * 16
    if n_z <= 4:
        own, *pieces = call(
            cut_kernel,
            [shape((piece, channels), F32)] + [shape((piece, channels), BF16)] * (n_z - 1),
            keep,
            send,
            *downs,
            scratch=[pltpu.VMEM((n_z, piece, channels), F32)],
        )
        pieces = [swapped(value, "gz", 2 * code + 2) for code, value in enumerate(pieces)]
        *pieces, near_even, near_odd = lax.optimization_barrier((*pieces, near_even, near_odd))
        total = own + sum(value.astype(F32) for value in pieces)
        first = lax.axis_index("gz") // 2 * piece
    else:
        down = sum(value.astype(F32) for value in downs)
        total = jnp.concatenate([keep + send.astype(F32), down], axis=0)
        code = n_gz // 2
        while code > 1:
            total = total + swapped(total, "gz", code)
            code //= 2
        first = 0
    row = first + lax.broadcasted_iota(jnp.int32, total.shape, 0)
    scale = jnp.where(
        row < 27 * half, 1 / math.sqrt(cell_total), 1 / math.sqrt(cell_total // 8)
    )
    total = (total * scale).astype(BF16)
    input_grad = input_part(near_even, near_odd)
    if n_z <= 4:
        pieces = [swapped(total, "gz", 2 * code) if code else total for code in range(n_z)]
        *pieces, input_grad = lax.optimization_barrier((*pieces, input_grad))
        total = jnp.stack(pieces)
    else:
        total = total[None]
    pair = [total, swapped(total, "gz", 1)]
    blocks = []
    for index, block in enumerate(pair):
        line = [block]
        code = n_gy // 2
        while code:
            line = line + [swapped(value, "gy", code) for value in line]
            code //= 2
        blocks += [line[reversed_bits(place, n_gy)] for place in range(n_gy)]
    conv_grad, down_grad = call(
        lambda *refs: place_kernel(n_gy, *refs),
        (
            shape((27, n_gy, 2, half, channels), BF16),
            shape((2, n_gy, 4 * channels // n_gy, deep_channels), BF16),
        ),
        *blocks,
    )
    return (
        input_grad[None],
        conv_grad.reshape(conv_weight.shape),
        down_grad.reshape(down_weight.shape),
    )


def solution(mesh):
    return jax.shard_map(
        per_device,
        mesh=mesh,
        in_specs=(
            P("gz", "gy", None, None),
            P("gz", "gy", None, None),
            P(),
            P(),
            P("gz", "gy", None, None),
            P(None, "gy", None, "gz"),
        ),
        out_specs=(P("gz", "gy", None, None), P(), P()),
        check_vma=False,
    )
```

```python
import math

import jax
import jax.numpy as jnp
from jax import lax
from jax.experimental import pallas as pl
from jax.experimental.pallas import tpu as pltpu
from jax.sharding import PartitionSpec as P

F32 = jnp.float32
BF16 = jnp.bfloat16
VMEM_LIMIT = 40 * 1024 * 1024


def call(kernel, out_shape, *operands, scratch=()):
    return pl.pallas_call(
        kernel,
        out_shape=out_shape,
        scratch_shapes=list(scratch),
        compiler_params=pltpu.CompilerParams(vmem_limit_bytes=VMEM_LIMIT),
    )(*operands)


def shifted(cells, step):
    if step == 0:
        return cells
    cols = cells.shape[1]
    moved = pltpu.roll(cells, step % cols, 1)
    col = lax.broadcasted_iota(jnp.int32, cells.shape, 1)
    keep = col >= step if step > 0 else col < cols + step
    return jnp.where(keep, moved, 0.0)


def deep_kernel(deep, keep, send, turned):
    planes = deep.shape[0]
    half = planes // 2
    for plane in range(planes):
        turned[plane] = deep[plane].astype(F32).T.astype(BF16)
    upper = lax.axis_index("gz") // planes
    keep[...] = turned[pl.ds(upper * half, half)]
    send[...] = turned[pl.ds((1 - upper) * half, half)]


def level_kernel(level, *rest):
    outs, level_t = rest[:-1], rest[-1]
    turned = level[...].astype(F32).T.astype(BF16)
    part = level_t.shape[1]
    for owner in range(len(outs)):
        level_t[owner] = turned[owner * part : (owner + 1) * part]
    me = lax.axis_index("gy")
    for code, out in enumerate(outs):
        out[...] = level_t[jnp.bitwise_xor(me, code)]


def mask_kernel(n_gy, pre, skip, weight, *rest):
    deeps, rest = rest[: -n_gy - 3], rest[-n_gy - 3 :]
    grad_out, kept, *outs, deep_t, down_all = rest
    if len(deeps) > 1:
        count, share = deeps[0].shape[:2]
        me = lax.axis_index("gz")
        for place in range(2 * count):
            owner = jnp.bitwise_xor(me, reversed_bits(place, 2 * count))
            first = pl.multiple_of(owner * share, share)
            deep_t[pl.ds(first, share)] = deeps[place // count][place % count]
    else:
        deep_t[...] = deeps[0][...]
    rows, cols, channels = pre.shape
    half = rows // 2
    deep_cols = cols // 2
    cells = half * cols
    deep_cells = half * deep_cols
    wide = lax.broadcasted_iota(jnp.int32, (deep_cells, cells), 1) // 2
    deep = lax.broadcasted_iota(jnp.int32, (deep_cells, cells), 0)
    repeat = (wide == deep).astype(BF16)
    spread = jnp.dot(deep_t[...], repeat, preferred_element_type=F32).astype(BF16)
    col = lax.broadcasted_iota(jnp.int32, (cells, channels), 0) % 2
    count = down_all.shape[1]
    for b in range(2):
        parts = [
            lax.dot_general(
                spread, weight[b, c], (((0,), (1,)), ((), ())), preferred_element_type=F32
            )
            for c in range(2)
        ]
        part = jnp.where(col == 0, parts[0], parts[1]).reshape(half, cols, channels)
        for y in range(half):
            row = 2 * y + b
            pre_row = pre[row].astype(F32)
            total = part[y] + skip[row].astype(F32)
            grad = jnp.where(pre_row > 0, total, 0.0).astype(BF16)
            grad_out[pl.ds(row * cols, cols)] = grad
        hidden = jnp.concatenate(
            [jnp.maximum(pre[2 * y + b].astype(F32), 0.0) for y in range(half)], axis=0
        )
        for c in range(2):
            one = jnp.where(col == c, hidden, 0.0).astype(BF16)
            down = lax.dot_general(
                one, spread, (((0,), (1,)), ((), ())), preferred_element_type=F32
            )
            for first, owner, inner, take in segments(channels, count, channels, (b * 2 + c) * channels):
                down_all[owner, pl.ds(inner, take)] = down[first : first + take]
    me = lax.axis_index("gy")
    for code, out in enumerate([kept, *outs]):
        owner = jnp.bitwise_xor(me, code)
        for side in range(down_all.shape[2] // channels):
            out[pl.ds(side * count, count)] = down_all[
                owner, :, pl.ds(side * channels, channels)
            ].astype(out.dtype)


def segments(rows, piece, unit, base=0):
    row = 0
    while row < rows:
        take = min(rows - row, unit - row % unit, piece - (base + row) % piece)
        yield row, (base + row) // piece, (base + row) % piece, take
        row += take


def sides(even, odd):
    upper = lax.axis_index("gz") % 2 == 0
    low = jnp.where(upper, odd[...].astype(F32), even[...].astype(F32)).astype(BF16)
    high = jnp.where(upper, even[...].astype(F32), odd[...].astype(F32)).astype(BF16)
    return low, high


def weight_kernel(n_gy, shape, *refs):
    even, own, odd = refs[:3]
    shared = refs[3 : 3 + n_gy]
    keep, send, near, wide, level, halves = refs[3 + n_gy :]
    rows, cols, channels = shape
    part = own.shape[1]
    cells = rows * cols
    half = part // 2
    rows_all = n_gy * rows
    me = lax.axis_index("gy")
    low, high = sides(even, odd)
    for edge in (0, rows_all + 1):
        wide[edge] = jnp.zeros(wide.shape[1:], BF16)
    for code in range(n_gy):
        owner = jnp.bitwise_xor(me, code)
        grads = shared[code][pl.ds(0, cells)].reshape(rows, cols, channels).astype(F32)
        for kx in range(3):
            wide[pl.ds(1 + owner * rows, rows), :, pl.ds(kx * channels, channels)] = shifted(
                grads, kx - 1
            ).astype(BF16)
        for kz, plane in enumerate((low[code], own[code], high[code])):
            level[owner, pl.ds(kz * part, part)] = plane
    near[...] = wide[pl.ds(me * rows, rows + 2), :, pl.ds(channels, channels)]
    for ky in range(3):
        total = None
        for owner in range(n_gy):
            slab = wide[pl.ds(2 - ky + owner * rows, rows)].reshape(cells, 3 * channels)
            term = jnp.dot(level[owner], slab, preferred_element_type=F32)
            total = term if total is None else total + term
        for kz in range(3):
            for kx in range(3):
                value = total[kz * part : (kz + 1) * part, kx * channels : (kx + 1) * channels]
                index = (kz * 3 + ky) * 3 + kx
                for side in range(2):
                    halves[side, pl.ds(index * half, half)] = value[side * half : (side + 1) * half]
    side = lax.axis_index("gz") % 2
    keep[...] = halves[side]
    send[...] = halves[1 - side].astype(send.dtype)


def input_kernel(even, own, odd, weight, out):
    rows, cols, channels = out.shape
    low, high = sides(even, odd)
    planes = (low, own, high)
    total = None
    for kz in range(3):
        for ky in range(3):
            slab = planes[2 - kz][2 - ky : 2 - ky + rows].reshape(rows * cols, channels)
            term = lax.dot_general(
                slab,
                weight[kz, ky].reshape(3 * channels, channels),
                (((1,), (1,)), ((), ())),
                preferred_element_type=F32,
            )
            total = term if total is None else total + term
    answer = None
    for kx in range(3):
        part = total[:, kx * channels : (kx + 1) * channels].reshape(rows, cols, channels)
        part = shifted(part, kx - 1)
        answer = part if answer is None else answer + part
    out[...] = answer.astype(BF16)


def reversed_bits(code, count):
    place, bit = 0, 1
    while bit < count:
        place = place * 2 + code // bit % 2
        bit *= 2
    return place


def cut_kernel(keep, other, *rest):
    downs, (own, *outs, pieces) = rest[: -len(rest) // 2], rest[-len(rest) // 2 :]
    me = lax.axis_index("gz") // 2
    rows = own.shape[0]
    down = sum(ref[...].astype(F32) for ref in downs)
    values = (keep[...] + other[...].astype(F32), down)
    first = 0
    for value in values:
        for row, owner, inner, take in segments(value.shape[0], rows, value.shape[0], first):
            pieces[owner, pl.ds(inner, take)] = value[row : row + take]
        first += value.shape[0]
    blank = pieces.shape[0] * rows - first
    for row, owner, inner, take in segments(blank, rows, rows, first):
        pieces[owner, pl.ds(inner, take)] = jnp.zeros((take, own.shape[1]), F32)
    own[...] = pieces[me]
    for code, out in enumerate(outs):
        out[...] = pieces[jnp.bitwise_xor(me, code + 1)].astype(BF16)


def place_kernel(n_gy, *refs):
    blocks, (conv, down) = refs[: 2 * n_gy], refs[2 * n_gy :]
    me = lax.axis_index("gy")
    line = lax.axis_index("gz") // 2
    parity = lax.axis_index("gz") % 2
    half, channels = conv.shape[3:]
    count, deep_channels = down.shape[2:]
    parts, rows = blocks[0].shape[:2]
    places = [jnp.bitwise_xor(line, owner) if parts > 1 else 0 for owner in range(parts)]
    for index, block in enumerate(blocks):
        side = jnp.bitwise_xor(parity, index // n_gy)
        column = jnp.bitwise_xor(me, index % n_gy)
        for k in range(27):
            for row, owner, inner, take in segments(half, rows, half, k * half):
                conv[k, column, side, pl.ds(row, take)] = block[places[owner], pl.ds(inner, take)]
        for wide in range(deep_channels // channels):
            first = 27 * half + wide * count
            for row, owner, inner, take in segments(count, rows, count, first):
                down[side, column, pl.ds(row, take), pl.ds(wide * channels, channels)] = block[
                    places[owner], pl.ds(inner, take)
                ]


def swapped(value, axis, code):
    return lax.ppermute(value, axis, [(i, i ^ code) for i in range(lax.axis_size(axis))])


def neighbours(value):
    last = lax.axis_size("gz") - 1
    odd = [(i + d, i + 1 - d) for i in range(1, last, 2) for d in range(2)]
    return swapped(value, "gz", 1), lax.ppermute(value, "gz", odd)


def exchanged(value, axis):
    return lax.all_to_all(value, axis, split_axis=0, concat_axis=0, tiled=True)


def per_device(
    level_input, pre_activation, conv_weight, down_weight, skip_cotangent, deep_cotangent
):
    n_gz = lax.axis_size("gz")
    n_gy = lax.axis_size("gy")
    _, rows, cols, channels = level_input.shape
    planes, deep_rows, deep_cols, share = deep_cotangent.shape
    deep_channels = down_weight.shape[4]
    parity = lax.axis_index("gz") % 2
    devices = n_gz * n_gy
    part = channels // n_gy
    cells = rows * cols
    deep_cells = deep_rows * deep_cols
    half = part // 2
    down_count = 4 * deep_channels // n_gy
    wire = BF16 if n_gz <= 8 else F32
    shape = jax.ShapeDtypeStruct

    level = level_input.reshape(cells, channels)
    deep = deep_cotangent.reshape(planes, deep_cells, share)
    if share % 16 == 0:
        keep, send = call(
            deep_kernel,
            [shape((planes // 2, share, deep_cells), BF16)] * 2,
            deep,
            scratch=[pltpu.VMEM((planes, share, deep_cells), BF16)],
        )
        code = planes
        held = jnp.stack([keep, swapped(send, "gz", code)], axis=1)
        while code > 2:
            code //= 2
            count = code // 2
            upper = lax.axis_index("gz") // code % 2
            keep = lax.dynamic_slice_in_dim(held, upper * count, count, axis=0)
            send = lax.dynamic_slice_in_dim(held, (1 - upper) * count, count, axis=0)
            held = jnp.concatenate([keep, swapped(send, "gz", code)], axis=1)
        deep_t = [held[0], swapped(held[0], "gz", 1)]
    else:
        deep_t = jnp.repeat(jnp.swapaxes(deep, 1, 2), 2, axis=0)
        deep_t = [exchanged(deep_t, "gz").reshape(deep_channels, deep_cells)]
    level_t = call(
        level_kernel,
        [shape((part, cells), BF16)] * n_gy,
        level,
        scratch=[pltpu.VMEM((n_gy, part, cells), BF16)],
    )
    level_t = [swapped(value, "gy", code) if code else value for code, value in enumerate(level_t)]
    level_t = jnp.stack(level_t)
    *deep_t, level_t = lax.optimization_barrier((*deep_t, level_t))
    down_slice = lax.dynamic_index_in_dim(down_weight, parity, 0, keepdims=False)
    grad, down, *others = call(
        lambda *refs: mask_kernel(n_gy, *refs),
        [shape((cells, channels), BF16), shape((down_count, channels), F32)]
        + [shape((down_count, channels), BF16)] * (n_gy - 1),
        pre_activation[0],
        skip_cotangent[0],
        down_slice,
        *deep_t,
        scratch=[
            pltpu.VMEM((deep_channels, deep_cells), BF16),
            pltpu.VMEM((n_gy, 4 * channels // n_gy, deep_channels), F32),
        ],
    )
    shared = [swapped(grad, "gy", code) if code else grad for code in range(n_gy)]
    shared[1], level_t = lax.optimization_barrier((shared[1], level_t))
    even, odd = neighbours(level_t)
    keep, send, near = call(
        lambda *refs: weight_kernel(n_gy, (rows, cols, channels), *refs),
        (
            shape((27 * half, channels), F32),
            shape((27 * half, channels), wire),
            shape((rows + 2, cols, channels), BF16),
        ),
        even,
        level_t,
        odd,
        *shared,
        scratch=[
            pltpu.VMEM((n_gy * rows + 2, cols, 3 * channels), BF16),
            pltpu.VMEM((n_gy, 3 * part, cells), BF16),
            pltpu.VMEM((2, 27 * half, channels), F32),
        ],
    )
    send, *others = lax.optimization_barrier((send, *others))
    downs = [down] + [swapped(value, "gy", code + 1) for code, value in enumerate(others)]
    send, near = lax.optimization_barrier((swapped(send, "gz", 1), near))
    near_even, near_odd = neighbours(near)

    def input_part(near_even, near_odd):
        return call(
            input_kernel,
            shape((rows, cols, channels), BF16),
            near_even,
            near,
            near_odd,
            conv_weight,
        )

    cell_total = devices * cells
    n_z = n_gz // 2
    total_rows = 27 * half + down_count
    piece = -(-total_rows // (16 * n_z)) * 16
    if n_z <= 4:
        own, *pieces = call(
            cut_kernel,
            [shape((piece, channels), F32)] + [shape((piece, channels), BF16)] * (n_z - 1),
            keep,
            send,
            *downs,
            scratch=[pltpu.VMEM((n_z, piece, channels), F32)],
        )
        pieces = [swapped(value, "gz", 2 * code + 2) for code, value in enumerate(pieces)]
        *pieces, near_even, near_odd = lax.optimization_barrier((*pieces, near_even, near_odd))
        total = own + sum(value.astype(F32) for value in pieces)
        first = lax.axis_index("gz") // 2 * piece
    else:
        down = sum(value.astype(F32) for value in downs)
        total = jnp.concatenate([keep + send.astype(F32), down], axis=0)
        code = n_gz // 2
        while code > 1:
            total = total + swapped(total, "gz", code)
            code //= 2
        first = 0
    row = first + lax.broadcasted_iota(jnp.int32, total.shape, 0)
    scale = jnp.where(
        row < 27 * half, 1 / math.sqrt(cell_total), 1 / math.sqrt(cell_total // 8)
    )
    total = (total * scale).astype(BF16)
    input_grad = input_part(near_even, near_odd)
    if n_z <= 4:
        pieces = [swapped(total, "gz", 2 * code) if code else total for code in range(n_z)]
        *pieces, input_grad = lax.optimization_barrier((*pieces, input_grad))
        total = jnp.stack(pieces)
    else:
        total = total[None]
    pair = [total, swapped(total, "gz", 1)]
    blocks = []
    for index, block in enumerate(pair):
        line = [block]
        code = n_gy // 2
        while code:
            line = line + [swapped(value, "gy", code) for value in line]
            code //= 2
        blocks += [line[reversed_bits(place, n_gy)] for place in range(n_gy)]
    conv_grad, down_grad = call(
        lambda *refs: place_kernel(n_gy, *refs),
        (
            shape((27, n_gy, 2, half, channels), BF16),
            shape((2, n_gy, 4 * channels // n_gy, deep_channels), BF16),
        ),
        *blocks,
    )
    return (
        input_grad[None],
        conv_grad.reshape(conv_weight.shape),
        down_grad.reshape(down_weight.shape),
    )


def solution(mesh):
    return jax.shard_map(
        per_device,
        mesh=mesh,
        in_specs=(
            P("gz", "gy", None, None),
            P("gz", "gy", None, None),
            P(),
            P(),
            P("gz", "gy", None, None),
            P(None, "gy", None, "gz"),
        ),
        out_specs=(P("gz", "gy", None, None), P(), P()),
        check_vma=False,
    )
```

```python
import math

import jax
import jax.numpy as jnp
from jax import lax
from jax.experimental import pallas as pl
from jax.experimental.pallas import tpu as pltpu
from jax.sharding import PartitionSpec as P

F32 = jnp.float32
BF16 = jnp.bfloat16
VMEM_LIMIT = 40 * 1024 * 1024


def call(kernel, out_shape, *operands, scratch=()):
    return pl.pallas_call(
        kernel,
        out_shape=out_shape,
        scratch_shapes=list(scratch),
        compiler_params=pltpu.CompilerParams(vmem_limit_bytes=VMEM_LIMIT),
    )(*operands)


def shifted(cells, step):
    if step == 0:
        return cells
    cols = cells.shape[1]
    moved = pltpu.roll(cells, step % cols, 1)
    col = lax.broadcasted_iota(jnp.int32, cells.shape, 1)
    keep = col >= step if step > 0 else col < cols + step
    return jnp.where(keep, moved, 0.0)


def deep_kernel(deep, keep, send, turned):
    planes = deep.shape[0]
    half = planes // 2
    for plane in range(planes):
        turned[plane] = deep[plane].astype(F32).T.astype(BF16)
    upper = lax.axis_index("gz") // planes
    keep[...] = turned[pl.ds(upper * half, half)]
    send[...] = turned[pl.ds((1 - upper) * half, half)]


def level_kernel(level, *rest):
    outs, level_t = rest[:-1], rest[-1]
    turned = level[...].astype(F32).T.astype(BF16)
    part = level_t.shape[1]
    for owner in range(len(outs)):
        level_t[owner] = turned[owner * part : (owner + 1) * part]
    me = lax.axis_index("gy")
    for code, out in enumerate(outs):
        out[...] = level_t[jnp.bitwise_xor(me, code)]


def mask_kernel(n_gy, pre, skip, weight, *rest):
    deeps, rest = rest[: -n_gy - 3], rest[-n_gy - 3 :]
    grad_out, kept, *outs, deep_t, down_all = rest
    if len(deeps) > 1:
        count, share = deeps[0].shape[:2]
        me = lax.axis_index("gz")
        for place in range(2 * count):
            owner = jnp.bitwise_xor(me, reversed_bits(place, 2 * count))
            first = pl.multiple_of(owner * share, share)
            deep_t[pl.ds(first, share)] = deeps[place // count][place % count]
    else:
        deep_t[...] = deeps[0][...]
    rows, cols, channels = pre.shape
    half = rows // 2
    deep_cols = cols // 2
    cells = half * cols
    deep_cells = half * deep_cols
    wide = lax.broadcasted_iota(jnp.int32, (deep_cells, cells), 1) // 2
    deep = lax.broadcasted_iota(jnp.int32, (deep_cells, cells), 0)
    repeat = (wide == deep).astype(BF16)
    spread = jnp.dot(deep_t[...], repeat, preferred_element_type=F32).astype(BF16)
    col = lax.broadcasted_iota(jnp.int32, (cells, channels), 0) % 2
    count = down_all.shape[1]
    for b in range(2):
        parts = [
            lax.dot_general(
                spread, weight[b, c], (((0,), (1,)), ((), ())), preferred_element_type=F32
            )
            for c in range(2)
        ]
        part = jnp.where(col == 0, parts[0], parts[1]).reshape(half, cols, channels)
        for y in range(half):
            row = 2 * y + b
            pre_row = pre[row].astype(F32)
            total = part[y] + skip[row].astype(F32)
            grad = jnp.where(pre_row > 0, total, 0.0).astype(BF16)
            grad_out[pl.ds(row * cols, cols)] = grad
        hidden = jnp.concatenate(
            [jnp.maximum(pre[2 * y + b].astype(F32), 0.0) for y in range(half)], axis=0
        )
        for c in range(2):
            one = jnp.where(col == c, hidden, 0.0).astype(BF16)
            down = lax.dot_general(
                one, spread, (((0,), (1,)), ((), ())), preferred_element_type=F32
            )
            for first, owner, inner, take in segments(channels, count, channels, (b * 2 + c) * channels):
                down_all[owner, pl.ds(inner, take)] = down[first : first + take]
    me = lax.axis_index("gy")
    for code, out in enumerate([kept, *outs]):
        owner = jnp.bitwise_xor(me, code)
        for side in range(down_all.shape[2] // channels):
            out[pl.ds(side * count, count)] = down_all[
                owner, :, pl.ds(side * channels, channels)
            ].astype(out.dtype)


def segments(rows, piece, unit, base=0):
    row = 0
    while row < rows:
        take = min(rows - row, unit - row % unit, piece - (base + row) % piece)
        yield row, (base + row) // piece, (base + row) % piece, take
        row += take


def sides(even, odd):
    upper = lax.axis_index("gz") % 2 == 0
    low = jnp.where(upper, odd[...].astype(F32), even[...].astype(F32)).astype(BF16)
    high = jnp.where(upper, even[...].astype(F32), odd[...].astype(F32)).astype(BF16)
    return low, high


def weight_kernel(n_gy, shape, *refs):
    even, own, odd = refs[:3]
    shared = refs[3 : 3 + n_gy]
    keep, send, near, wide, level, halves = refs[3 + n_gy :]
    rows, cols, channels = shape
    part = own.shape[1]
    cells = rows * cols
    half = part // 2
    rows_all = n_gy * rows
    me = lax.axis_index("gy")
    low, high = sides(even, odd)
    for edge in (0, rows_all + 1):
        wide[edge] = jnp.zeros(wide.shape[1:], BF16)
    for code in range(n_gy):
        owner = jnp.bitwise_xor(me, code)
        grads = shared[code][pl.ds(0, cells)].reshape(rows, cols, channels).astype(F32)
        for kx in range(3):
            wide[pl.ds(1 + owner * rows, rows), :, pl.ds(kx * channels, channels)] = shifted(
                grads, kx - 1
            ).astype(BF16)
        for kz, plane in enumerate((low[code], own[code], high[code])):
            level[owner, pl.ds(kz * part, part)] = plane
    near[...] = wide[pl.ds(me * rows, rows + 2), :, pl.ds(channels, channels)]
    for ky in range(3):
        total = None
        for owner in range(n_gy):
            slab = wide[pl.ds(2 - ky + owner * rows, rows)].reshape(cells, 3 * channels)
            term = jnp.dot(level[owner], slab, preferred_element_type=F32)
            total = term if total is None else total + term
        for kz in range(3):
            for kx in range(3):
                value = total[kz * part : (kz + 1) * part, kx * channels : (kx + 1) * channels]
                index = (kz * 3 + ky) * 3 + kx
                for side in range(2):
                    halves[side, pl.ds(index * half, half)] = value[side * half : (side + 1) * half]
    side = lax.axis_index("gz") % 2
    keep[...] = halves[side]
    send[...] = halves[1 - side].astype(send.dtype)


def input_kernel(even, own, odd, weight, out):
    rows, cols, channels = out.shape
    low, high = sides(even, odd)
    planes = (low, own, high)
    total = None
    for kz in range(3):
        for ky in range(3):
            slab = planes[2 - kz][2 - ky : 2 - ky + rows].reshape(rows * cols, channels)
            term = lax.dot_general(
                slab,
                weight[kz, ky].reshape(3 * channels, channels),
                (((1,), (1,)), ((), ())),
                preferred_element_type=F32,
            )
            total = term if total is None else total + term
    answer = None
    for kx in range(3):
        part = total[:, kx * channels : (kx + 1) * channels].reshape(rows, cols, channels)
        part = shifted(part, kx - 1)
        answer = part if answer is None else answer + part
    out[...] = answer.astype(BF16)


def reversed_bits(code, count):
    place, bit = 0, 1
    while bit < count:
        place = place * 2 + code // bit % 2
        bit *= 2
    return place


def cut_kernel(keep, other, *rest):
    downs, (own, *outs, pieces) = rest[: -len(rest) // 2], rest[-len(rest) // 2 :]
    me = lax.axis_index("gz") // 2
    rows = own.shape[0]
    down = sum(ref[...].astype(F32) for ref in downs)
    values = (keep[...] + other[...].astype(F32), down)
    first = 0
    for value in values:
        for row, owner, inner, take in segments(value.shape[0], rows, value.shape[0], first):
            pieces[owner, pl.ds(inner, take)] = value[row : row + take]
        first += value.shape[0]
    blank = pieces.shape[0] * rows - first
    for row, owner, inner, take in segments(blank, rows, rows, first):
        pieces[owner, pl.ds(inner, take)] = jnp.zeros((take, own.shape[1]), F32)
    own[...] = pieces[me]
    for code, out in enumerate(outs):
        out[...] = pieces[jnp.bitwise_xor(me, code + 1)].astype(BF16)


def place_kernel(n_gy, *refs):
    blocks, (conv, down) = refs[: 2 * n_gy], refs[2 * n_gy :]
    me = lax.axis_index("gy")
    line = lax.axis_index("gz") // 2
    parity = lax.axis_index("gz") % 2
    half, channels = conv.shape[3:]
    count, deep_channels = down.shape[2:]
    parts, rows = blocks[0].shape[:2]
    places = [jnp.bitwise_xor(line, owner) if parts > 1 else 0 for owner in range(parts)]
    for index, block in enumerate(blocks):
        side = jnp.bitwise_xor(parity, index // n_gy)
        column = jnp.bitwise_xor(me, index % n_gy)
        for k in range(27):
            for row, owner, inner, take in segments(half, rows, half, k * half):
                conv[k, column, side, pl.ds(row, take)] = block[places[owner], pl.ds(inner, take)]
        for wide in range(deep_channels // channels):
            first = 27 * half + wide * count
            for row, owner, inner, take in segments(count, rows, count, first):
                down[side, column, pl.ds(row, take), pl.ds(wide * channels, channels)] = block[
                    places[owner], pl.ds(inner, take)
                ]


def swapped(value, axis, code):
    return lax.ppermute(value, axis, [(i, i ^ code) for i in range(lax.axis_size(axis))])


def neighbours(value):
    last = lax.axis_size("gz") - 1
    odd = [(i + d, i + 1 - d) for i in range(1, last, 2) for d in range(2)]
    return swapped(value, "gz", 1), lax.ppermute(value, "gz", odd)


def exchanged(value, axis):
    return lax.all_to_all(value, axis, split_axis=0, concat_axis=0, tiled=True)


def per_device(
    level_input, pre_activation, conv_weight, down_weight, skip_cotangent, deep_cotangent
):
    n_gz = lax.axis_size("gz")
    n_gy = lax.axis_size("gy")
    _, rows, cols, channels = level_input.shape
    planes, deep_rows, deep_cols, share = deep_cotangent.shape
    deep_channels = down_weight.shape[4]
    parity = lax.axis_index("gz") % 2
    devices = n_gz * n_gy
    part = channels // n_gy
    cells = rows * cols
    deep_cells = deep_rows * deep_cols
    half = part // 2
    down_count = 4 * deep_channels // n_gy
    wire = BF16 if n_gz <= 8 else F32
    shape = jax.ShapeDtypeStruct

    level = level_input.reshape(cells, channels)
    deep = deep_cotangent.reshape(planes, deep_cells, share)
    if share % 16 == 0:
        keep, send = call(
            deep_kernel,
            [shape((planes // 2, share, deep_cells), BF16)] * 2,
            deep,
            scratch=[pltpu.VMEM((planes, share, deep_cells), BF16)],
        )
        code = planes
        held = jnp.stack([keep, swapped(send, "gz", code)], axis=1)
        while code > 2:
            code //= 2
            count = code // 2
            upper = lax.axis_index("gz") // code % 2
            keep = lax.dynamic_slice_in_dim(held, upper * count, count, axis=0)
            send = lax.dynamic_slice_in_dim(held, (1 - upper) * count, count, axis=0)
            held = jnp.concatenate([keep, swapped(send, "gz", code)], axis=1)
        deep_t = [held[0], swapped(held[0], "gz", 1)]
    else:
        deep_t = jnp.repeat(jnp.swapaxes(deep, 1, 2), 2, axis=0)
        deep_t = [exchanged(deep_t, "gz").reshape(deep_channels, deep_cells)]
    level_t = call(
        level_kernel,
        [shape((part, cells), BF16)] * n_gy,
        level,
        scratch=[pltpu.VMEM((n_gy, part, cells), BF16)],
    )
    level_t = [swapped(value, "gy", code) if code else value for code, value in enumerate(level_t)]
    level_t = jnp.stack(level_t)
    even, odd = neighbours(level_t)
    *deep_t, level_t = lax.optimization_barrier((*deep_t, level_t))
    down_slice = lax.dynamic_index_in_dim(down_weight, parity, 0, keepdims=False)
    grad, down, *others = call(
        lambda *refs: mask_kernel(n_gy, *refs),
        [shape((cells, channels), BF16), shape((down_count, channels), F32)]
        + [shape((down_count, channels), BF16)] * (n_gy - 1),
        pre_activation[0],
        skip_cotangent[0],
        down_slice,
        *deep_t,
        scratch=[
            pltpu.VMEM((deep_channels, deep_cells), BF16),
            pltpu.VMEM((n_gy, 4 * channels // n_gy, deep_channels), F32),
        ],
    )
    shared = [swapped(grad, "gy", code) if code else grad for code in range(n_gy)]
    even, odd, *others = lax.optimization_barrier((even, odd, *others))
    downs = [down] + [swapped(value, "gy", code + 1) for code, value in enumerate(others)]
    keep, send, near = call(
        lambda *refs: weight_kernel(n_gy, (rows, cols, channels), *refs),
        (
            shape((27 * half, channels), F32),
            shape((27 * half, channels), wire),
            shape((rows + 2, cols, channels), BF16),
        ),
        even,
        level_t,
        odd,
        *shared,
        scratch=[
            pltpu.VMEM((n_gy * rows + 2, cols, 3 * channels), BF16),
            pltpu.VMEM((n_gy, 3 * part, cells), BF16),
            pltpu.VMEM((2, 27 * half, channels), F32),
        ],
    )
    send = swapped(send, "gz", 1)

    def input_part(near_even, near_odd):
        return call(
            input_kernel,
            shape((rows, cols, channels), BF16),
            near_even,
            near,
            near_odd,
            conv_weight,
        )

    cell_total = devices * cells
    n_z = n_gz // 2
    total_rows = 27 * half + down_count
    piece = -(-total_rows // (16 * n_z)) * 16
    if n_z <= 4:
        own, *pieces = call(
            cut_kernel,
            [shape((piece, channels), F32)] + [shape((piece, channels), BF16)] * (n_z - 1),
            keep,
            send,
            *downs,
            scratch=[pltpu.VMEM((n_z, piece, channels), F32)],
        )
        own, near, *pieces = lax.optimization_barrier((own, near, *pieces))
        near_even, near_odd = neighbours(near)
        pieces = [swapped(value, "gz", 2 * code + 2) for code, value in enumerate(pieces)]
        *pieces, near_even, near_odd = lax.optimization_barrier((*pieces, near_even, near_odd))
        total = own + sum(value.astype(F32) for value in pieces)
        first = lax.axis_index("gz") // 2 * piece
    else:
        down = sum(value.astype(F32) for value in downs)
        total = jnp.concatenate([keep + send.astype(F32), down], axis=0)
        code = n_gz // 2
        while code > 1:
            total = total + swapped(total, "gz", code)
            code //= 2
        first = 0
        near_even, near_odd = neighbours(near)
    row = first + lax.broadcasted_iota(jnp.int32, total.shape, 0)
    scale = jnp.where(
        row < 27 * half, 1 / math.sqrt(cell_total), 1 / math.sqrt(cell_total // 8)
    )
    total = (total * scale).astype(BF16)
    input_grad = input_part(near_even, near_odd)
    if n_z <= 4:
        pieces = [swapped(total, "gz", 2 * code) if code else total for code in range(n_z)]
        *pieces, input_grad = lax.optimization_barrier((*pieces, input_grad))
        total = jnp.stack(pieces)
    else:
        total = total[None]
    pair = [total, swapped(total, "gz", 1)]
    blocks = []
    for index, block in enumerate(pair):
        line = [block]
        code = n_gy // 2
        while code:
            line = line + [swapped(value, "gy", code) for value in line]
            code //= 2
        blocks += [line[reversed_bits(place, n_gy)] for place in range(n_gy)]
    conv_grad, down_grad = call(
        lambda *refs: place_kernel(n_gy, *refs),
        (
            shape((27, n_gy, 2, half, channels), BF16),
            shape((2, n_gy, 4 * channels // n_gy, deep_channels), BF16),
        ),
        *blocks,
    )
    return (
        input_grad[None],
        conv_grad.reshape(conv_weight.shape),
        down_grad.reshape(down_weight.shape),
    )


def solution(mesh):
    return jax.shard_map(
        per_device,
        mesh=mesh,
        in_specs=(
            P("gz", "gy", None, None),
            P("gz", "gy", None, None),
            P(),
            P(),
            P("gz", "gy", None, None),
            P(None, "gy", None, "gz"),
        ),
        out_specs=(P("gz", "gy", None, None), P(), P()),
        check_vma=False,
    )
```

```python
import math

import jax
import jax.numpy as jnp
from jax import lax
from jax.experimental import pallas as pl
from jax.experimental.pallas import tpu as pltpu
from jax.sharding import PartitionSpec as P

F32 = jnp.float32
BF16 = jnp.bfloat16
VMEM_LIMIT = 40 * 1024 * 1024


def call(kernel, out_shape, *operands, scratch=()):
    return pl.pallas_call(
        kernel,
        out_shape=out_shape,
        scratch_shapes=list(scratch),
        compiler_params=pltpu.CompilerParams(vmem_limit_bytes=VMEM_LIMIT),
    )(*operands)


def shifted(cells, step):
    if step == 0:
        return cells
    cols = cells.shape[1]
    moved = pltpu.roll(cells, step % cols, 1)
    col = lax.broadcasted_iota(jnp.int32, cells.shape, 1)
    keep = col >= step if step > 0 else col < cols + step
    return jnp.where(keep, moved, 0.0)


def deep_kernel(deep, keep, send, turned):
    planes = deep.shape[0]
    half = planes // 2
    for plane in range(planes):
        turned[plane] = deep[plane].astype(F32).T.astype(BF16)
    upper = lax.axis_index("gz") // planes
    keep[...] = turned[pl.ds(upper * half, half)]
    send[...] = turned[pl.ds((1 - upper) * half, half)]


def level_kernel(level, *rest):
    outs, level_t = rest[:-1], rest[-1]
    turned = level[...].astype(F32).T.astype(BF16)
    part = level_t.shape[1]
    for owner in range(len(outs)):
        level_t[owner] = turned[owner * part : (owner + 1) * part]
    me = lax.axis_index("gy")
    for code, out in enumerate(outs):
        out[...] = level_t[jnp.bitwise_xor(me, code)]


def mask_kernel(n_gy, pre, skip, weight, *rest):
    deeps, rest = rest[: -n_gy - 3], rest[-n_gy - 3 :]
    grad_out, kept, *outs, deep_t, down_all = rest
    if len(deeps) > 1:
        count, share = deeps[0].shape[:2]
        me = lax.axis_index("gz")
        for place in range(2 * count):
            owner = jnp.bitwise_xor(me, reversed_bits(place, 2 * count))
            first = pl.multiple_of(owner * share, share)
            deep_t[pl.ds(first, share)] = deeps[place // count][place % count]
    else:
        deep_t[...] = deeps[0][...]
    rows, cols, channels = pre.shape
    half = rows // 2
    deep_cols = cols // 2
    cells = half * cols
    deep_cells = half * deep_cols
    wide = lax.broadcasted_iota(jnp.int32, (deep_cells, cells), 1) // 2
    deep = lax.broadcasted_iota(jnp.int32, (deep_cells, cells), 0)
    repeat = (wide == deep).astype(BF16)
    spread = jnp.dot(deep_t[...], repeat, preferred_element_type=F32).astype(BF16)
    col = lax.broadcasted_iota(jnp.int32, (cells, channels), 0) % 2
    count = down_all.shape[1]
    for b in range(2):
        parts = [
            lax.dot_general(
                spread, weight[b, c], (((0,), (1,)), ((), ())), preferred_element_type=F32
            )
            for c in range(2)
        ]
        part = jnp.where(col == 0, parts[0], parts[1]).reshape(half, cols, channels)
        for y in range(half):
            row = 2 * y + b
            pre_row = pre[row].astype(F32)
            total = part[y] + skip[row].astype(F32)
            grad = jnp.where(pre_row > 0, total, 0.0).astype(BF16)
            grad_out[pl.ds(row * cols, cols)] = grad
        hidden = jnp.concatenate(
            [jnp.maximum(pre[2 * y + b].astype(F32), 0.0) for y in range(half)], axis=0
        )
        for c in range(2):
            one = jnp.where(col == c, hidden, 0.0).astype(BF16)
            down = lax.dot_general(
                one, spread, (((0,), (1,)), ((), ())), preferred_element_type=F32
            )
            for first, owner, inner, take in segments(channels, count, channels, (b * 2 + c) * channels):
                down_all[owner, pl.ds(inner, take)] = down[first : first + take]
    me = lax.axis_index("gy")
    for code, out in enumerate([kept, *outs]):
        owner = jnp.bitwise_xor(me, code)
        for side in range(down_all.shape[2] // channels):
            out[pl.ds(side * count, count)] = down_all[
                owner, :, pl.ds(side * channels, channels)
            ].astype(out.dtype)


def segments(rows, piece, unit, base=0):
    row = 0
    while row < rows:
        take = min(rows - row, unit - row % unit, piece - (base + row) % piece)
        yield row, (base + row) // piece, (base + row) % piece, take
        row += take


def sides(even, odd):
    upper = lax.axis_index("gz") % 2 == 0
    low = jnp.where(upper, odd[...].astype(F32), even[...].astype(F32)).astype(BF16)
    high = jnp.where(upper, even[...].astype(F32), odd[...].astype(F32)).astype(BF16)
    return low, high


def weight_kernel(n_gy, shape, *refs):
    even, own, odd = refs[:3]
    shared = refs[3 : 3 + n_gy]
    keep, send, near, wide, level, halves = refs[3 + n_gy :]
    rows, cols, channels = shape
    part = own.shape[1]
    cells = rows * cols
    half = part // 2
    rows_all = n_gy * rows
    me = lax.axis_index("gy")
    low, high = sides(even, odd)
    for edge in (0, rows_all + 1):
        wide[edge] = jnp.zeros(wide.shape[1:], BF16)
    for code in range(n_gy):
        owner = jnp.bitwise_xor(me, code)
        grads = shared[code][pl.ds(0, cells)].reshape(rows, cols, channels).astype(F32)
        for kx in range(3):
            wide[pl.ds(1 + owner * rows, rows), :, pl.ds(kx * channels, channels)] = shifted(
                grads, kx - 1
            ).astype(BF16)
        for kz, plane in enumerate((low[code], own[code], high[code])):
            level[owner, pl.ds(kz * part, part)] = plane
    near[...] = wide[pl.ds(me * rows, rows + 2), :, pl.ds(channels, channels)]
    for ky in range(3):
        total = None
        for owner in range(n_gy):
            slab = wide[pl.ds(2 - ky + owner * rows, rows)].reshape(cells, 3 * channels)
            term = jnp.dot(level[owner], slab, preferred_element_type=F32)
            total = term if total is None else total + term
        for kz in range(3):
            for kx in range(3):
                value = total[kz * part : (kz + 1) * part, kx * channels : (kx + 1) * channels]
                index = (kz * 3 + ky) * 3 + kx
                for side in range(2):
                    halves[side, pl.ds(index * half, half)] = value[side * half : (side + 1) * half]
    side = lax.axis_index("gz") % 2
    keep[...] = halves[side]
    send[...] = halves[1 - side].astype(send.dtype)


def input_kernel(even, own, odd, weight, out):
    rows, cols, channels = out.shape
    low, high = sides(even, odd)
    planes = (low, own, high)
    total = None
    for kz in range(3):
        for ky in range(3):
            slab = planes[2 - kz][2 - ky : 2 - ky + rows].reshape(rows * cols, channels)
            term = lax.dot_general(
                slab,
                weight[kz, ky].reshape(3 * channels, channels),
                (((1,), (1,)), ((), ())),
                preferred_element_type=F32,
            )
            total = term if total is None else total + term
    answer = None
    for kx in range(3):
        part = total[:, kx * channels : (kx + 1) * channels].reshape(rows, cols, channels)
        part = shifted(part, kx - 1)
        answer = part if answer is None else answer + part
    out[...] = answer.astype(BF16)


def reversed_bits(code, count):
    place, bit = 0, 1
    while bit < count:
        place = place * 2 + code // bit % 2
        bit *= 2
    return place


def cut_kernel(keep, other, *rest):
    downs, (own, *outs, pieces) = rest[: -len(rest) // 2], rest[-len(rest) // 2 :]
    me = lax.axis_index("gz") // 2
    rows = own.shape[0]
    down = sum(ref[...].astype(F32) for ref in downs)
    values = (keep[...] + other[...].astype(F32), down)
    first = 0
    for value in values:
        for row, owner, inner, take in segments(value.shape[0], rows, value.shape[0], first):
            pieces[owner, pl.ds(inner, take)] = value[row : row + take]
        first += value.shape[0]
    blank = pieces.shape[0] * rows - first
    for row, owner, inner, take in segments(blank, rows, rows, first):
        pieces[owner, pl.ds(inner, take)] = jnp.zeros((take, own.shape[1]), F32)
    own[...] = pieces[me]
    for code, out in enumerate(outs):
        out[...] = pieces[jnp.bitwise_xor(me, code + 1)].astype(BF16)


def place_kernel(n_gy, *refs):
    blocks, (conv, down) = refs[: 2 * n_gy], refs[2 * n_gy :]
    me = lax.axis_index("gy")
    line = lax.axis_index("gz") // 2
    parity = lax.axis_index("gz") % 2
    half, channels = conv.shape[3:]
    count, deep_channels = down.shape[2:]
    parts, rows = blocks[0].shape[:2]
    places = [jnp.bitwise_xor(line, owner) if parts > 1 else 0 for owner in range(parts)]
    for index, block in enumerate(blocks):
        side = jnp.bitwise_xor(parity, index // n_gy)
        column = jnp.bitwise_xor(me, index % n_gy)
        for k in range(27):
            for row, owner, inner, take in segments(half, rows, half, k * half):
                conv[k, column, side, pl.ds(row, take)] = block[places[owner], pl.ds(inner, take)]
        for wide in range(deep_channels // channels):
            first = 27 * half + wide * count
            for row, owner, inner, take in segments(count, rows, count, first):
                down[side, column, pl.ds(row, take), pl.ds(wide * channels, channels)] = block[
                    places[owner], pl.ds(inner, take)
                ]


def swapped(value, axis, code):
    return lax.ppermute(value, axis, [(i, i ^ code) for i in range(lax.axis_size(axis))])


def even_pairs(value):
    return swapped(value, "gz", 1)


def odd_pairs(value):
    last = lax.axis_size("gz") - 1
    pairs = [(i + d, i + 1 - d) for i in range(1, last, 2) for d in range(2)]
    return lax.ppermute(value, "gz", pairs)


def exchanged(value, axis):
    return lax.all_to_all(value, axis, split_axis=0, concat_axis=0, tiled=True)


def per_device(
    level_input, pre_activation, conv_weight, down_weight, skip_cotangent, deep_cotangent
):
    n_gz = lax.axis_size("gz")
    n_gy = lax.axis_size("gy")
    _, rows, cols, channels = level_input.shape
    planes, deep_rows, deep_cols, share = deep_cotangent.shape
    deep_channels = down_weight.shape[4]
    parity = lax.axis_index("gz") % 2
    devices = n_gz * n_gy
    part = channels // n_gy
    cells = rows * cols
    deep_cells = deep_rows * deep_cols
    half = part // 2
    down_count = 4 * deep_channels // n_gy
    wire = BF16 if n_gz <= 8 else F32
    shape = jax.ShapeDtypeStruct

    level = level_input.reshape(cells, channels)
    deep = deep_cotangent.reshape(planes, deep_cells, share)
    if share % 16 == 0:
        keep, send = call(
            deep_kernel,
            [shape((planes // 2, share, deep_cells), BF16)] * 2,
            deep,
            scratch=[pltpu.VMEM((planes, share, deep_cells), BF16)],
        )
        code = planes
        held = jnp.stack([keep, swapped(send, "gz", code)], axis=1)
        while code > 2:
            code //= 2
            count = code // 2
            upper = lax.axis_index("gz") // code % 2
            keep = lax.dynamic_slice_in_dim(held, upper * count, count, axis=0)
            send = lax.dynamic_slice_in_dim(held, (1 - upper) * count, count, axis=0)
            held = jnp.concatenate([keep, swapped(send, "gz", code)], axis=1)
        deep_t = [held[0], swapped(held[0], "gz", 1)]
    else:
        deep_t = jnp.repeat(jnp.swapaxes(deep, 1, 2), 2, axis=0)
        deep_t = [exchanged(deep_t, "gz").reshape(deep_channels, deep_cells)]
    level_t = call(
        level_kernel,
        [shape((part, cells), BF16)] * n_gy,
        level,
        scratch=[pltpu.VMEM((n_gy, part, cells), BF16)],
    )
    level_t = [swapped(value, "gy", code) if code else value for code, value in enumerate(level_t)]
    level_t = jnp.stack(level_t)
    even = even_pairs(level_t)
    *deep_t, level_t = lax.optimization_barrier((*deep_t, level_t))
    down_slice = lax.dynamic_index_in_dim(down_weight, parity, 0, keepdims=False)
    grad, down, *others = call(
        lambda *refs: mask_kernel(n_gy, *refs),
        [shape((cells, channels), BF16), shape((down_count, channels), F32)]
        + [shape((down_count, channels), BF16)] * (n_gy - 1),
        pre_activation[0],
        skip_cotangent[0],
        down_slice,
        *deep_t,
        scratch=[
            pltpu.VMEM((deep_channels, deep_cells), BF16),
            pltpu.VMEM((n_gy, 4 * channels // n_gy, deep_channels), F32),
        ],
    )
    shared = [swapped(grad, "gy", code) if code else grad for code in range(n_gy)]
    shared[1], level_t = lax.optimization_barrier((shared[1], level_t))
    odd = odd_pairs(level_t)
    keep, send, near = call(
        lambda *refs: weight_kernel(n_gy, (rows, cols, channels), *refs),
        (
            shape((27 * half, channels), F32),
            shape((27 * half, channels), wire),
            shape((rows + 2, cols, channels), BF16),
        ),
        even,
        level_t,
        odd,
        *shared,
        scratch=[
            pltpu.VMEM((n_gy * rows + 2, cols, 3 * channels), BF16),
            pltpu.VMEM((n_gy, 3 * part, cells), BF16),
            pltpu.VMEM((2, 27 * half, channels), F32),
        ],
    )
    send, *others = lax.optimization_barrier((send, *others))
    downs = [down] + [swapped(value, "gy", code + 1) for code, value in enumerate(others)]
    send = swapped(send, "gz", 1)

    def input_part(near_even, near_odd):
        return call(
            input_kernel,
            shape((rows, cols, channels), BF16),
            near_even,
            near,
            near_odd,
            conv_weight,
        )

    cell_total = devices * cells
    n_z = n_gz // 2
    total_rows = 27 * half + down_count
    piece = -(-total_rows // (16 * n_z)) * 16
    if n_z <= 4:
        own, *pieces = call(
            cut_kernel,
            [shape((piece, channels), F32)] + [shape((piece, channels), BF16)] * (n_z - 1),
            keep,
            send,
            *downs,
            scratch=[pltpu.VMEM((n_z, piece, channels), F32)],
        )
        own, near, *pieces = lax.optimization_barrier((own, near, *pieces))
        near_even = even_pairs(near)
        pieces = [swapped(value, "gz", 2 * code + 2) for code, value in enumerate(pieces)]
        *pieces, near_even = lax.optimization_barrier((*pieces, near_even))
        total = own + sum(value.astype(F32) for value in pieces)
        first = lax.axis_index("gz") // 2 * piece
    else:
        down = sum(value.astype(F32) for value in downs)
        total = jnp.concatenate([keep + send.astype(F32), down], axis=0)
        code = n_gz // 2
        while code > 1:
            total = total + swapped(total, "gz", code)
            code //= 2
        first = 0
        near_even = even_pairs(near)
    row = first + lax.broadcasted_iota(jnp.int32, total.shape, 0)
    scale = jnp.where(
        row < 27 * half, 1 / math.sqrt(cell_total), 1 / math.sqrt(cell_total // 8)
    )
    total = (total * scale).astype(BF16)
    total, near = lax.optimization_barrier((total, near))
    near_odd = odd_pairs(near)
    input_grad = input_part(near_even, near_odd)
    if n_z <= 4:
        pieces = [swapped(total, "gz", 2 * code) if code else total for code in range(n_z)]
        total = jnp.stack(pieces)
    else:
        total = total[None]
    pair = [total, swapped(total, "gz", 1)]
    blocks = []
    for index, block in enumerate(pair):
        line = [block]
        code = n_gy // 2
        while code:
            if code == 1 and index == 1:
                input_grad, *line = lax.optimization_barrier((input_grad, *line))
            line = line + [swapped(value, "gy", code) for value in line]
            code //= 2
        blocks += [line[reversed_bits(place, n_gy)] for place in range(n_gy)]
    conv_grad, down_grad = call(
        lambda *refs: place_kernel(n_gy, *refs),
        (
            shape((27, n_gy, 2, half, channels), BF16),
            shape((2, n_gy, 4 * channels // n_gy, deep_channels), BF16),
        ),
        *blocks,
    )
    return (
        input_grad[None],
        conv_grad.reshape(conv_weight.shape),
        down_grad.reshape(down_weight.shape),
    )


def solution(mesh):
    return jax.shard_map(
        per_device,
        mesh=mesh,
        in_specs=(
            P("gz", "gy", None, None),
            P("gz", "gy", None, None),
            P(),
            P(),
            P("gz", "gy", None, None),
            P(None, "gy", None, "gz"),
        ),
        out_specs=(P("gz", "gy", None, None), P(), P()),
        check_vma=False,
    )
```

```python
import math

import jax
import jax.numpy as jnp
from jax import lax
from jax.experimental import pallas as pl
from jax.experimental.pallas import tpu as pltpu
from jax.sharding import PartitionSpec as P

F32 = jnp.float32
BF16 = jnp.bfloat16
VMEM_LIMIT = 40 * 1024 * 1024


def call(kernel, out_shape, *operands, scratch=()):
    return pl.pallas_call(
        kernel,
        out_shape=out_shape,
        scratch_shapes=list(scratch),
        compiler_params=pltpu.CompilerParams(vmem_limit_bytes=VMEM_LIMIT),
    )(*operands)


def shifted(cells, step):
    if step == 0:
        return cells
    cols = cells.shape[1]
    moved = pltpu.roll(cells, step % cols, 1)
    col = lax.broadcasted_iota(jnp.int32, cells.shape, 1)
    keep = col >= step if step > 0 else col < cols + step
    return jnp.where(keep, moved, 0.0)


def deep_kernel(deep, keep, send, turned):
    planes = deep.shape[0]
    half = planes // 2
    for plane in range(planes):
        turned[plane] = deep[plane].astype(F32).T.astype(BF16)
    upper = lax.axis_index("gz") // planes
    keep[...] = turned[pl.ds(upper * half, half)]
    send[...] = turned[pl.ds((1 - upper) * half, half)]


def level_kernel(level, *rest):
    outs, level_t = rest[:-1], rest[-1]
    turned = level[...].astype(F32).T.astype(BF16)
    part = level_t.shape[1]
    for owner in range(len(outs)):
        level_t[owner] = turned[owner * part : (owner + 1) * part]
    me = lax.axis_index("gy")
    for code, out in enumerate(outs):
        out[...] = level_t[jnp.bitwise_xor(me, code)]


def mask_kernel(n_gy, pre, skip, weight, *rest):
    deeps, rest = rest[: -n_gy - 3], rest[-n_gy - 3 :]
    grad_out, kept, *outs, deep_t, down_all = rest
    if len(deeps) > 1:
        count, share = deeps[0].shape[:2]
        me = lax.axis_index("gz")
        for place in range(2 * count):
            owner = jnp.bitwise_xor(me, reversed_bits(place, 2 * count))
            first = pl.multiple_of(owner * share, share)
            deep_t[pl.ds(first, share)] = deeps[place // count][place % count]
    else:
        deep_t[...] = deeps[0][...]
    rows, cols, channels = pre.shape
    half = rows // 2
    deep_cols = cols // 2
    cells = half * cols
    deep_cells = half * deep_cols
    wide = lax.broadcasted_iota(jnp.int32, (deep_cells, cells), 1) // 2
    deep = lax.broadcasted_iota(jnp.int32, (deep_cells, cells), 0)
    repeat = (wide == deep).astype(BF16)
    spread = jnp.dot(deep_t[...], repeat, preferred_element_type=F32).astype(BF16)
    col = lax.broadcasted_iota(jnp.int32, (cells, channels), 0) % 2
    count = down_all.shape[1]
    for b in range(2):
        parts = [
            lax.dot_general(
                spread, weight[b, c], (((0,), (1,)), ((), ())), preferred_element_type=F32
            )
            for c in range(2)
        ]
        part = jnp.where(col == 0, parts[0], parts[1]).reshape(half, cols, channels)
        for y in range(half):
            row = 2 * y + b
            pre_row = pre[row].astype(F32)
            total = part[y] + skip[row].astype(F32)
            grad = jnp.where(pre_row > 0, total, 0.0).astype(BF16)
            grad_out[pl.ds(row * cols, cols)] = grad
        hidden = jnp.concatenate(
            [jnp.maximum(pre[2 * y + b].astype(F32), 0.0) for y in range(half)], axis=0
        )
        for c in range(2):
            one = jnp.where(col == c, hidden, 0.0).astype(BF16)
            down = lax.dot_general(
                one, spread, (((0,), (1,)), ((), ())), preferred_element_type=F32
            )
            for first, owner, inner, take in segments(channels, count, channels, (b * 2 + c) * channels):
                down_all[owner, pl.ds(inner, take)] = down[first : first + take]
    me = lax.axis_index("gy")
    for code, out in enumerate([kept, *outs]):
        owner = jnp.bitwise_xor(me, code)
        for side in range(down_all.shape[2] // channels):
            out[pl.ds(side * count, count)] = down_all[
                owner, :, pl.ds(side * channels, channels)
            ].astype(out.dtype)


def segments(rows, piece, unit, base=0):
    row = 0
    while row < rows:
        take = min(rows - row, unit - row % unit, piece - (base + row) % piece)
        yield row, (base + row) // piece, (base + row) % piece, take
        row += take


def sides(even, odd):
    upper = lax.axis_index("gz") % 2 == 0
    low = jnp.where(upper, odd[...].astype(F32), even[...].astype(F32)).astype(BF16)
    high = jnp.where(upper, even[...].astype(F32), odd[...].astype(F32)).astype(BF16)
    return low, high


def weight_kernel(n_gy, shape, *refs):
    even, own, odd = refs[:3]
    shared = refs[3 : 3 + n_gy]
    keep, send, near, wide, level, halves = refs[3 + n_gy :]
    rows, cols, channels = shape
    part = own.shape[1]
    cells = rows * cols
    half = part // 2
    rows_all = n_gy * rows
    me = lax.axis_index("gy")
    low, high = sides(even, odd)
    for edge in (0, rows_all + 1):
        wide[edge] = jnp.zeros(wide.shape[1:], BF16)
    for code in range(n_gy):
        owner = jnp.bitwise_xor(me, code)
        grads = shared[code][pl.ds(0, cells)].reshape(rows, cols, channels).astype(F32)
        for kx in range(3):
            wide[pl.ds(1 + owner * rows, rows), :, pl.ds(kx * channels, channels)] = shifted(
                grads, kx - 1
            ).astype(BF16)
        for kz, plane in enumerate((low[code], own[code], high[code])):
            level[owner, pl.ds(kz * part, part)] = plane
    near[...] = wide[pl.ds(me * rows, rows + 2), :, pl.ds(channels, channels)]
    for ky in range(3):
        total = None
        for owner in range(n_gy):
            slab = wide[pl.ds(2 - ky + owner * rows, rows)].reshape(cells, 3 * channels)
            term = jnp.dot(level[owner], slab, preferred_element_type=F32)
            total = term if total is None else total + term
        for kz in range(3):
            for kx in range(3):
                value = total[kz * part : (kz + 1) * part, kx * channels : (kx + 1) * channels]
                index = (kz * 3 + ky) * 3 + kx
                for side in range(2):
                    halves[side, pl.ds(index * half, half)] = value[side * half : (side + 1) * half]
    side = lax.axis_index("gz") % 2
    keep[...] = halves[side]
    send[...] = halves[1 - side].astype(send.dtype)


def input_kernel(even, own, odd, weight, out):
    rows, cols, channels = out.shape
    low, high = sides(even, odd)
    planes = (low, own, high)
    total = None
    for kz in range(3):
        for ky in range(3):
            slab = planes[2 - kz][2 - ky : 2 - ky + rows].reshape(rows * cols, channels)
            term = lax.dot_general(
                slab,
                weight[kz, ky].reshape(3 * channels, channels),
                (((1,), (1,)), ((), ())),
                preferred_element_type=F32,
            )
            total = term if total is None else total + term
    answer = None
    for kx in range(3):
        part = total[:, kx * channels : (kx + 1) * channels].reshape(rows, cols, channels)
        part = shifted(part, kx - 1)
        answer = part if answer is None else answer + part
    out[...] = answer.astype(BF16)


def reversed_bits(code, count):
    place, bit = 0, 1
    while bit < count:
        place = place * 2 + code // bit % 2
        bit *= 2
    return place


def place_kernel(n_gy, *refs):
    blocks, (conv, down) = refs[: 2 * n_gy], refs[2 * n_gy :]
    me = lax.axis_index("gy")
    parity = lax.axis_index("gz") % 2
    half, channels = conv.shape[3:]
    count, deep_channels = down.shape[2:]
    for index, block in enumerate(blocks):
        side = jnp.bitwise_xor(parity, index // n_gy)
        column = jnp.bitwise_xor(me, index % n_gy)
        for k in range(27):
            conv[k, column, side] = block[pl.ds(k * half, half)]
        for wide in range(deep_channels // channels):
            down[side, column, :, pl.ds(wide * channels, channels)] = block[
                pl.ds(27 * half + wide * count, count)
            ]


def swapped(value, axis, code):
    return lax.ppermute(value, axis, [(i, i ^ code) for i in range(lax.axis_size(axis))])


def even_pairs(value):
    return swapped(value, "gz", 1)


def odd_pairs(value):
    last = lax.axis_size("gz") - 1
    pairs = [(i + d, i + 1 - d) for i in range(1, last, 2) for d in range(2)]
    return lax.ppermute(value, "gz", pairs)


def exchanged(value, axis):
    return lax.all_to_all(value, axis, split_axis=0, concat_axis=0, tiled=True)


def per_device(
    level_input, pre_activation, conv_weight, down_weight, skip_cotangent, deep_cotangent
):
    n_gz = lax.axis_size("gz")
    n_gy = lax.axis_size("gy")
    _, rows, cols, channels = level_input.shape
    planes, deep_rows, deep_cols, share = deep_cotangent.shape
    deep_channels = down_weight.shape[4]
    parity = lax.axis_index("gz") % 2
    devices = n_gz * n_gy
    part = channels // n_gy
    cells = rows * cols
    deep_cells = deep_rows * deep_cols
    half = part // 2
    down_count = 4 * deep_channels // n_gy
    wire = BF16 if n_gz <= 8 else F32
    shape = jax.ShapeDtypeStruct

    level = level_input.reshape(cells, channels)
    deep = deep_cotangent.reshape(planes, deep_cells, share)
    if share % 16 == 0:
        keep, send = call(
            deep_kernel,
            [shape((planes // 2, share, deep_cells), BF16)] * 2,
            deep,
            scratch=[pltpu.VMEM((planes, share, deep_cells), BF16)],
        )
        code = planes
        held = jnp.stack([keep, swapped(send, "gz", code)], axis=1)
        while code > 2:
            code //= 2
            count = code // 2
            upper = lax.axis_index("gz") // code % 2
            keep = lax.dynamic_slice_in_dim(held, upper * count, count, axis=0)
            send = lax.dynamic_slice_in_dim(held, (1 - upper) * count, count, axis=0)
            held = jnp.concatenate([keep, swapped(send, "gz", code)], axis=1)
        deep_t = [held[0], swapped(held[0], "gz", 1)]
    else:
        deep_t = jnp.repeat(jnp.swapaxes(deep, 1, 2), 2, axis=0)
        deep_t = [exchanged(deep_t, "gz").reshape(deep_channels, deep_cells)]
    level_t = call(
        level_kernel,
        [shape((part, cells), BF16)] * n_gy,
        level,
        scratch=[pltpu.VMEM((n_gy, part, cells), BF16)],
    )
    level_t = [swapped(value, "gy", code) if code else value for code, value in enumerate(level_t)]
    level_t = jnp.stack(level_t)
    even = even_pairs(level_t)
    *deep_t, level_t = lax.optimization_barrier((*deep_t, level_t))
    down_slice = lax.dynamic_index_in_dim(down_weight, parity, 0, keepdims=False)
    grad, down, *others = call(
        lambda *refs: mask_kernel(n_gy, *refs),
        [shape((cells, channels), BF16), shape((down_count, channels), F32)]
        + [shape((down_count, channels), BF16)] * (n_gy - 1),
        pre_activation[0],
        skip_cotangent[0],
        down_slice,
        *deep_t,
        scratch=[
            pltpu.VMEM((deep_channels, deep_cells), BF16),
            pltpu.VMEM((n_gy, 4 * channels // n_gy, deep_channels), F32),
        ],
    )
    shared = [swapped(grad, "gy", code) if code else grad for code in range(n_gy)]
    shared[1], level_t = lax.optimization_barrier((shared[1], level_t))
    odd = odd_pairs(level_t)
    even, *others = lax.optimization_barrier((even, *others))
    for code, value in enumerate(others):
        down = down + swapped(value, "gy", code + 1).astype(F32)
    keep, send, near = call(
        lambda *refs: weight_kernel(n_gy, (rows, cols, channels), *refs),
        (
            shape((27 * half, channels), F32),
            shape((27 * half, channels), wire),
            shape((rows + 2, cols, channels), BF16),
        ),
        even,
        level_t,
        odd,
        *shared,
        scratch=[
            pltpu.VMEM((n_gy * rows + 2, cols, 3 * channels), BF16),
            pltpu.VMEM((n_gy, 3 * part, cells), BF16),
            pltpu.VMEM((2, 27 * half, channels), F32),
        ],
    )
    near_even, near_odd = even_pairs(near), odd_pairs(near)
    conv = (keep + swapped(send, "gz", 1).astype(F32)).astype(wire)
    total = jnp.concatenate([conv, down.astype(wire)], axis=0)
    total = lax.optimization_barrier(total)
    code = n_gz // 2
    while code > 1:
        other = swapped(total, "gz", code)
        if code == 4:
            other, near_even, near_odd = lax.optimization_barrier((other, near_even, near_odd))
        if code == 2:
            input_grad = call(
                input_kernel,
                shape((rows, cols, channels), BF16),
                near_even,
                near,
                near_odd,
                conv_weight,
            )
            other, input_grad = lax.optimization_barrier((other, input_grad))
        total = total.astype(F32) + other.astype(F32)
        if code > 2:
            total = lax.optimization_barrier(total.astype(wire))
        code //= 2
    cell_total = devices * cells
    row = lax.broadcasted_iota(jnp.int32, total.shape, 0)
    scale = jnp.where(
        row < 27 * half, 1 / math.sqrt(cell_total), 1 / math.sqrt(cell_total // 8)
    )
    total = (total * scale).astype(BF16)
    pair = [total, swapped(total, "gz", 1)]
    blocks = []
    for index, block in enumerate(pair):
        line = [block]
        code = n_gy // 2
        while code:
            line = line + [swapped(value, "gy", code) for value in line]
            code //= 2
        blocks += [line[reversed_bits(place, n_gy)] for place in range(n_gy)]
    conv_grad, down_grad = call(
        lambda *refs: place_kernel(n_gy, *refs),
        (
            shape((27, n_gy, 2, half, channels), BF16),
            shape((2, n_gy, 4 * channels // n_gy, deep_channels), BF16),
        ),
        *blocks,
    )
    return (
        input_grad[None],
        conv_grad.reshape(conv_weight.shape),
        down_grad.reshape(down_weight.shape),
    )


def solution(mesh):
    return jax.shard_map(
        per_device,
        mesh=mesh,
        in_specs=(
            P("gz", "gy", None, None),
            P("gz", "gy", None, None),
            P(),
            P(),
            P("gz", "gy", None, None),
            P(None, "gy", None, "gz"),
        ),
        out_specs=(P("gz", "gy", None, None), P(), P()),
        check_vma=False,
    )
```

```python
import math

import jax
import jax.numpy as jnp
from jax import lax
from jax.experimental import pallas as pl
from jax.experimental.pallas import tpu as pltpu
from jax.sharding import PartitionSpec as P

F32 = jnp.float32
BF16 = jnp.bfloat16
VMEM_LIMIT = 40 * 1024 * 1024


def call(kernel, out_shape, *operands, scratch=()):
    return pl.pallas_call(
        kernel,
        out_shape=out_shape,
        scratch_shapes=list(scratch),
        compiler_params=pltpu.CompilerParams(vmem_limit_bytes=VMEM_LIMIT),
    )(*operands)


def shifted(cells, step):
    if step == 0:
        return cells
    cols = cells.shape[1]
    moved = pltpu.roll(cells, step % cols, 1)
    col = lax.broadcasted_iota(jnp.int32, cells.shape, 1)
    keep = col >= step if step > 0 else col < cols + step
    return jnp.where(keep, moved, 0.0)


def deep_kernel(deep, keep, send, turned):
    planes = deep.shape[0]
    half = planes // 2
    for plane in range(planes):
        turned[plane] = deep[plane].astype(F32).T.astype(BF16)
    upper = lax.axis_index("gz") // planes
    keep[...] = turned[pl.ds(upper * half, half)]
    send[...] = turned[pl.ds((1 - upper) * half, half)]


def level_kernel(level, *rest):
    outs, level_t = rest[:-1], rest[-1]
    turned = level[...].astype(F32).T.astype(BF16)
    part = level_t.shape[1]
    for owner in range(len(outs)):
        level_t[owner] = turned[owner * part : (owner + 1) * part]
    me = lax.axis_index("gy")
    for code, out in enumerate(outs):
        out[...] = level_t[jnp.bitwise_xor(me, code)]


def mask_kernel(n_gy, pre, skip, weight, *rest):
    deeps, rest = rest[: -n_gy - 3], rest[-n_gy - 3 :]
    grad_out, kept, *outs, deep_t, down_all = rest
    if len(deeps) > 1:
        count, share = deeps[0].shape[:2]
        me = lax.axis_index("gz")
        for place in range(2 * count):
            owner = jnp.bitwise_xor(me, reversed_bits(place, 2 * count))
            first = pl.multiple_of(owner * share, share)
            deep_t[pl.ds(first, share)] = deeps[place // count][place % count]
    else:
        deep_t[...] = deeps[0][...]
    rows, cols, channels = pre.shape
    half = rows // 2
    deep_cols = cols // 2
    cells = half * cols
    deep_cells = half * deep_cols
    wide = lax.broadcasted_iota(jnp.int32, (deep_cells, cells), 1) // 2
    deep = lax.broadcasted_iota(jnp.int32, (deep_cells, cells), 0)
    repeat = (wide == deep).astype(BF16)
    spread = jnp.dot(deep_t[...], repeat, preferred_element_type=F32).astype(BF16)
    col = lax.broadcasted_iota(jnp.int32, (cells, channels), 0) % 2
    count = down_all.shape[1]
    for b in range(2):
        parts = [
            lax.dot_general(
                spread, weight[b, c], (((0,), (1,)), ((), ())), preferred_element_type=F32
            )
            for c in range(2)
        ]
        part = jnp.where(col == 0, parts[0], parts[1]).reshape(half, cols, channels)
        for y in range(half):
            row = 2 * y + b
            pre_row = pre[row].astype(F32)
            total = part[y] + skip[row].astype(F32)
            grad = jnp.where(pre_row > 0, total, 0.0).astype(BF16)
            grad_out[pl.ds(row * cols, cols)] = grad
        hidden = jnp.concatenate(
            [jnp.maximum(pre[2 * y + b].astype(F32), 0.0) for y in range(half)], axis=0
        )
        for c in range(2):
            one = jnp.where(col == c, hidden, 0.0).astype(BF16)
            down = lax.dot_general(
                one, spread, (((0,), (1,)), ((), ())), preferred_element_type=F32
            )
            for first, owner, inner, take in segments(channels, count, channels, (b * 2 + c) * channels):
                down_all[owner, pl.ds(inner, take)] = down[first : first + take]
    me = lax.axis_index("gy")
    for code, out in enumerate([kept, *outs]):
        owner = jnp.bitwise_xor(me, code)
        for side in range(down_all.shape[2] // channels):
            out[pl.ds(side * count, count)] = down_all[
                owner, :, pl.ds(side * channels, channels)
            ].astype(out.dtype)


def segments(rows, piece, unit, base=0):
    row = 0
    while row < rows:
        take = min(rows - row, unit - row % unit, piece - (base + row) % piece)
        yield row, (base + row) // piece, (base + row) % piece, take
        row += take


def sides(even, odd):
    upper = lax.axis_index("gz") % 2 == 0
    low = jnp.where(upper, odd[...].astype(F32), even[...].astype(F32)).astype(BF16)
    high = jnp.where(upper, even[...].astype(F32), odd[...].astype(F32)).astype(BF16)
    return low, high


def weight_kernel(n_gy, shape, *refs):
    even, own, odd = refs[:3]
    shared = refs[3 : 3 + n_gy]
    keep, send, near, wide, level, halves = refs[3 + n_gy :]
    rows, cols, channels = shape
    part = own.shape[1]
    cells = rows * cols
    half = part // 2
    rows_all = n_gy * rows
    me = lax.axis_index("gy")
    low, high = sides(even, odd)
    for edge in (0, rows_all + 1):
        wide[edge] = jnp.zeros(wide.shape[1:], BF16)
    for code in range(n_gy):
        owner = jnp.bitwise_xor(me, code)
        grads = shared[code][pl.ds(0, cells)].reshape(rows, cols, channels).astype(F32)
        for kx in range(3):
            wide[pl.ds(1 + owner * rows, rows), :, pl.ds(kx * channels, channels)] = shifted(
                grads, kx - 1
            ).astype(BF16)
        for kz, plane in enumerate((low[code], own[code], high[code])):
            level[owner, pl.ds(kz * part, part)] = plane
    near[...] = wide[pl.ds(me * rows, rows + 2), :, pl.ds(channels, channels)]
    for ky in range(3):
        total = None
        for owner in range(n_gy):
            slab = wide[pl.ds(2 - ky + owner * rows, rows)].reshape(cells, 3 * channels)
            term = jnp.dot(level[owner], slab, preferred_element_type=F32)
            total = term if total is None else total + term
        for kz in range(3):
            for kx in range(3):
                value = total[kz * part : (kz + 1) * part, kx * channels : (kx + 1) * channels]
                index = (kz * 3 + ky) * 3 + kx
                for side in range(2):
                    halves[side, pl.ds(index * half, half)] = value[side * half : (side + 1) * half]
    side = lax.axis_index("gz") % 2
    keep[...] = halves[side]
    send[...] = halves[1 - side].astype(send.dtype)


def input_kernel(even, own, odd, weight, out):
    rows, cols, channels = out.shape
    low, high = sides(even, odd)
    planes = (low, own, high)
    total = None
    for kz in range(3):
        for ky in range(3):
            slab = planes[2 - kz][2 - ky : 2 - ky + rows].reshape(rows * cols, channels)
            term = lax.dot_general(
                slab,
                weight[kz, ky].reshape(3 * channels, channels),
                (((1,), (1,)), ((), ())),
                preferred_element_type=F32,
            )
            total = term if total is None else total + term
    answer = None
    for kx in range(3):
        part = total[:, kx * channels : (kx + 1) * channels].reshape(rows, cols, channels)
        part = shifted(part, kx - 1)
        answer = part if answer is None else answer + part
    out[...] = answer.astype(BF16)


def reversed_bits(code, count):
    place, bit = 0, 1
    while bit < count:
        place = place * 2 + code // bit % 2
        bit *= 2
    return place


def place_kernel(n_gy, *refs):
    blocks, (conv, down) = refs[: 2 * n_gy], refs[2 * n_gy :]
    me = lax.axis_index("gy")
    parity = lax.axis_index("gz") % 2
    half, channels = conv.shape[3:]
    count, deep_channels = down.shape[2:]
    for index, block in enumerate(blocks):
        side = jnp.bitwise_xor(parity, index // n_gy)
        column = jnp.bitwise_xor(me, index % n_gy)
        for k in range(27):
            conv[k, column, side] = block[pl.ds(k * half, half)]
        for wide in range(deep_channels // channels):
            down[side, column, :, pl.ds(wide * channels, channels)] = block[
                pl.ds(27 * half + wide * count, count)
            ]


def swapped(value, axis, code):
    return lax.ppermute(value, axis, [(i, i ^ code) for i in range(lax.axis_size(axis))])


def crossed(value, code_gz, code_gy):
    count = lax.axis_size("gy")
    pairs = [
        (i * count + j, (i ^ code_gz) * count + (j ^ code_gy))
        for i in range(lax.axis_size("gz"))
        for j in range(count)
    ]
    return lax.ppermute(value, ("gz", "gy"), pairs)


def even_pairs(value):
    return swapped(value, "gz", 1)


def odd_pairs(value):
    last = lax.axis_size("gz") - 1
    pairs = [(i + d, i + 1 - d) for i in range(1, last, 2) for d in range(2)]
    return lax.ppermute(value, "gz", pairs)


def exchanged(value, axis):
    return lax.all_to_all(value, axis, split_axis=0, concat_axis=0, tiled=True)


def per_device(
    level_input, pre_activation, conv_weight, down_weight, skip_cotangent, deep_cotangent
):
    n_gz = lax.axis_size("gz")
    n_gy = lax.axis_size("gy")
    _, rows, cols, channels = level_input.shape
    planes, deep_rows, deep_cols, share = deep_cotangent.shape
    deep_channels = down_weight.shape[4]
    parity = lax.axis_index("gz") % 2
    devices = n_gz * n_gy
    part = channels // n_gy
    cells = rows * cols
    deep_cells = deep_rows * deep_cols
    half = part // 2
    down_count = 4 * deep_channels // n_gy
    wire = BF16 if n_gz <= 8 else F32
    shape = jax.ShapeDtypeStruct

    level = level_input.reshape(cells, channels)
    deep = deep_cotangent.reshape(planes, deep_cells, share)
    if share % 16 == 0:
        keep, send = call(
            deep_kernel,
            [shape((planes // 2, share, deep_cells), BF16)] * 2,
            deep,
            scratch=[pltpu.VMEM((planes, share, deep_cells), BF16)],
        )
        code = planes
        held = jnp.stack([keep, swapped(send, "gz", code)], axis=1)
        while code > 2:
            code //= 2
            count = code // 2
            upper = lax.axis_index("gz") // code % 2
            keep = lax.dynamic_slice_in_dim(held, upper * count, count, axis=0)
            send = lax.dynamic_slice_in_dim(held, (1 - upper) * count, count, axis=0)
            held = jnp.concatenate([keep, swapped(send, "gz", code)], axis=1)
        deep_t = [held[0], swapped(held[0], "gz", 1)]
    else:
        deep_t = jnp.repeat(jnp.swapaxes(deep, 1, 2), 2, axis=0)
        deep_t = [exchanged(deep_t, "gz").reshape(deep_channels, deep_cells)]
    level_t = call(
        level_kernel,
        [shape((part, cells), BF16)] * n_gy,
        level,
        scratch=[pltpu.VMEM((n_gy, part, cells), BF16)],
    )
    level_t = [swapped(value, "gy", code) if code else value for code, value in enumerate(level_t)]
    level_t = jnp.stack(level_t)
    even = even_pairs(level_t)
    *deep_t, level_t = lax.optimization_barrier((*deep_t, level_t))
    down_slice = lax.dynamic_index_in_dim(down_weight, parity, 0, keepdims=False)
    grad, down, *others = call(
        lambda *refs: mask_kernel(n_gy, *refs),
        [shape((cells, channels), BF16), shape((down_count, channels), F32)]
        + [shape((down_count, channels), BF16)] * (n_gy - 1),
        pre_activation[0],
        skip_cotangent[0],
        down_slice,
        *deep_t,
        scratch=[
            pltpu.VMEM((deep_channels, deep_cells), BF16),
            pltpu.VMEM((n_gy, 4 * channels // n_gy, deep_channels), F32),
        ],
    )
    shared = [swapped(grad, "gy", code) if code else grad for code in range(n_gy)]
    shared[1], level_t = lax.optimization_barrier((shared[1], level_t))
    odd = odd_pairs(level_t)
    even, *others = lax.optimization_barrier((even, *others))
    for code, value in enumerate(others):
        down = down + swapped(value, "gy", code + 1).astype(F32)
    keep, send, near = call(
        lambda *refs: weight_kernel(n_gy, (rows, cols, channels), *refs),
        (
            shape((27 * half, channels), F32),
            shape((27 * half, channels), wire),
            shape((rows + 2, cols, channels), BF16),
        ),
        even,
        level_t,
        odd,
        *shared,
        scratch=[
            pltpu.VMEM((n_gy * rows + 2, cols, 3 * channels), BF16),
            pltpu.VMEM((n_gy, 3 * part, cells), BF16),
            pltpu.VMEM((2, 27 * half, channels), F32),
        ],
    )
    near_even, near_odd = even_pairs(near), odd_pairs(near)
    conv = (keep + swapped(send, "gz", 1).astype(F32)).astype(wire)
    total = jnp.concatenate([conv, down.astype(wire)], axis=0)
    total = lax.optimization_barrier(total)
    code = n_gz // 2
    while code > 1:
        other = swapped(total, "gz", code)
        if code == 4:
            other, near_even, near_odd = lax.optimization_barrier((other, near_even, near_odd))
        if code == 2:
            input_grad = call(
                input_kernel,
                shape((rows, cols, channels), BF16),
                near_even,
                near,
                near_odd,
                conv_weight,
            )
            other, input_grad = lax.optimization_barrier((other, input_grad))
        total = total.astype(F32) + other.astype(F32)
        if code > 2:
            total = lax.optimization_barrier(total.astype(wire))
        code //= 2
    cell_total = devices * cells
    row = lax.broadcasted_iota(jnp.int32, total.shape, 0)
    scale = jnp.where(
        row < 27 * half, 1 / math.sqrt(cell_total), 1 / math.sqrt(cell_total // 8)
    )
    total = (total * scale).astype(BF16)
    if n_gy == 4:
        lines = [
            [total, swapped(total, "gy", 2)],
            [swapped(total, "gz", 1), crossed(total, 1, 2)],
        ]
        blocks = []
        for near_block, far_block in lines:
            blocks += [near_block, swapped(near_block, "gy", 1)]
            blocks += [far_block, swapped(far_block, "gy", 1)]
    else:
        blocks = [
            swapped(block, "gy", code) if code else block
            for block in (total, swapped(total, "gz", 1))
            for code in range(n_gy)
        ]
    conv_grad, down_grad = call(
        lambda *refs: place_kernel(n_gy, *refs),
        (
            shape((27, n_gy, 2, half, channels), BF16),
            shape((2, n_gy, 4 * channels // n_gy, deep_channels), BF16),
        ),
        *blocks,
    )
    return (
        input_grad[None],
        conv_grad.reshape(conv_weight.shape),
        down_grad.reshape(down_weight.shape),
    )


def solution(mesh):
    return jax.shard_map(
        per_device,
        mesh=mesh,
        in_specs=(
            P("gz", "gy", None, None),
            P("gz", "gy", None, None),
            P(),
            P(),
            P("gz", "gy", None, None),
            P(None, "gy", None, "gz"),
        ),
        out_specs=(P("gz", "gy", None, None), P(), P()),
        check_vma=False,
    )
```

```python
import math

import jax
import jax.numpy as jnp
from jax import lax
from jax.experimental import pallas as pl
from jax.experimental.pallas import tpu as pltpu
from jax.sharding import PartitionSpec as P

F32 = jnp.float32
BF16 = jnp.bfloat16
VMEM_LIMIT = 40 * 1024 * 1024


def call(kernel, out_shape, *operands, scratch=()):
    return pl.pallas_call(
        kernel,
        out_shape=out_shape,
        scratch_shapes=list(scratch),
        compiler_params=pltpu.CompilerParams(vmem_limit_bytes=VMEM_LIMIT),
    )(*operands)


def shifted(cells, step):
    if step == 0:
        return cells
    cols = cells.shape[1]
    moved = pltpu.roll(cells, step % cols, 1)
    col = lax.broadcasted_iota(jnp.int32, cells.shape, 1)
    keep = col >= step if step > 0 else col < cols + step
    return jnp.where(keep, moved, 0.0)


def deep_kernel(deep, keep, send, turned):
    planes = deep.shape[0]
    half = planes // 2
    for plane in range(planes):
        turned[plane] = deep[plane].astype(F32).T.astype(BF16)
    upper = lax.axis_index("gz") // planes
    keep[...] = turned[pl.ds(upper * half, half)]
    send[...] = turned[pl.ds((1 - upper) * half, half)]


def level_kernel(level, *rest):
    outs, level_t = rest[:-1], rest[-1]
    turned = level[...].astype(F32).T.astype(BF16)
    part = level_t.shape[1]
    for owner in range(len(outs)):
        level_t[owner] = turned[owner * part : (owner + 1) * part]
    me = lax.axis_index("gy")
    for code, out in enumerate(outs):
        out[...] = level_t[jnp.bitwise_xor(me, code)]


def mask_kernel(n_gy, pre, skip, weight, *rest):
    deeps, rest = rest[: -n_gy - 3], rest[-n_gy - 3 :]
    grad_out, kept, *outs, deep_t, down_all = rest
    if len(deeps) > 1:
        count, share = deeps[0].shape[:2]
        me = lax.axis_index("gz")
        for place in range(2 * count):
            owner = jnp.bitwise_xor(me, reversed_bits(place, 2 * count))
            first = pl.multiple_of(owner * share, share)
            deep_t[pl.ds(first, share)] = deeps[place // count][place % count]
    else:
        deep_t[...] = deeps[0][...]
    rows, cols, channels = pre.shape
    half = rows // 2
    deep_cols = cols // 2
    cells = half * cols
    deep_cells = half * deep_cols
    wide = lax.broadcasted_iota(jnp.int32, (deep_cells, cells), 1) // 2
    deep = lax.broadcasted_iota(jnp.int32, (deep_cells, cells), 0)
    repeat = (wide == deep).astype(BF16)
    spread = jnp.dot(deep_t[...], repeat, preferred_element_type=F32).astype(BF16)
    col = lax.broadcasted_iota(jnp.int32, (cells, channels), 0) % 2
    count = down_all.shape[1]
    for b in range(2):
        parts = [
            lax.dot_general(
                spread, weight[b, c], (((0,), (1,)), ((), ())), preferred_element_type=F32
            )
            for c in range(2)
        ]
        part = jnp.where(col == 0, parts[0], parts[1]).reshape(half, cols, channels)
        for y in range(half):
            row = 2 * y + b
            pre_row = pre[row].astype(F32)
            total = part[y] + skip[row].astype(F32)
            grad = jnp.where(pre_row > 0, total, 0.0).astype(BF16)
            grad_out[pl.ds(row * cols, cols)] = grad
        hidden = jnp.concatenate(
            [jnp.maximum(pre[2 * y + b].astype(F32), 0.0) for y in range(half)], axis=0
        )
        for c in range(2):
            one = jnp.where(col == c, hidden, 0.0).astype(BF16)
            down = lax.dot_general(
                one, spread, (((0,), (1,)), ((), ())), preferred_element_type=F32
            )
            for first, owner, inner, take in segments(channels, count, channels, (b * 2 + c) * channels):
                down_all[owner, pl.ds(inner, take)] = down[first : first + take]
    me = lax.axis_index("gy")
    for code, out in enumerate([kept, *outs]):
        owner = jnp.bitwise_xor(me, code)
        for side in range(down_all.shape[2] // channels):
            out[pl.ds(side * count, count)] = down_all[
                owner, :, pl.ds(side * channels, channels)
            ].astype(out.dtype)


def segments(rows, piece, unit, base=0):
    row = 0
    while row < rows:
        take = min(rows - row, unit - row % unit, piece - (base + row) % piece)
        yield row, (base + row) // piece, (base + row) % piece, take
        row += take


def sides(even, odd):
    upper = lax.axis_index("gz") % 2 == 0
    low = jnp.where(upper, odd[...].astype(F32), even[...].astype(F32)).astype(BF16)
    high = jnp.where(upper, even[...].astype(F32), odd[...].astype(F32)).astype(BF16)
    return low, high


def weight_kernel(n_gy, shape, *refs):
    even, own, odd = refs[:3]
    shared = refs[3 : 3 + n_gy]
    keep, send, near, wide, level, halves = refs[3 + n_gy :]
    rows, cols, channels = shape
    part = own.shape[1]
    cells = rows * cols
    half = part // 2
    rows_all = n_gy * rows
    me = lax.axis_index("gy")
    low, high = sides(even, odd)
    for edge in (0, rows_all + 1):
        wide[edge] = jnp.zeros(wide.shape[1:], BF16)
    for code in range(n_gy):
        owner = jnp.bitwise_xor(me, code)
        grads = shared[code][pl.ds(0, cells)].reshape(rows, cols, channels).astype(F32)
        for kx in range(3):
            wide[pl.ds(1 + owner * rows, rows), :, pl.ds(kx * channels, channels)] = shifted(
                grads, kx - 1
            ).astype(BF16)
        for kz, plane in enumerate((low[code], own[code], high[code])):
            level[owner, pl.ds(kz * part, part)] = plane
    near[...] = wide[pl.ds(me * rows, rows + 2), :, pl.ds(channels, channels)]
    for ky in range(3):
        total = None
        for owner in range(n_gy):
            slab = wide[pl.ds(2 - ky + owner * rows, rows)].reshape(cells, 3 * channels)
            term = jnp.dot(level[owner], slab, preferred_element_type=F32)
            total = term if total is None else total + term
        for kz in range(3):
            for kx in range(3):
                value = total[kz * part : (kz + 1) * part, kx * channels : (kx + 1) * channels]
                index = (kz * 3 + ky) * 3 + kx
                for side in range(2):
                    halves[side, pl.ds(index * half, half)] = value[side * half : (side + 1) * half]
    side = lax.axis_index("gz") % 2
    keep[...] = halves[side]
    send[...] = halves[1 - side].astype(send.dtype)


def input_kernel(even, own, odd, weight, out):
    rows, cols, channels = out.shape
    low, high = sides(even, odd)
    planes = (low, own, high)
    total = None
    for kz in range(3):
        for ky in range(3):
            slab = planes[2 - kz][2 - ky : 2 - ky + rows].reshape(rows * cols, channels)
            term = lax.dot_general(
                slab,
                weight[kz, ky].reshape(3 * channels, channels),
                (((1,), (1,)), ((), ())),
                preferred_element_type=F32,
            )
            total = term if total is None else total + term
    answer = None
    for kx in range(3):
        part = total[:, kx * channels : (kx + 1) * channels].reshape(rows, cols, channels)
        part = shifted(part, kx - 1)
        answer = part if answer is None else answer + part
    out[...] = answer.astype(BF16)


def reversed_bits(code, count):
    place, bit = 0, 1
    while bit < count:
        place = place * 2 + code // bit % 2
        bit *= 2
    return place


def place_kernel(n_gy, *refs):
    blocks, (conv, down) = refs[: 2 * n_gy], refs[2 * n_gy :]
    me = lax.axis_index("gy")
    parity = lax.axis_index("gz") % 2
    half, channels = conv.shape[3:]
    count, deep_channels = down.shape[2:]
    for index, block in enumerate(blocks):
        side = jnp.bitwise_xor(parity, index // n_gy)
        column = jnp.bitwise_xor(me, index % n_gy)
        for k in range(27):
            conv[k, column, side] = block[pl.ds(k * half, half)]
        for wide in range(deep_channels // channels):
            down[side, column, :, pl.ds(wide * channels, channels)] = block[
                pl.ds(27 * half + wide * count, count)
            ]


def swapped(value, axis, code):
    return lax.ppermute(value, axis, [(i, i ^ code) for i in range(lax.axis_size(axis))])


def crossed(value, code_gz, code_gy):
    count = lax.axis_size("gy")
    pairs = [
        (i * count + j, (i ^ code_gz) * count + (j ^ code_gy))
        for i in range(lax.axis_size("gz"))
        for j in range(count)
    ]
    return lax.ppermute(value, ("gz", "gy"), pairs)


def even_pairs(value):
    return swapped(value, "gz", 1)


def odd_pairs(value):
    last = lax.axis_size("gz") - 1
    pairs = [(i + d, i + 1 - d) for i in range(1, last, 2) for d in range(2)]
    return lax.ppermute(value, "gz", pairs)


def exchanged(value, axis):
    return lax.all_to_all(value, axis, split_axis=0, concat_axis=0, tiled=True)


def per_device(
    level_input, pre_activation, conv_weight, down_weight, skip_cotangent, deep_cotangent
):
    n_gz = lax.axis_size("gz")
    n_gy = lax.axis_size("gy")
    _, rows, cols, channels = level_input.shape
    planes, deep_rows, deep_cols, share = deep_cotangent.shape
    deep_channels = down_weight.shape[4]
    parity = lax.axis_index("gz") % 2
    devices = n_gz * n_gy
    part = channels // n_gy
    cells = rows * cols
    deep_cells = deep_rows * deep_cols
    half = part // 2
    down_count = 4 * deep_channels // n_gy
    wire = BF16 if n_gz <= 8 else F32
    shape = jax.ShapeDtypeStruct

    level = level_input.reshape(cells, channels)
    deep = deep_cotangent.reshape(planes, deep_cells, share)
    if share % 16 == 0:
        keep, send = call(
            deep_kernel,
            [shape((planes // 2, share, deep_cells), BF16)] * 2,
            deep,
            scratch=[pltpu.VMEM((planes, share, deep_cells), BF16)],
        )
        code = planes
        held = jnp.stack([keep, swapped(send, "gz", code)], axis=1)
        while code > 2:
            code //= 2
            count = code // 2
            upper = lax.axis_index("gz") // code % 2
            keep = lax.dynamic_slice_in_dim(held, upper * count, count, axis=0)
            send = lax.dynamic_slice_in_dim(held, (1 - upper) * count, count, axis=0)
            held = jnp.concatenate([keep, swapped(send, "gz", code)], axis=1)
        deep_t = [held[0], swapped(held[0], "gz", 1)]
    else:
        deep_t = jnp.repeat(jnp.swapaxes(deep, 1, 2), 2, axis=0)
        deep_t = [exchanged(deep_t, "gz").reshape(deep_channels, deep_cells)]
    level_t = call(
        level_kernel,
        [shape((part, cells), BF16)] * n_gy,
        level,
        scratch=[pltpu.VMEM((n_gy, part, cells), BF16)],
    )
    level_t = [swapped(value, "gy", code) if code else value for code, value in enumerate(level_t)]
    level_t = jnp.stack(level_t)
    even = even_pairs(level_t)
    *deep_t, level_t = lax.optimization_barrier((*deep_t, level_t))
    down_slice = lax.dynamic_index_in_dim(down_weight, parity, 0, keepdims=False)
    grad, down, *others = call(
        lambda *refs: mask_kernel(n_gy, *refs),
        [shape((cells, channels), BF16), shape((down_count, channels), F32)]
        + [shape((down_count, channels), BF16)] * (n_gy - 1),
        pre_activation[0],
        skip_cotangent[0],
        down_slice,
        *deep_t,
        scratch=[
            pltpu.VMEM((deep_channels, deep_cells), BF16),
            pltpu.VMEM((n_gy, 4 * channels // n_gy, deep_channels), F32),
        ],
    )
    shared = [swapped(grad, "gy", code) if code else grad for code in range(n_gy)]
    shared[1], level_t = lax.optimization_barrier((shared[1], level_t))
    odd = odd_pairs(level_t)
    even, *others = lax.optimization_barrier((even, *others))
    for code, value in enumerate(others):
        down = down + swapped(value, "gy", code + 1).astype(F32)
    keep, send, near = call(
        lambda *refs: weight_kernel(n_gy, (rows, cols, channels), *refs),
        (
            shape((27 * half, channels), F32),
            shape((27 * half, channels), wire),
            shape((rows + 2, cols, channels), BF16),
        ),
        even,
        level_t,
        odd,
        *shared,
        scratch=[
            pltpu.VMEM((n_gy * rows + 2, cols, 3 * channels), BF16),
            pltpu.VMEM((n_gy, 3 * part, cells), BF16),
            pltpu.VMEM((2, 27 * half, channels), F32),
        ],
    )
    near_odd, near_even = odd_pairs(near), even_pairs(near)
    def rounded(value):
        return lax.optimization_barrier(value.astype(wire))

    def added(value, other):
        return value.astype(F32) + other.astype(F32)

    cell_total = devices * cells
    down = rounded(down)
    codes = []
    code = n_gz // 2
    while code > 1:
        codes.append(code)
        code //= 2
    send = swapped(send, "gz", 1)
    for index, code in enumerate(codes):
        down_other = swapped(down, "gz", code)
        if index == 0:
            send, down_other = lax.optimization_barrier((send, down_other))
            conv = rounded(keep + send.astype(F32))
        else:
            conv_other = swapped(conv, "gz", codes[index - 1])
            if index == 1:
                tied = (conv_other, down_other, near_odd, near_even)
                conv_other, down_other, near_odd, near_even = lax.optimization_barrier(tied)
            conv = rounded(added(conv, conv_other))
        down = added(down, down_other)
        if index < len(codes) - 1:
            down = rounded(down)
    conv_other = swapped(conv, "gz", codes[-1])
    input_grad = call(
        input_kernel,
        shape((rows, cols, channels), BF16),
        near_even,
        near,
        near_odd,
        conv_weight,
    )
    conv_other, input_grad = lax.optimization_barrier((conv_other, input_grad))
    conv = added(conv, conv_other) * (1 / math.sqrt(cell_total))
    down = down * (1 / math.sqrt(cell_total // 8))
    total = jnp.concatenate([conv.astype(BF16), down.astype(BF16)], axis=0)
    if n_gy == 4:
        lines = [
            [total, swapped(total, "gy", 2)],
            [swapped(total, "gz", 1), crossed(total, 1, 2)],
        ]
        blocks = []
        for near_block, far_block in lines:
            blocks += [near_block, swapped(near_block, "gy", 1)]
            blocks += [far_block, swapped(far_block, "gy", 1)]
    else:
        blocks = [
            swapped(block, "gy", code) if code else block
            for block in (total, swapped(total, "gz", 1))
            for code in range(n_gy)
        ]
    conv_grad, down_grad = call(
        lambda *refs: place_kernel(n_gy, *refs),
        (
            shape((27, n_gy, 2, half, channels), BF16),
            shape((2, n_gy, 4 * channels // n_gy, deep_channels), BF16),
        ),
        *blocks,
    )
    return (
        input_grad[None],
        conv_grad.reshape(conv_weight.shape),
        down_grad.reshape(down_weight.shape),
    )


def solution(mesh):
    return jax.shard_map(
        per_device,
        mesh=mesh,
        in_specs=(
            P("gz", "gy", None, None),
            P("gz", "gy", None, None),
            P(),
            P(),
            P("gz", "gy", None, None),
            P(None, "gy", None, "gz"),
        ),
        out_specs=(P("gz", "gy", None, None), P(), P()),
        check_vma=False,
    )
```

```python
import math

import jax
import jax.numpy as jnp
from jax import lax
from jax.experimental import pallas as pl
from jax.experimental.pallas import tpu as pltpu
from jax.sharding import PartitionSpec as P

F32 = jnp.float32
BF16 = jnp.bfloat16
VMEM_LIMIT = 40 * 1024 * 1024


def call(kernel, out_shape, *operands, scratch=()):
    return pl.pallas_call(
        kernel,
        out_shape=out_shape,
        scratch_shapes=list(scratch),
        compiler_params=pltpu.CompilerParams(vmem_limit_bytes=VMEM_LIMIT),
    )(*operands)


def shifted(cells, step):
    if step == 0:
        return cells
    cols = cells.shape[1]
    moved = pltpu.roll(cells, step % cols, 1)
    col = lax.broadcasted_iota(jnp.int32, cells.shape, 1)
    keep = col >= step if step > 0 else col < cols + step
    return jnp.where(keep, moved, 0.0)


def deep_kernel(deep, keep, send, turned):
    planes = deep.shape[0]
    half = planes // 2
    for plane in range(planes):
        turned[plane] = deep[plane].astype(F32).T.astype(BF16)
    upper = lax.axis_index("gz") // planes
    keep[...] = turned[pl.ds(upper * half, half)]
    send[...] = turned[pl.ds((1 - upper) * half, half)]


def level_kernel(level, *rest):
    outs, level_t = rest[:-1], rest[-1]
    turned = level[...].astype(F32).T.astype(BF16)
    part = level_t.shape[1]
    for owner in range(len(outs)):
        level_t[owner] = turned[owner * part : (owner + 1) * part]
    me = lax.axis_index("gy")
    for code, out in enumerate(outs):
        out[...] = level_t[jnp.bitwise_xor(me, code)]


def mask_kernel(n_gy, pre, skip, weight, *rest):
    deeps, rest = rest[: -n_gy - 3], rest[-n_gy - 3 :]
    grad_out, kept, *outs, deep_t, down_all = rest
    if len(deeps) > 1:
        count, share = deeps[0].shape[:2]
        me = lax.axis_index("gz")
        for place in range(2 * count):
            owner = jnp.bitwise_xor(me, reversed_bits(place, 2 * count))
            first = pl.multiple_of(owner * share, share)
            deep_t[pl.ds(first, share)] = deeps[place // count][place % count]
    else:
        deep_t[...] = deeps[0][...]
    rows, cols, channels = pre.shape
    half = rows // 2
    deep_cols = cols // 2
    cells = half * cols
    deep_cells = half * deep_cols
    wide = lax.broadcasted_iota(jnp.int32, (deep_cells, cells), 1) // 2
    deep = lax.broadcasted_iota(jnp.int32, (deep_cells, cells), 0)
    repeat = (wide == deep).astype(BF16)
    spread = jnp.dot(deep_t[...], repeat, preferred_element_type=F32).astype(BF16)
    col = lax.broadcasted_iota(jnp.int32, (cells, channels), 0) % 2
    count = down_all.shape[1]
    for b in range(2):
        parts = [
            lax.dot_general(
                spread, weight[b, c], (((0,), (1,)), ((), ())), preferred_element_type=F32
            )
            for c in range(2)
        ]
        part = jnp.where(col == 0, parts[0], parts[1]).reshape(half, cols, channels)
        for y in range(half):
            row = 2 * y + b
            pre_row = pre[row].astype(F32)
            total = part[y] + skip[row].astype(F32)
            grad = jnp.where(pre_row > 0, total, 0.0).astype(BF16)
            grad_out[pl.ds(row * cols, cols)] = grad
        hidden = jnp.concatenate(
            [jnp.maximum(pre[2 * y + b].astype(F32), 0.0) for y in range(half)], axis=0
        )
        for c in range(2):
            one = jnp.where(col == c, hidden, 0.0).astype(BF16)
            down = lax.dot_general(
                one, spread, (((0,), (1,)), ((), ())), preferred_element_type=F32
            )
            for first, owner, inner, take in segments(channels, count, channels, (b * 2 + c) * channels):
                down_all[owner, pl.ds(inner, take)] = down[first : first + take]
    me = lax.axis_index("gy")
    for code, out in enumerate([kept, *outs]):
        owner = jnp.bitwise_xor(me, code)
        for side in range(down_all.shape[2] // channels):
            out[pl.ds(side * count, count)] = down_all[
                owner, :, pl.ds(side * channels, channels)
            ].astype(out.dtype)


def segments(rows, piece, unit, base=0):
    row = 0
    while row < rows:
        take = min(rows - row, unit - row % unit, piece - (base + row) % piece)
        yield row, (base + row) // piece, (base + row) % piece, take
        row += take


def sides(even, odd):
    upper = lax.axis_index("gz") % 2 == 0
    low = jnp.where(upper, odd[...].astype(F32), even[...].astype(F32)).astype(BF16)
    high = jnp.where(upper, even[...].astype(F32), odd[...].astype(F32)).astype(BF16)
    return low, high


def weight_kernel(n_gy, shape, *refs):
    even, own, odd = refs[:3]
    shared = refs[3 : 3 + n_gy]
    keep, send, near, wide, level, halves = refs[3 + n_gy :]
    rows, cols, channels = shape
    part = own.shape[1]
    cells = rows * cols
    half = part // 2
    rows_all = n_gy * rows
    me = lax.axis_index("gy")
    low, high = sides(even, odd)
    for edge in (0, rows_all + 1):
        wide[edge] = jnp.zeros(wide.shape[1:], BF16)
    for code in range(n_gy):
        owner = jnp.bitwise_xor(me, code)
        grads = shared[code][pl.ds(0, cells)].reshape(rows, cols, channels).astype(F32)
        for kx in range(3):
            wide[pl.ds(1 + owner * rows, rows), :, pl.ds(kx * channels, channels)] = shifted(
                grads, kx - 1
            ).astype(BF16)
        for kz, plane in enumerate((low[code], own[code], high[code])):
            level[owner, pl.ds(kz * part, part)] = plane
    near[...] = wide[pl.ds(me * rows, rows + 2), :, pl.ds(channels, channels)]
    for ky in range(3):
        total = None
        for owner in range(n_gy):
            slab = wide[pl.ds(2 - ky + owner * rows, rows)].reshape(cells, 3 * channels)
            term = jnp.dot(level[owner], slab, preferred_element_type=F32)
            total = term if total is None else total + term
        for kz in range(3):
            for kx in range(3):
                value = total[kz * part : (kz + 1) * part, kx * channels : (kx + 1) * channels]
                index = (kz * 3 + ky) * 3 + kx
                for side in range(2):
                    halves[side, pl.ds(index * half, half)] = value[side * half : (side + 1) * half]
    side = lax.axis_index("gz") % 2
    keep[...] = halves[side]
    send[...] = halves[1 - side].astype(send.dtype)


def input_kernel(even, own, odd, weight, out):
    rows, cols, channels = out.shape
    low, high = sides(even, odd)
    planes = (low, own, high)
    total = None
    for kz in range(3):
        for ky in range(3):
            slab = planes[2 - kz][2 - ky : 2 - ky + rows].reshape(rows * cols, channels)
            term = lax.dot_general(
                slab,
                weight[kz, ky].reshape(3 * channels, channels),
                (((1,), (1,)), ((), ())),
                preferred_element_type=F32,
            )
            total = term if total is None else total + term
    answer = None
    for kx in range(3):
        part = total[:, kx * channels : (kx + 1) * channels].reshape(rows, cols, channels)
        part = shifted(part, kx - 1)
        answer = part if answer is None else answer + part
    out[...] = answer.astype(BF16)


def reversed_bits(code, count):
    place, bit = 0, 1
    while bit < count:
        place = place * 2 + code // bit % 2
        bit *= 2
    return place


def place_kernel(n_gy, *refs):
    blocks, (conv, down) = refs[: 2 * n_gy], refs[2 * n_gy :]
    me = lax.axis_index("gy")
    parity = lax.axis_index("gz") % 2
    half, channels = conv.shape[3:]
    count, deep_channels = down.shape[2:]
    for index, block in enumerate(blocks):
        side = jnp.bitwise_xor(parity, index // n_gy)
        column = jnp.bitwise_xor(me, index % n_gy)
        for k in range(27):
            conv[k, column, side] = block[pl.ds(k * half, half)]
        for wide in range(deep_channels // channels):
            down[side, column, :, pl.ds(wide * channels, channels)] = block[
                pl.ds(27 * half + wide * count, count)
            ]


def swapped(value, axis, code):
    return lax.ppermute(value, axis, [(i, i ^ code) for i in range(lax.axis_size(axis))])


def crossed(value, code_gz, code_gy):
    count = lax.axis_size("gy")
    pairs = [
        (i * count + j, (i ^ code_gz) * count + (j ^ code_gy))
        for i in range(lax.axis_size("gz"))
        for j in range(count)
    ]
    return lax.ppermute(value, ("gz", "gy"), pairs)


def even_pairs(value):
    return swapped(value, "gz", 1)


def odd_pairs(value):
    last = lax.axis_size("gz") - 1
    pairs = [(i + d, i + 1 - d) for i in range(1, last, 2) for d in range(2)]
    return lax.ppermute(value, "gz", pairs)


def exchanged(value, axis):
    return lax.all_to_all(value, axis, split_axis=0, concat_axis=0, tiled=True)


def per_device(
    level_input, pre_activation, conv_weight, down_weight, skip_cotangent, deep_cotangent
):
    n_gz = lax.axis_size("gz")
    n_gy = lax.axis_size("gy")
    _, rows, cols, channels = level_input.shape
    planes, deep_rows, deep_cols, share = deep_cotangent.shape
    deep_channels = down_weight.shape[4]
    parity = lax.axis_index("gz") % 2
    devices = n_gz * n_gy
    part = channels // n_gy
    cells = rows * cols
    deep_cells = deep_rows * deep_cols
    half = part // 2
    down_count = 4 * deep_channels // n_gy
    wire = BF16 if n_gz <= 8 else F32
    shape = jax.ShapeDtypeStruct

    level = level_input.reshape(cells, channels)
    deep = deep_cotangent.reshape(planes, deep_cells, share)
    if share % 16 == 0:
        keep, send = call(
            deep_kernel,
            [shape((planes // 2, share, deep_cells), BF16)] * 2,
            deep,
            scratch=[pltpu.VMEM((planes, share, deep_cells), BF16)],
        )
        code = planes
        held = jnp.stack([keep, swapped(send, "gz", code)], axis=1)
        while code > 2:
            code //= 2
            count = code // 2
            upper = lax.axis_index("gz") // code % 2
            keep = lax.dynamic_slice_in_dim(held, upper * count, count, axis=0)
            send = lax.dynamic_slice_in_dim(held, (1 - upper) * count, count, axis=0)
            held = jnp.concatenate([keep, swapped(send, "gz", code)], axis=1)
        deep_t = [held[0], swapped(held[0], "gz", 1)]
    else:
        deep_t = jnp.repeat(jnp.swapaxes(deep, 1, 2), 2, axis=0)
        deep_t = [exchanged(deep_t, "gz").reshape(deep_channels, deep_cells)]
    level_t = call(
        level_kernel,
        [shape((part, cells), BF16)] * n_gy,
        level,
        scratch=[pltpu.VMEM((n_gy, part, cells), BF16)],
    )
    level_t = [swapped(value, "gy", code) if code else value for code, value in enumerate(level_t)]
    level_t = jnp.stack(level_t)
    even = even_pairs(level_t)
    *deep_t, level_t = lax.optimization_barrier((*deep_t, level_t))
    down_slice = lax.dynamic_index_in_dim(down_weight, parity, 0, keepdims=False)
    grad, down, *others = call(
        lambda *refs: mask_kernel(n_gy, *refs),
        [shape((cells, channels), BF16), shape((down_count, channels), F32)]
        + [shape((down_count, channels), BF16)] * (n_gy - 1),
        pre_activation[0],
        skip_cotangent[0],
        down_slice,
        *deep_t,
        scratch=[
            pltpu.VMEM((deep_channels, deep_cells), BF16),
            pltpu.VMEM((n_gy, 4 * channels // n_gy, deep_channels), F32),
        ],
    )
    shared = [swapped(grad, "gy", code) if code else grad for code in range(n_gy)]
    shared[1], level_t = lax.optimization_barrier((shared[1], level_t))
    odd = odd_pairs(level_t)
    even, *others = lax.optimization_barrier((even, *others))
    for code, value in enumerate(others):
        down = down + swapped(value, "gy", code + 1).astype(F32)
    keep, send, near = call(
        lambda *refs: weight_kernel(n_gy, (rows, cols, channels), *refs),
        (
            shape((27 * half, channels), F32),
            shape((27 * half, channels), wire),
            shape((rows + 2, cols, channels), BF16),
        ),
        even,
        level_t,
        odd,
        *shared,
        scratch=[
            pltpu.VMEM((n_gy * rows + 2, cols, 3 * channels), BF16),
            pltpu.VMEM((n_gy, 3 * part, cells), BF16),
            pltpu.VMEM((2, 27 * half, channels), F32),
        ],
    )
    near_odd, near_even = odd_pairs(near), even_pairs(near)
    def rounded(value):
        return lax.optimization_barrier(value.astype(wire))

    def added(value, other):
        return value.astype(F32) + other.astype(F32)

    cell_total = devices * cells
    down = rounded(down)
    codes = []
    code = n_gz // 2
    while code > 1:
        codes.append(code)
        code //= 2
    send = swapped(send, "gz", 1)
    for index, code in enumerate(codes):
        down_other = swapped(down, "gz", code)
        if index == 0:
            send, down_other = lax.optimization_barrier((send, down_other))
            conv = rounded(keep + send.astype(F32))
        else:
            conv_other = swapped(conv, "gz", codes[index - 1])
            if index == 1:
                tied = (conv_other, down_other, near_odd, near_even)
                conv_other, down_other, near_odd, near_even = lax.optimization_barrier(tied)
            conv = rounded(added(conv, conv_other))
        down = added(down, down_other)
        if index < len(codes) - 1:
            down = rounded(down)
    conv_other = swapped(conv, "gz", codes[-1])
    input_grad = call(
        input_kernel,
        shape((rows, cols, channels), BF16),
        near_even,
        near,
        near_odd,
        conv_weight,
    )
    down = (down * (1 / math.sqrt(cell_total // 8))).astype(BF16)

    def spread(value):
        return [
            value,
            swapped(value, "gy", 2),
            swapped(value, "gz", 1),
            crossed(value, 1, 2),
        ]

    downs = spread(down)
    conv_other, *downs = lax.optimization_barrier((conv_other, *downs))
    conv = (added(conv, conv_other) * (1 / math.sqrt(cell_total))).astype(BF16)
    convs = spread(conv)
    convs[3], input_grad = lax.optimization_barrier((convs[3], input_grad))
    blocks = []
    for pieces in zip(convs, downs):
        block = jnp.concatenate(pieces, axis=0)
        blocks += [block, swapped(block, "gy", 1)]
    conv_grad, down_grad = call(
        lambda *refs: place_kernel(n_gy, *refs),
        (
            shape((27, n_gy, 2, half, channels), BF16),
            shape((2, n_gy, 4 * channels // n_gy, deep_channels), BF16),
        ),
        *blocks,
    )
    return (
        input_grad[None],
        conv_grad.reshape(conv_weight.shape),
        down_grad.reshape(down_weight.shape),
    )


def solution(mesh):
    return jax.shard_map(
        per_device,
        mesh=mesh,
        in_specs=(
            P("gz", "gy", None, None),
            P("gz", "gy", None, None),
            P(),
            P(),
            P("gz", "gy", None, None),
            P(None, "gy", None, "gz"),
        ),
        out_specs=(P("gz", "gy", None, None), P(), P()),
        check_vma=False,
    )
```

```python
import math

import jax
import jax.numpy as jnp
from jax import lax
from jax.experimental import pallas as pl
from jax.experimental.pallas import tpu as pltpu
from jax.sharding import PartitionSpec as P

F32 = jnp.float32
BF16 = jnp.bfloat16
VMEM_LIMIT = 40 * 1024 * 1024


def call(kernel, out_shape, *operands, scratch=()):
    return pl.pallas_call(
        kernel,
        out_shape=out_shape,
        scratch_shapes=list(scratch),
        compiler_params=pltpu.CompilerParams(vmem_limit_bytes=VMEM_LIMIT),
    )(*operands)


def shifted(cells, step):
    if step == 0:
        return cells
    cols = cells.shape[1]
    moved = pltpu.roll(cells, step % cols, 1)
    col = lax.broadcasted_iota(jnp.int32, cells.shape, 1)
    keep = col >= step if step > 0 else col < cols + step
    return jnp.where(keep, moved, 0.0)


def deep_kernel(deep, keep, send, turned):
    planes = deep.shape[0]
    half = planes // 2
    for plane in range(planes):
        turned[plane] = deep[plane].astype(F32).T.astype(BF16)
    upper = lax.axis_index("gz") // planes
    keep[...] = turned[pl.ds(upper * half, half)]
    send[...] = turned[pl.ds((1 - upper) * half, half)]


def level_kernel(level, *rest):
    outs, level_t = rest[:-1], rest[-1]
    turned = level[...].astype(F32).T.astype(BF16)
    part = level_t.shape[1]
    for owner in range(len(outs)):
        level_t[owner] = turned[owner * part : (owner + 1) * part]
    me = lax.axis_index("gy")
    for code, out in enumerate(outs):
        out[...] = level_t[jnp.bitwise_xor(me, code)]


def mask_kernel(n_gy, pre, skip, weight, *rest):
    deeps, rest = rest[: -n_gy - 3], rest[-n_gy - 3 :]
    grad_out, kept, *outs, deep_t, down_all = rest
    if len(deeps) > 1:
        count, share = deeps[0].shape[:2]
        me = lax.axis_index("gz")
        for place in range(2 * count):
            owner = jnp.bitwise_xor(me, reversed_bits(place, 2 * count))
            first = pl.multiple_of(owner * share, share)
            deep_t[pl.ds(first, share)] = deeps[place // count][place % count]
    else:
        deep_t[...] = deeps[0][...]
    rows, cols, channels = pre.shape
    half = rows // 2
    deep_cols = cols // 2
    cells = half * cols
    deep_cells = half * deep_cols
    wide = lax.broadcasted_iota(jnp.int32, (deep_cells, cells), 1) // 2
    deep = lax.broadcasted_iota(jnp.int32, (deep_cells, cells), 0)
    repeat = (wide == deep).astype(BF16)
    spread = jnp.dot(deep_t[...], repeat, preferred_element_type=F32).astype(BF16)
    col = lax.broadcasted_iota(jnp.int32, (cells, channels), 0) % 2
    count = down_all.shape[1]
    for b in range(2):
        parts = [
            lax.dot_general(
                spread, weight[b, c], (((0,), (1,)), ((), ())), preferred_element_type=F32
            )
            for c in range(2)
        ]
        part = jnp.where(col == 0, parts[0], parts[1]).reshape(half, cols, channels)
        for y in range(half):
            row = 2 * y + b
            pre_row = pre[row].astype(F32)
            total = part[y] + skip[row].astype(F32)
            grad = jnp.where(pre_row > 0, total, 0.0).astype(BF16)
            grad_out[pl.ds(row * cols, cols)] = grad
        hidden = jnp.concatenate(
            [jnp.maximum(pre[2 * y + b].astype(F32), 0.0) for y in range(half)], axis=0
        )
        for c in range(2):
            one = jnp.where(col == c, hidden, 0.0).astype(BF16)
            down = lax.dot_general(
                one, spread, (((0,), (1,)), ((), ())), preferred_element_type=F32
            )
            for first, owner, inner, take in segments(channels, count, channels, (b * 2 + c) * channels):
                down_all[owner, pl.ds(inner, take)] = down[first : first + take]
    me = lax.axis_index("gy")
    for code, out in enumerate([kept, *outs]):
        owner = jnp.bitwise_xor(me, code)
        for side in range(down_all.shape[2] // channels):
            out[pl.ds(side * count, count)] = down_all[
                owner, :, pl.ds(side * channels, channels)
            ].astype(out.dtype)


def segments(rows, piece, unit, base=0):
    row = 0
    while row < rows:
        take = min(rows - row, unit - row % unit, piece - (base + row) % piece)
        yield row, (base + row) // piece, (base + row) % piece, take
        row += take


def sides(even, odd):
    upper = lax.axis_index("gz") % 2 == 0
    low = jnp.where(upper, odd[...].astype(F32), even[...].astype(F32)).astype(BF16)
    high = jnp.where(upper, even[...].astype(F32), odd[...].astype(F32)).astype(BF16)
    return low, high


def weight_kernel(n_gy, shape, *refs):
    even, own, odd = refs[:3]
    shared = refs[3 : 3 + n_gy]
    keep, send, near, wide, level, halves = refs[3 + n_gy :]
    rows, cols, channels = shape
    part = own.shape[1]
    cells = rows * cols
    half = part // 2
    rows_all = n_gy * rows
    me = lax.axis_index("gy")
    low, high = sides(even, odd)
    for edge in (0, rows_all + 1):
        wide[edge] = jnp.zeros(wide.shape[1:], BF16)
    for code in range(n_gy):
        owner = jnp.bitwise_xor(me, code)
        grads = shared[code][pl.ds(0, cells)].reshape(rows, cols, channels).astype(F32)
        for kx in range(3):
            wide[pl.ds(1 + owner * rows, rows), :, pl.ds(kx * channels, channels)] = shifted(
                grads, kx - 1
            ).astype(BF16)
        for kz, plane in enumerate((low[code], own[code], high[code])):
            level[owner, pl.ds(kz * part, part)] = plane
    near[...] = wide[pl.ds(me * rows, rows + 2), :, pl.ds(channels, channels)]
    for ky in range(3):
        total = None
        for owner in range(n_gy):
            slab = wide[pl.ds(2 - ky + owner * rows, rows)].reshape(cells, 3 * channels)
            term = jnp.dot(level[owner], slab, preferred_element_type=F32)
            total = term if total is None else total + term
        for kz in range(3):
            for kx in range(3):
                value = total[kz * part : (kz + 1) * part, kx * channels : (kx + 1) * channels]
                index = (kz * 3 + ky) * 3 + kx
                for side in range(2):
                    halves[side, pl.ds(index * half, half)] = value[side * half : (side + 1) * half]
    side = lax.axis_index("gz") % 2
    keep[...] = halves[side]
    send[...] = halves[1 - side].astype(send.dtype)


def input_kernel(even, own, odd, weight, out):
    rows, cols, channels = out.shape
    low, high = sides(even, odd)
    planes = (low, own, high)
    total = None
    for kz in range(3):
        for ky in range(3):
            slab = planes[2 - kz][2 - ky : 2 - ky + rows].reshape(rows * cols, channels)
            term = lax.dot_general(
                slab,
                weight[kz, ky].reshape(3 * channels, channels),
                (((1,), (1,)), ((), ())),
                preferred_element_type=F32,
            )
            total = term if total is None else total + term
    answer = None
    for kx in range(3):
        part = total[:, kx * channels : (kx + 1) * channels].reshape(rows, cols, channels)
        part = shifted(part, kx - 1)
        answer = part if answer is None else answer + part
    out[...] = answer.astype(BF16)


def reversed_bits(code, count):
    place, bit = 0, 1
    while bit < count:
        place = place * 2 + code // bit % 2
        bit *= 2
    return place


def place_kernel(n_gy, *refs):
    blocks, (conv, down) = refs[: 2 * n_gy], refs[2 * n_gy :]
    me = lax.axis_index("gy")
    parity = lax.axis_index("gz") % 2
    half, channels = conv.shape[3:]
    count, deep_channels = down.shape[2:]
    for index, block in enumerate(blocks):
        side = jnp.bitwise_xor(parity, index // n_gy)
        column = jnp.bitwise_xor(me, index % n_gy)
        for k in range(27):
            conv[k, column, side] = block[pl.ds(k * half, half)]
        for wide in range(deep_channels // channels):
            down[side, column, :, pl.ds(wide * channels, channels)] = block[
                pl.ds(27 * half + wide * count, count)
            ]


def swapped(value, axis, code):
    return lax.ppermute(value, axis, [(i, i ^ code) for i in range(lax.axis_size(axis))])


def crossed(value, code_gz, code_gy):
    count = lax.axis_size("gy")
    pairs = [
        (i * count + j, (i ^ code_gz) * count + (j ^ code_gy))
        for i in range(lax.axis_size("gz"))
        for j in range(count)
    ]
    return lax.ppermute(value, ("gz", "gy"), pairs)


def even_pairs(value):
    return swapped(value, "gz", 1)


def odd_pairs(value):
    last = lax.axis_size("gz") - 1
    pairs = [(i + d, i + 1 - d) for i in range(1, last, 2) for d in range(2)]
    return lax.ppermute(value, "gz", pairs)


def exchanged(value, axis):
    return lax.all_to_all(value, axis, split_axis=0, concat_axis=0, tiled=True)


def per_device(
    level_input, pre_activation, conv_weight, down_weight, skip_cotangent, deep_cotangent
):
    n_gz = lax.axis_size("gz")
    n_gy = lax.axis_size("gy")
    _, rows, cols, channels = level_input.shape
    planes, deep_rows, deep_cols, share = deep_cotangent.shape
    deep_channels = down_weight.shape[4]
    parity = lax.axis_index("gz") % 2
    devices = n_gz * n_gy
    part = channels // n_gy
    cells = rows * cols
    deep_cells = deep_rows * deep_cols
    half = part // 2
    down_count = 4 * deep_channels // n_gy
    wire = BF16 if n_gz <= 8 else F32
    shape = jax.ShapeDtypeStruct

    level = level_input.reshape(cells, channels)
    deep = deep_cotangent.reshape(planes, deep_cells, share)
    if share % 16 == 0:
        keep, send = call(
            deep_kernel,
            [shape((planes // 2, share, deep_cells), BF16)] * 2,
            deep,
            scratch=[pltpu.VMEM((planes, share, deep_cells), BF16)],
        )
        code = planes
        held = jnp.stack([keep, swapped(send, "gz", code)], axis=1)
        while code > 2:
            code //= 2
            count = code // 2
            upper = lax.axis_index("gz") // code % 2
            keep = lax.dynamic_slice_in_dim(held, upper * count, count, axis=0)
            send = lax.dynamic_slice_in_dim(held, (1 - upper) * count, count, axis=0)
            held = jnp.concatenate([keep, swapped(send, "gz", code)], axis=1)
        deep_t = [held[0], swapped(held[0], "gz", 1)]
    else:
        deep_t = jnp.repeat(jnp.swapaxes(deep, 1, 2), 2, axis=0)
        deep_t = [exchanged(deep_t, "gz").reshape(deep_channels, deep_cells)]
    level_t = call(
        level_kernel,
        [shape((part, cells), BF16)] * n_gy,
        level,
        scratch=[pltpu.VMEM((n_gy, part, cells), BF16)],
    )
    level_t = [swapped(value, "gy", code) if code else value for code, value in enumerate(level_t)]
    level_t = jnp.stack(level_t)
    even = even_pairs(level_t)
    *deep_t, level_t = lax.optimization_barrier((*deep_t, level_t))
    down_slice = lax.dynamic_index_in_dim(down_weight, parity, 0, keepdims=False)
    grad, down, *others = call(
        lambda *refs: mask_kernel(n_gy, *refs),
        [shape((cells, channels), BF16), shape((down_count, channels), F32)]
        + [shape((down_count, channels), BF16)] * (n_gy - 1),
        pre_activation[0],
        skip_cotangent[0],
        down_slice,
        *deep_t,
        scratch=[
            pltpu.VMEM((deep_channels, deep_cells), BF16),
            pltpu.VMEM((n_gy, 4 * channels // n_gy, deep_channels), F32),
        ],
    )
    shared = [swapped(grad, "gy", code) if code else grad for code in range(n_gy)]
    shared[1], level_t = lax.optimization_barrier((shared[1], level_t))
    odd = odd_pairs(level_t)
    even, *others = lax.optimization_barrier((even, *others))
    for code, value in enumerate(others):
        down = down + swapped(value, "gy", code + 1).astype(F32)
    keep, send, near = call(
        lambda *refs: weight_kernel(n_gy, (rows, cols, channels), *refs),
        (
            shape((27 * half, channels), F32),
            shape((27 * half, channels), wire),
            shape((rows + 2, cols, channels), BF16),
        ),
        even,
        level_t,
        odd,
        *shared,
        scratch=[
            pltpu.VMEM((n_gy * rows + 2, cols, 3 * channels), BF16),
            pltpu.VMEM((n_gy, 3 * part, cells), BF16),
            pltpu.VMEM((2, 27 * half, channels), F32),
        ],
    )
    near_odd = odd_pairs(near)
    def rounded(value):
        return lax.optimization_barrier(value.astype(wire))

    def added(value, other):
        return value.astype(F32) + other.astype(F32)

    cell_total = devices * cells
    down = rounded(down)
    codes = []
    code = n_gz // 2
    while code > 1:
        codes.append(code)
        code //= 2
    send = swapped(send, "gz", 1)
    for index, code in enumerate(codes):
        down_other = swapped(down, "gz", code)
        if index == 0:
            send, down_other = lax.optimization_barrier((send, down_other))
            conv = (keep + send.astype(F32)).astype(wire)
            conv, late = lax.optimization_barrier((conv, near))
            cut = late.shape[0] // 2
            evens = even_pairs(late[:cut]), even_pairs(late[cut:])
        else:
            conv_other = swapped(conv, "gz", codes[index - 1])
            if index == 1:
                tied = (conv_other, down_other, near_odd, *evens)
                conv_other, down_other, near_odd, *evens = lax.optimization_barrier(tied)
            conv = rounded(added(conv, conv_other))
        down = added(down, down_other)
        if index < len(codes) - 1:
            down = rounded(down)
    conv_other = swapped(conv, "gz", codes[-1])
    input_grad = call(
        input_kernel,
        shape((rows, cols, channels), BF16),
        jnp.concatenate(evens, axis=0),
        near,
        near_odd,
        conv_weight,
    )
    conv_other, input_grad = lax.optimization_barrier((conv_other, input_grad))
    conv = added(conv, conv_other) * (1 / math.sqrt(cell_total))
    down = down * (1 / math.sqrt(cell_total // 8))
    total = jnp.concatenate([conv.astype(BF16), down.astype(BF16)], axis=0)
    if n_gy == 4:
        lines = [
            [total, swapped(total, "gy", 2)],
            [swapped(total, "gz", 1), crossed(total, 1, 2)],
        ]
        blocks = []
        for near_block, far_block in lines:
            blocks += [near_block, swapped(near_block, "gy", 1)]
            blocks += [far_block, swapped(far_block, "gy", 1)]
    else:
        blocks = [
            swapped(block, "gy", code) if code else block
            for block in (total, swapped(total, "gz", 1))
            for code in range(n_gy)
        ]
    conv_grad, down_grad = call(
        lambda *refs: place_kernel(n_gy, *refs),
        (
            shape((27, n_gy, 2, half, channels), BF16),
            shape((2, n_gy, 4 * channels // n_gy, deep_channels), BF16),
        ),
        *blocks,
    )
    return (
        input_grad[None],
        conv_grad.reshape(conv_weight.shape),
        down_grad.reshape(down_weight.shape),
    )


def solution(mesh):
    return jax.shard_map(
        per_device,
        mesh=mesh,
        in_specs=(
            P("gz", "gy", None, None),
            P("gz", "gy", None, None),
            P(),
            P(),
            P("gz", "gy", None, None),
            P(None, "gy", None, "gz"),
        ),
        out_specs=(P("gz", "gy", None, None), P(), P()),
        check_vma=False,
    )
```

```python
import math

import jax
import jax.numpy as jnp
from jax import lax
from jax.experimental import pallas as pl
from jax.experimental.pallas import tpu as pltpu
from jax.sharding import PartitionSpec as P

F32 = jnp.float32
BF16 = jnp.bfloat16
VMEM_LIMIT = 40 * 1024 * 1024


def call(kernel, out_shape, *operands, scratch=()):
    return pl.pallas_call(
        kernel,
        out_shape=out_shape,
        scratch_shapes=list(scratch),
        compiler_params=pltpu.CompilerParams(vmem_limit_bytes=VMEM_LIMIT),
    )(*operands)


def shifted(cells, step):
    if step == 0:
        return cells
    cols = cells.shape[1]
    moved = pltpu.roll(cells, step % cols, 1)
    col = lax.broadcasted_iota(jnp.int32, cells.shape, 1)
    keep = col >= step if step > 0 else col < cols + step
    return jnp.where(keep, moved, 0.0)


def deep_kernel(deep, keep, send, turned):
    planes = deep.shape[0]
    half = planes // 2
    for plane in range(planes):
        turned[plane] = deep[plane].astype(F32).T.astype(BF16)
    upper = lax.axis_index("gz") // planes
    keep[...] = turned[pl.ds(upper * half, half)]
    send[...] = turned[pl.ds((1 - upper) * half, half)]


def level_kernel(level, *rest):
    outs, level_t = rest[:-1], rest[-1]
    turned = level[...].astype(F32).T.astype(BF16)
    part = level_t.shape[1]
    for owner in range(len(outs)):
        level_t[owner] = turned[owner * part : (owner + 1) * part]
    me = lax.axis_index("gy")
    for code, out in enumerate(outs):
        out[...] = level_t[jnp.bitwise_xor(me, code)]


def mask_kernel(n_gy, pre, skip, weight, *rest):
    deeps, rest = rest[: -n_gy - 3], rest[-n_gy - 3 :]
    grad_out, kept, *outs, deep_t, down_all = rest
    if len(deeps) > 1:
        count, share = deeps[0].shape[:2]
        me = lax.axis_index("gz")
        for place in range(2 * count):
            owner = jnp.bitwise_xor(me, reversed_bits(place, 2 * count))
            first = pl.multiple_of(owner * share, share)
            deep_t[pl.ds(first, share)] = deeps[place // count][place % count]
    else:
        deep_t[...] = deeps[0][...]
    rows, cols, channels = pre.shape
    half = rows // 2
    deep_cols = cols // 2
    cells = half * cols
    deep_cells = half * deep_cols
    wide = lax.broadcasted_iota(jnp.int32, (deep_cells, cells), 1) // 2
    deep = lax.broadcasted_iota(jnp.int32, (deep_cells, cells), 0)
    repeat = (wide == deep).astype(BF16)
    spread = jnp.dot(deep_t[...], repeat, preferred_element_type=F32).astype(BF16)
    col = lax.broadcasted_iota(jnp.int32, (cells, channels), 0) % 2
    count = down_all.shape[1]
    for b in range(2):
        parts = [
            lax.dot_general(
                spread, weight[b, c], (((0,), (1,)), ((), ())), preferred_element_type=F32
            )
            for c in range(2)
        ]
        part = jnp.where(col == 0, parts[0], parts[1]).reshape(half, cols, channels)
        for y in range(half):
            row = 2 * y + b
            pre_row = pre[row].astype(F32)
            total = part[y] + skip[row].astype(F32)
            grad = jnp.where(pre_row > 0, total, 0.0).astype(BF16)
            grad_out[pl.ds(row * cols, cols)] = grad
        hidden = jnp.concatenate(
            [jnp.maximum(pre[2 * y + b].astype(F32), 0.0) for y in range(half)], axis=0
        )
        for c in range(2):
            one = jnp.where(col == c, hidden, 0.0).astype(BF16)
            down = lax.dot_general(
                one, spread, (((0,), (1,)), ((), ())), preferred_element_type=F32
            )
            for first, owner, inner, take in segments(channels, count, channels, (b * 2 + c) * channels):
                down_all[owner, pl.ds(inner, take)] = down[first : first + take]
    me = lax.axis_index("gy")
    for code, out in enumerate([kept, *outs]):
        owner = jnp.bitwise_xor(me, code)
        for side in range(down_all.shape[2] // channels):
            out[pl.ds(side * count, count)] = down_all[
                owner, :, pl.ds(side * channels, channels)
            ].astype(out.dtype)


def segments(rows, piece, unit, base=0):
    row = 0
    while row < rows:
        take = min(rows - row, unit - row % unit, piece - (base + row) % piece)
        yield row, (base + row) // piece, (base + row) % piece, take
        row += take


def sides(even, odd):
    upper = lax.axis_index("gz") % 2 == 0
    low = jnp.where(upper, odd[...].astype(F32), even[...].astype(F32)).astype(BF16)
    high = jnp.where(upper, even[...].astype(F32), odd[...].astype(F32)).astype(BF16)
    return low, high


def weight_kernel(n_gy, shape, *refs):
    even, own, odd = refs[:3]
    shared = refs[3 : 3 + n_gy]
    keep, send, near, wide, level, halves = refs[3 + n_gy :]
    rows, cols, channels = shape
    part = own.shape[1]
    cells = rows * cols
    half = part // 2
    rows_all = n_gy * rows
    me = lax.axis_index("gy")
    low, high = sides(even, odd)
    for edge in (0, rows_all + 1):
        wide[edge] = jnp.zeros(wide.shape[1:], BF16)
    for code in range(n_gy):
        owner = jnp.bitwise_xor(me, code)
        grads = shared[code][pl.ds(0, cells)].reshape(rows, cols, channels).astype(F32)
        for kx in range(3):
            wide[pl.ds(1 + owner * rows, rows), :, pl.ds(kx * channels, channels)] = shifted(
                grads, kx - 1
            ).astype(BF16)
        for kz, plane in enumerate((low[code], own[code], high[code])):
            level[owner, pl.ds(kz * part, part)] = plane
    near[...] = wide[pl.ds(me * rows, rows + 2), :, pl.ds(channels, channels)]
    for ky in range(3):
        total = None
        for owner in range(n_gy):
            slab = wide[pl.ds(2 - ky + owner * rows, rows)].reshape(cells, 3 * channels)
            term = jnp.dot(level[owner], slab, preferred_element_type=F32)
            total = term if total is None else total + term
        for kz in range(3):
            for kx in range(3):
                value = total[kz * part : (kz + 1) * part, kx * channels : (kx + 1) * channels]
                index = (kz * 3 + ky) * 3 + kx
                for side in range(2):
                    halves[side, pl.ds(index * half, half)] = value[side * half : (side + 1) * half]
    side = lax.axis_index("gz") % 2
    keep[...] = halves[side]
    send[...] = halves[1 - side].astype(send.dtype)


def input_kernel(even, own, odd, weight, out):
    rows, cols, channels = out.shape
    low, high = sides(even, odd)
    planes = (low, own, high)
    total = None
    for kz in range(3):
        for ky in range(3):
            slab = planes[2 - kz][2 - ky : 2 - ky + rows].reshape(rows * cols, channels)
            term = lax.dot_general(
                slab,
                weight[kz, ky].reshape(3 * channels, channels),
                (((1,), (1,)), ((), ())),
                preferred_element_type=F32,
            )
            total = term if total is None else total + term
    answer = None
    for kx in range(3):
        part = total[:, kx * channels : (kx + 1) * channels].reshape(rows, cols, channels)
        part = shifted(part, kx - 1)
        answer = part if answer is None else answer + part
    out[...] = answer.astype(BF16)


def reversed_bits(code, count):
    place, bit = 0, 1
    while bit < count:
        place = place * 2 + code // bit % 2
        bit *= 2
    return place


def place_kernel(n_gy, *refs):
    blocks, (conv, down) = refs[: 2 * n_gy], refs[2 * n_gy :]
    me = lax.axis_index("gy")
    parity = lax.axis_index("gz") % 2
    half, channels = conv.shape[3:]
    count, deep_channels = down.shape[2:]
    for index, block in enumerate(blocks):
        side = jnp.bitwise_xor(parity, index // n_gy)
        column = jnp.bitwise_xor(me, index % n_gy)
        for k in range(27):
            conv[k, column, side] = block[pl.ds(k * half, half)]
        for wide in range(deep_channels // channels):
            down[side, column, :, pl.ds(wide * channels, channels)] = block[
                pl.ds(27 * half + wide * count, count)
            ]


def swapped(value, axis, code):
    return lax.ppermute(value, axis, [(i, i ^ code) for i in range(lax.axis_size(axis))])


def crossed(value, code_gz, code_gy):
    count = lax.axis_size("gy")
    pairs = [
        (i * count + j, (i ^ code_gz) * count + (j ^ code_gy))
        for i in range(lax.axis_size("gz"))
        for j in range(count)
    ]
    return lax.ppermute(value, ("gz", "gy"), pairs)


def even_pairs(value):
    return swapped(value, "gz", 1)


def odd_pairs(value):
    last = lax.axis_size("gz") - 1
    pairs = [(i + d, i + 1 - d) for i in range(1, last, 2) for d in range(2)]
    return lax.ppermute(value, "gz", pairs)


def exchanged(value, axis):
    return lax.all_to_all(value, axis, split_axis=0, concat_axis=0, tiled=True)


def per_device(
    level_input, pre_activation, conv_weight, down_weight, skip_cotangent, deep_cotangent
):
    n_gz = lax.axis_size("gz")
    n_gy = lax.axis_size("gy")
    _, rows, cols, channels = level_input.shape
    planes, deep_rows, deep_cols, share = deep_cotangent.shape
    deep_channels = down_weight.shape[4]
    parity = lax.axis_index("gz") % 2
    devices = n_gz * n_gy
    part = channels // n_gy
    cells = rows * cols
    deep_cells = deep_rows * deep_cols
    half = part // 2
    down_count = 4 * deep_channels // n_gy
    wire = BF16 if n_gz <= 8 else F32
    shape = jax.ShapeDtypeStruct

    level = level_input.reshape(cells, channels)
    deep = deep_cotangent.reshape(planes, deep_cells, share)
    if share % 16 == 0:
        keep, send = call(
            deep_kernel,
            [shape((planes // 2, share, deep_cells), BF16)] * 2,
            deep,
            scratch=[pltpu.VMEM((planes, share, deep_cells), BF16)],
        )
        code = planes
        held = jnp.stack([keep, swapped(send, "gz", code)], axis=1)
        while code > 2:
            code //= 2
            count = code // 2
            upper = lax.axis_index("gz") // code % 2
            keep = lax.dynamic_slice_in_dim(held, upper * count, count, axis=0)
            send = lax.dynamic_slice_in_dim(held, (1 - upper) * count, count, axis=0)
            held = jnp.concatenate([keep, swapped(send, "gz", code)], axis=1)
        deep_t = [held[0], swapped(held[0], "gz", 1)]
    else:
        deep_t = jnp.repeat(jnp.swapaxes(deep, 1, 2), 2, axis=0)
        deep_t = [exchanged(deep_t, "gz").reshape(deep_channels, deep_cells)]
    level_t = call(
        level_kernel,
        [shape((part, cells), BF16)] * n_gy,
        level,
        scratch=[pltpu.VMEM((n_gy, part, cells), BF16)],
    )
    level_t = [swapped(value, "gy", code) if code else value for code, value in enumerate(level_t)]
    level_t = jnp.stack(level_t)
    even = even_pairs(level_t)
    *deep_t, level_t = lax.optimization_barrier((*deep_t, level_t))
    down_slice = lax.dynamic_index_in_dim(down_weight, parity, 0, keepdims=False)
    grad, down, *others = call(
        lambda *refs: mask_kernel(n_gy, *refs),
        [shape((cells, channels), BF16), shape((down_count, channels), F32)]
        + [shape((down_count, channels), BF16)] * (n_gy - 1),
        pre_activation[0],
        skip_cotangent[0],
        down_slice,
        *deep_t,
        scratch=[
            pltpu.VMEM((deep_channels, deep_cells), BF16),
            pltpu.VMEM((n_gy, 4 * channels // n_gy, deep_channels), F32),
        ],
    )
    shared = [swapped(grad, "gy", code) if code else grad for code in range(n_gy)]
    shared[1], level_t = lax.optimization_barrier((shared[1], level_t))
    odd = odd_pairs(level_t)
    even, *others = lax.optimization_barrier((even, *others))
    for code, value in enumerate(others):
        down = down + swapped(value, "gy", code + 1).astype(F32)
    keep, send, near = call(
        lambda *refs: weight_kernel(n_gy, (rows, cols, channels), *refs),
        (
            shape((27 * half, channels), F32),
            shape((27 * half, channels), wire),
            shape((rows + 2, cols, channels), BF16),
        ),
        even,
        level_t,
        odd,
        *shared,
        scratch=[
            pltpu.VMEM((n_gy * rows + 2, cols, 3 * channels), BF16),
            pltpu.VMEM((n_gy, 3 * part, cells), BF16),
            pltpu.VMEM((2, 27 * half, channels), F32),
        ],
    )
    near_odd = odd_pairs(near)
    def rounded(value):
        return lax.optimization_barrier(value.astype(wire))

    def added(value, other):
        return value.astype(F32) + other.astype(F32)

    cell_total = devices * cells
    down = rounded(down)
    codes = []
    code = n_gz // 2
    while code > 1:
        codes.append(code)
        code //= 2
    send = swapped(send, "gz", 1)
    for index, code in enumerate(codes):
        down_other = swapped(down, "gz", code)
        if index == 0:
            conv = (keep + send.astype(F32)).astype(wire)
            conv, late = lax.optimization_barrier((conv, near))
            cut = late.shape[0] // 2
            evens = even_pairs(late[:cut]), even_pairs(late[cut:])
        else:
            conv_other = swapped(conv, "gz", codes[index - 1])
            if index == 1:
                tied = (conv_other, down_other, near_odd, *evens)
                conv_other, down_other, near_odd, *evens = lax.optimization_barrier(tied)
            conv = rounded(added(conv, conv_other))
        down = added(down, down_other)
        if index < len(codes) - 1:
            down = rounded(down)
    conv_other = swapped(conv, "gz", codes[-1])
    input_grad = call(
        input_kernel,
        shape((rows, cols, channels), BF16),
        jnp.concatenate(evens, axis=0),
        near,
        near_odd,
        conv_weight,
    )
    conv_other, input_grad = lax.optimization_barrier((conv_other, input_grad))
    conv = added(conv, conv_other) * (1 / math.sqrt(cell_total))
    down = down * (1 / math.sqrt(cell_total // 8))
    total = jnp.concatenate([conv.astype(BF16), down.astype(BF16)], axis=0)
    if n_gy == 4:
        lines = [
            [total, swapped(total, "gy", 2)],
            [swapped(total, "gz", 1), crossed(total, 1, 2)],
        ]
        blocks = []
        for near_block, far_block in lines:
            blocks += [near_block, swapped(near_block, "gy", 1)]
            blocks += [far_block, swapped(far_block, "gy", 1)]
    else:
        blocks = [
            swapped(block, "gy", code) if code else block
            for block in (total, swapped(total, "gz", 1))
            for code in range(n_gy)
        ]
    conv_grad, down_grad = call(
        lambda *refs: place_kernel(n_gy, *refs),
        (
            shape((27, n_gy, 2, half, channels), BF16),
            shape((2, n_gy, 4 * channels // n_gy, deep_channels), BF16),
        ),
        *blocks,
    )
    return (
        input_grad[None],
        conv_grad.reshape(conv_weight.shape),
        down_grad.reshape(down_weight.shape),
    )


def solution(mesh):
    return jax.shard_map(
        per_device,
        mesh=mesh,
        in_specs=(
            P("gz", "gy", None, None),
            P("gz", "gy", None, None),
            P(),
            P(),
            P("gz", "gy", None, None),
            P(None, "gy", None, "gz"),
        ),
        out_specs=(P("gz", "gy", None, None), P(), P()),
        check_vma=False,
    )
```

```python
import math

import jax
import jax.numpy as jnp
from jax import lax
from jax.experimental import pallas as pl
from jax.experimental.pallas import tpu as pltpu
from jax.sharding import PartitionSpec as P

F32 = jnp.float32
BF16 = jnp.bfloat16
VMEM_LIMIT = 40 * 1024 * 1024


def call(kernel, out_shape, *operands, scratch=()):
    return pl.pallas_call(
        kernel,
        out_shape=out_shape,
        scratch_shapes=list(scratch),
        compiler_params=pltpu.CompilerParams(vmem_limit_bytes=VMEM_LIMIT),
    )(*operands)


def shifted(cells, step):
    if step == 0:
        return cells
    cols = cells.shape[1]
    moved = pltpu.roll(cells, step % cols, 1)
    col = lax.broadcasted_iota(jnp.int32, cells.shape, 1)
    keep = col >= step if step > 0 else col < cols + step
    return jnp.where(keep, moved, 0.0)


def deep_kernel(deep, keep, send, turned):
    planes = deep.shape[0]
    half = planes // 2
    for plane in range(planes):
        turned[plane] = deep[plane].astype(F32).T.astype(BF16)
    upper = lax.axis_index("gz") // planes
    keep[...] = turned[pl.ds(upper * half, half)]
    send[...] = turned[pl.ds((1 - upper) * half, half)]


def level_kernel(level, *rest):
    outs, level_t = rest[:-1], rest[-1]
    turned = level[...].astype(F32).T.astype(BF16)
    part = level_t.shape[1]
    for owner in range(len(outs)):
        level_t[owner] = turned[owner * part : (owner + 1) * part]
    me = lax.axis_index("gy")
    for code, out in enumerate(outs):
        out[...] = level_t[jnp.bitwise_xor(me, code)]


def mask_kernel(n_gy, pre, skip, weight, *rest):
    deeps, rest = rest[: -n_gy - 3], rest[-n_gy - 3 :]
    grad_out, kept, *outs, deep_t, down_all = rest
    if len(deeps) > 1:
        count, share = deeps[0].shape[:2]
        me = lax.axis_index("gz")
        for place in range(2 * count):
            owner = jnp.bitwise_xor(me, reversed_bits(place, 2 * count))
            first = pl.multiple_of(owner * share, share)
            deep_t[pl.ds(first, share)] = deeps[place // count][place % count]
    else:
        deep_t[...] = deeps[0][...]
    rows, cols, channels = pre.shape
    half = rows // 2
    deep_cols = cols // 2
    cells = half * cols
    deep_cells = half * deep_cols
    wide = lax.broadcasted_iota(jnp.int32, (deep_cells, cells), 1) // 2
    deep = lax.broadcasted_iota(jnp.int32, (deep_cells, cells), 0)
    repeat = (wide == deep).astype(BF16)
    spread = jnp.dot(deep_t[...], repeat, preferred_element_type=F32).astype(BF16)
    col = lax.broadcasted_iota(jnp.int32, (cells, channels), 0) % 2
    count = down_all.shape[1]
    for b in range(2):
        parts = [
            lax.dot_general(
                spread, weight[b, c], (((0,), (1,)), ((), ())), preferred_element_type=F32
            )
            for c in range(2)
        ]
        part = jnp.where(col == 0, parts[0], parts[1]).reshape(half, cols, channels)
        for y in range(half):
            row = 2 * y + b
            pre_row = pre[row].astype(F32)
            total = part[y] + skip[row].astype(F32)
            grad = jnp.where(pre_row > 0, total, 0.0).astype(BF16)
            grad_out[pl.ds(row * cols, cols)] = grad
        hidden = jnp.concatenate(
            [jnp.maximum(pre[2 * y + b].astype(F32), 0.0) for y in range(half)], axis=0
        )
        for c in range(2):
            one = jnp.where(col == c, hidden, 0.0).astype(BF16)
            down = lax.dot_general(
                one, spread, (((0,), (1,)), ((), ())), preferred_element_type=F32
            )
            for first, owner, inner, take in segments(channels, count, channels, (b * 2 + c) * channels):
                down_all[owner, pl.ds(inner, take)] = down[first : first + take]
    me = lax.axis_index("gy")
    for code, out in enumerate([kept, *outs]):
        owner = jnp.bitwise_xor(me, code)
        for side in range(down_all.shape[2] // channels):
            out[pl.ds(side * count, count)] = down_all[
                owner, :, pl.ds(side * channels, channels)
            ].astype(out.dtype)


def segments(rows, piece, unit, base=0):
    row = 0
    while row < rows:
        take = min(rows - row, unit - row % unit, piece - (base + row) % piece)
        yield row, (base + row) // piece, (base + row) % piece, take
        row += take


def sides(even, odd):
    upper = lax.axis_index("gz") % 2 == 0
    low = jnp.where(upper, odd[...].astype(F32), even[...].astype(F32)).astype(BF16)
    high = jnp.where(upper, even[...].astype(F32), odd[...].astype(F32)).astype(BF16)
    return low, high


def weight_kernel(n_gy, shape, *refs):
    even, own, odd = refs[:3]
    shared = refs[3 : 3 + n_gy]
    keep, send, near, wide, level, halves = refs[3 + n_gy :]
    rows, cols, channels = shape
    part = own.shape[1]
    cells = rows * cols
    half = part // 2
    rows_all = n_gy * rows
    me = lax.axis_index("gy")
    low, high = sides(even, odd)
    for edge in (0, rows_all + 1):
        wide[edge] = jnp.zeros(wide.shape[1:], BF16)
    for code in range(n_gy):
        owner = jnp.bitwise_xor(me, code)
        grads = shared[code][pl.ds(0, cells)].reshape(rows, cols, channels).astype(F32)
        for kx in range(3):
            wide[pl.ds(1 + owner * rows, rows), :, pl.ds(kx * channels, channels)] = shifted(
                grads, kx - 1
            ).astype(BF16)
        for kz, plane in enumerate((low[code], own[code], high[code])):
            level[owner, pl.ds(kz * part, part)] = plane
    near[...] = wide[pl.ds(me * rows, rows + 2), :, pl.ds(channels, channels)]
    for ky in range(3):
        total = None
        for owner in range(n_gy):
            slab = wide[pl.ds(2 - ky + owner * rows, rows)].reshape(cells, 3 * channels)
            term = jnp.dot(level[owner], slab, preferred_element_type=F32)
            total = term if total is None else total + term
        for kz in range(3):
            for kx in range(3):
                value = total[kz * part : (kz + 1) * part, kx * channels : (kx + 1) * channels]
                index = (kz * 3 + ky) * 3 + kx
                for side in range(2):
                    halves[side, pl.ds(index * half, half)] = value[side * half : (side + 1) * half]
    side = lax.axis_index("gz") % 2
    keep[...] = halves[side]
    send[...] = halves[1 - side].astype(send.dtype)


def input_kernel(even, own, odd, weight, out):
    rows, cols, channels = out.shape
    low, high = sides(even, odd)
    planes = (low, own, high)
    total = None
    for kz in range(3):
        for ky in range(3):
            slab = planes[2 - kz][2 - ky : 2 - ky + rows].reshape(rows * cols, channels)
            term = lax.dot_general(
                slab,
                weight[kz, ky].reshape(3 * channels, channels),
                (((1,), (1,)), ((), ())),
                preferred_element_type=F32,
            )
            total = term if total is None else total + term
    answer = None
    for kx in range(3):
        part = total[:, kx * channels : (kx + 1) * channels].reshape(rows, cols, channels)
        part = shifted(part, kx - 1)
        answer = part if answer is None else answer + part
    out[...] = answer.astype(BF16)


def reversed_bits(code, count):
    place, bit = 0, 1
    while bit < count:
        place = place * 2 + code // bit % 2
        bit *= 2
    return place


def place_kernel(n_gy, *refs):
    blocks, (conv, down) = refs[: 2 * n_gy], refs[2 * n_gy :]
    me = lax.axis_index("gy")
    parity = lax.axis_index("gz") % 2
    half, channels = conv.shape[3:]
    count, deep_channels = down.shape[2:]
    for index, block in enumerate(blocks):
        side = jnp.bitwise_xor(parity, index // n_gy)
        column = jnp.bitwise_xor(me, index % n_gy)
        for k in range(27):
            conv[k, column, side] = block[pl.ds(k * half, half)]
        for wide in range(deep_channels // channels):
            down[side, column, :, pl.ds(wide * channels, channels)] = block[
                pl.ds(27 * half + wide * count, count)
            ]


def swapped(value, axis, code):
    return lax.ppermute(value, axis, [(i, i ^ code) for i in range(lax.axis_size(axis))])


def crossed(value, code_gz, code_gy):
    count = lax.axis_size("gy")
    pairs = [
        (i * count + j, (i ^ code_gz) * count + (j ^ code_gy))
        for i in range(lax.axis_size("gz"))
        for j in range(count)
    ]
    return lax.ppermute(value, ("gz", "gy"), pairs)


def even_pairs(value):
    return swapped(value, "gz", 1)


def odd_pairs(value):
    last = lax.axis_size("gz") - 1
    pairs = [(i + d, i + 1 - d) for i in range(1, last, 2) for d in range(2)]
    return lax.ppermute(value, "gz", pairs)


def exchanged(value, axis):
    return lax.all_to_all(value, axis, split_axis=0, concat_axis=0, tiled=True)


def per_device(
    level_input, pre_activation, conv_weight, down_weight, skip_cotangent, deep_cotangent
):
    n_gz = lax.axis_size("gz")
    n_gy = lax.axis_size("gy")
    _, rows, cols, channels = level_input.shape
    planes, deep_rows, deep_cols, share = deep_cotangent.shape
    deep_channels = down_weight.shape[4]
    parity = lax.axis_index("gz") % 2
    devices = n_gz * n_gy
    part = channels // n_gy
    cells = rows * cols
    deep_cells = deep_rows * deep_cols
    half = part // 2
    down_count = 4 * deep_channels // n_gy
    wire = BF16 if n_gz <= 8 else F32
    shape = jax.ShapeDtypeStruct

    level = level_input.reshape(cells, channels)
    deep = deep_cotangent.reshape(planes, deep_cells, share)
    if share % 16 == 0:
        keep, send = call(
            deep_kernel,
            [shape((planes // 2, share, deep_cells), BF16)] * 2,
            deep,
            scratch=[pltpu.VMEM((planes, share, deep_cells), BF16)],
        )
        code = planes
        held = jnp.stack([keep, swapped(send, "gz", code)], axis=1)
        while code > 2:
            code //= 2
            count = code // 2
            upper = lax.axis_index("gz") // code % 2
            keep = lax.dynamic_slice_in_dim(held, upper * count, count, axis=0)
            send = lax.dynamic_slice_in_dim(held, (1 - upper) * count, count, axis=0)
            held = jnp.concatenate([keep, swapped(send, "gz", code)], axis=1)
        deep_t = [held[0], swapped(held[0], "gz", 1)]
    else:
        deep_t = jnp.repeat(jnp.swapaxes(deep, 1, 2), 2, axis=0)
        deep_t = [exchanged(deep_t, "gz").reshape(deep_channels, deep_cells)]
    level_t = call(
        level_kernel,
        [shape((part, cells), BF16)] * n_gy,
        level,
        scratch=[pltpu.VMEM((n_gy, part, cells), BF16)],
    )
    level_t = [swapped(value, "gy", code) if code else value for code, value in enumerate(level_t)]
    level_t = jnp.stack(level_t)
    even = even_pairs(level_t)
    *deep_t, level_t = lax.optimization_barrier((*deep_t, level_t))
    down_slice = lax.dynamic_index_in_dim(down_weight, parity, 0, keepdims=False)
    grad, down, *others = call(
        lambda *refs: mask_kernel(n_gy, *refs),
        [shape((cells, channels), BF16), shape((down_count, channels), F32)]
        + [shape((down_count, channels), BF16)] * (n_gy - 1),
        pre_activation[0],
        skip_cotangent[0],
        down_slice,
        *deep_t,
        scratch=[
            pltpu.VMEM((deep_channels, deep_cells), BF16),
            pltpu.VMEM((n_gy, 4 * channels // n_gy, deep_channels), F32),
        ],
    )
    shared = [swapped(grad, "gy", code) if code else grad for code in range(n_gy)]
    shared[1], level_t = lax.optimization_barrier((shared[1], level_t))
    odd = odd_pairs(level_t)
    even, *others = lax.optimization_barrier((even, *others))
    for code, value in enumerate(others):
        down = down + swapped(value, "gy", code + 1).astype(F32)
    keep, send, near = call(
        lambda *refs: weight_kernel(n_gy, (rows, cols, channels), *refs),
        (
            shape((27 * half, channels), F32),
            shape((27 * half, channels), wire),
            shape((rows + 2, cols, channels), BF16),
        ),
        even,
        level_t,
        odd,
        *shared,
        scratch=[
            pltpu.VMEM((n_gy * rows + 2, cols, 3 * channels), BF16),
            pltpu.VMEM((n_gy, 3 * part, cells), BF16),
            pltpu.VMEM((2, 27 * half, channels), F32),
        ],
    )
    def rounded(value):
        return lax.optimization_barrier(value.astype(wire))

    def added(value, other):
        return value.astype(F32) + other.astype(F32)

    cell_total = devices * cells
    down = rounded(down)
    codes = []
    code = n_gz // 2
    while code > 1:
        codes.append(code)
        code //= 2
    send = swapped(send, "gz", 1)
    for index, code in enumerate(codes):
        down_other = swapped(down, "gz", code)
        if index == 0:
            conv = (keep + send.astype(F32)).astype(wire)
            conv, late = lax.optimization_barrier((conv, near))
            cut = late.shape[0] // 2
            evens = even_pairs(late[:cut]), even_pairs(late[cut:])
        else:
            conv_other = swapped(conv, "gz", codes[index - 1])
            if index == 1:
                tied = (conv_other, down_other, *evens)
                conv_other, down_other, *evens = lax.optimization_barrier(tied)
            conv = added(conv, conv_other).astype(wire)
            if index == 1:
                conv, late = lax.optimization_barrier((conv, near))
                odds = odd_pairs(late[:cut]), odd_pairs(late[cut:])
            else:
                conv = lax.optimization_barrier(conv)
        down = added(down, down_other)
        if index < len(codes) - 1:
            down = rounded(down)
    conv_other = swapped(conv, "gz", codes[-1])
    input_grad = call(
        input_kernel,
        shape((rows, cols, channels), BF16),
        jnp.concatenate(evens, axis=0),
        near,
        jnp.concatenate(odds, axis=0),
        conv_weight,
    )
    conv = added(conv, conv_other) * (1 / math.sqrt(cell_total))
    down = down * (1 / math.sqrt(cell_total // 8))
    total = jnp.concatenate([conv.astype(BF16), down.astype(BF16)], axis=0)
    if n_gy == 4:
        lines = [
            [total, swapped(total, "gy", 2)],
            [swapped(total, "gz", 1), crossed(total, 1, 2)],
        ]
        lines[1][1], input_grad = lax.optimization_barrier((lines[1][1], input_grad))
        blocks = []
        for near_block, far_block in lines:
            blocks += [near_block, swapped(near_block, "gy", 1)]
            blocks += [far_block, swapped(far_block, "gy", 1)]
    else:
        blocks = [
            swapped(block, "gy", code) if code else block
            for block in (total, swapped(total, "gz", 1))
            for code in range(n_gy)
        ]
    conv_grad, down_grad = call(
        lambda *refs: place_kernel(n_gy, *refs),
        (
            shape((27, n_gy, 2, half, channels), BF16),
            shape((2, n_gy, 4 * channels // n_gy, deep_channels), BF16),
        ),
        *blocks,
    )
    return (
        input_grad[None],
        conv_grad.reshape(conv_weight.shape),
        down_grad.reshape(down_weight.shape),
    )


def solution(mesh):
    return jax.shard_map(
        per_device,
        mesh=mesh,
        in_specs=(
            P("gz", "gy", None, None),
            P("gz", "gy", None, None),
            P(),
            P(),
            P("gz", "gy", None, None),
            P(None, "gy", None, "gz"),
        ),
        out_specs=(P("gz", "gy", None, None), P(), P()),
        check_vma=False,
    )
```

```python
import math

import jax
import jax.numpy as jnp
from jax import lax
from jax.experimental import pallas as pl
from jax.experimental.pallas import tpu as pltpu
from jax.sharding import PartitionSpec as P

F32 = jnp.float32
BF16 = jnp.bfloat16
VMEM_LIMIT = 40 * 1024 * 1024


def call(kernel, out_shape, *operands, scratch=()):
    return pl.pallas_call(
        kernel,
        out_shape=out_shape,
        scratch_shapes=list(scratch),
        compiler_params=pltpu.CompilerParams(vmem_limit_bytes=VMEM_LIMIT),
    )(*operands)


def shifted(cells, step):
    if step == 0:
        return cells
    cols = cells.shape[1]
    moved = pltpu.roll(cells, step % cols, 1)
    col = lax.broadcasted_iota(jnp.int32, cells.shape, 1)
    keep = col >= step if step > 0 else col < cols + step
    return jnp.where(keep, moved, 0.0)


def deep_kernel(deep, keep, send, turned):
    planes = deep.shape[0]
    half = planes // 2
    for plane in range(planes):
        turned[plane] = deep[plane].astype(F32).T.astype(BF16)
    upper = lax.axis_index("gz") // planes
    keep[...] = turned[pl.ds(upper * half, half)]
    send[...] = turned[pl.ds((1 - upper) * half, half)]


def level_kernel(level, *rest):
    outs, level_t = rest[:-1], rest[-1]
    turned = level[...].astype(F32).T.astype(BF16)
    part = level_t.shape[1]
    for owner in range(len(outs)):
        level_t[owner] = turned[owner * part : (owner + 1) * part]
    me = lax.axis_index("gy")
    for code, out in enumerate(outs):
        out[...] = level_t[jnp.bitwise_xor(me, code)]


def mask_kernel(n_gy, pre, skip, weight, *rest):
    deeps, rest = rest[: -n_gy - 3], rest[-n_gy - 3 :]
    grad_out, kept, *outs, deep_t, down_all = rest
    if len(deeps) > 1:
        count, share = deeps[0].shape[:2]
        me = lax.axis_index("gz")
        for place in range(2 * count):
            owner = jnp.bitwise_xor(me, reversed_bits(place, 2 * count))
            first = pl.multiple_of(owner * share, share)
            deep_t[pl.ds(first, share)] = deeps[place // count][place % count]
    else:
        deep_t[...] = deeps[0][...]
    rows, cols, channels = pre.shape
    half = rows // 2
    deep_cols = cols // 2
    cells = half * cols
    deep_cells = half * deep_cols
    wide = lax.broadcasted_iota(jnp.int32, (deep_cells, cells), 1) // 2
    deep = lax.broadcasted_iota(jnp.int32, (deep_cells, cells), 0)
    repeat = (wide == deep).astype(BF16)
    spread = jnp.dot(deep_t[...], repeat, preferred_element_type=F32).astype(BF16)
    col = lax.broadcasted_iota(jnp.int32, (cells, channels), 0) % 2
    count = down_all.shape[1]
    for b in range(2):
        parts = [
            lax.dot_general(
                spread, weight[b, c], (((0,), (1,)), ((), ())), preferred_element_type=F32
            )
            for c in range(2)
        ]
        part = jnp.where(col == 0, parts[0], parts[1]).reshape(half, cols, channels)
        for y in range(half):
            row = 2 * y + b
            pre_row = pre[row].astype(F32)
            total = part[y] + skip[row].astype(F32)
            grad = jnp.where(pre_row > 0, total, 0.0).astype(BF16)
            grad_out[pl.ds(row * cols, cols)] = grad
        hidden = jnp.concatenate(
            [jnp.maximum(pre[2 * y + b].astype(F32), 0.0) for y in range(half)], axis=0
        )
        for c in range(2):
            one = jnp.where(col == c, hidden, 0.0).astype(BF16)
            down = lax.dot_general(
                one, spread, (((0,), (1,)), ((), ())), preferred_element_type=F32
            )
            for first, owner, inner, take in segments(channels, count, channels, (b * 2 + c) * channels):
                down_all[owner, pl.ds(inner, take)] = down[first : first + take]
    me = lax.axis_index("gy")
    for code, out in enumerate([kept, *outs]):
        owner = jnp.bitwise_xor(me, code)
        for side in range(down_all.shape[2] // channels):
            out[pl.ds(side * count, count)] = down_all[
                owner, :, pl.ds(side * channels, channels)
            ].astype(out.dtype)


def segments(rows, piece, unit, base=0):
    row = 0
    while row < rows:
        take = min(rows - row, unit - row % unit, piece - (base + row) % piece)
        yield row, (base + row) // piece, (base + row) % piece, take
        row += take


def sides(even, odd):
    upper = lax.axis_index("gz") % 2 == 0
    low = jnp.where(upper, odd[...].astype(F32), even[...].astype(F32)).astype(BF16)
    high = jnp.where(upper, even[...].astype(F32), odd[...].astype(F32)).astype(BF16)
    return low, high


def weight_kernel(n_gy, shape, *refs):
    even, own, odd = refs[:3]
    shared = refs[3 : 3 + n_gy]
    keep, send, near, wide, level, halves = refs[3 + n_gy :]
    rows, cols, channels = shape
    part = own.shape[1]
    cells = rows * cols
    half = part // 2
    rows_all = n_gy * rows
    me = lax.axis_index("gy")
    low, high = sides(even, odd)
    for edge in (0, rows_all + 1):
        wide[edge] = jnp.zeros(wide.shape[1:], BF16)
    for code in range(n_gy):
        owner = jnp.bitwise_xor(me, code)
        grads = shared[code][pl.ds(0, cells)].reshape(rows, cols, channels).astype(F32)
        for kx in range(3):
            wide[pl.ds(1 + owner * rows, rows), :, pl.ds(kx * channels, channels)] = shifted(
                grads, kx - 1
            ).astype(BF16)
        for kz, plane in enumerate((low[code], own[code], high[code])):
            level[owner, pl.ds(kz * part, part)] = plane
    near[...] = wide[pl.ds(me * rows, rows + 2), :, pl.ds(channels, channels)]
    for ky in range(3):
        total = None
        for owner in range(n_gy):
            slab = wide[pl.ds(2 - ky + owner * rows, rows)].reshape(cells, 3 * channels)
            term = jnp.dot(level[owner], slab, preferred_element_type=F32)
            total = term if total is None else total + term
        for kz in range(3):
            for kx in range(3):
                value = total[kz * part : (kz + 1) * part, kx * channels : (kx + 1) * channels]
                index = (kz * 3 + ky) * 3 + kx
                for side in range(2):
                    halves[side, pl.ds(index * half, half)] = value[side * half : (side + 1) * half]
    side = lax.axis_index("gz") % 2
    keep[...] = halves[side]
    send[...] = halves[1 - side].astype(send.dtype)


def input_kernel(even, own, odd, weight, out):
    rows, cols, channels = out.shape
    low, high = sides(even, odd)
    planes = (low, own, high)
    total = None
    for kz in range(3):
        for ky in range(3):
            slab = planes[2 - kz][2 - ky : 2 - ky + rows].reshape(rows * cols, channels)
            term = lax.dot_general(
                slab,
                weight[kz, ky].reshape(3 * channels, channels),
                (((1,), (1,)), ((), ())),
                preferred_element_type=F32,
            )
            total = term if total is None else total + term
    answer = None
    for kx in range(3):
        part = total[:, kx * channels : (kx + 1) * channels].reshape(rows, cols, channels)
        part = shifted(part, kx - 1)
        answer = part if answer is None else answer + part
    out[...] = answer.astype(BF16)


def reversed_bits(code, count):
    place, bit = 0, 1
    while bit < count:
        place = place * 2 + code // bit % 2
        bit *= 2
    return place


def place_kernel(n_gy, *refs):
    blocks, (conv, down) = refs[: 2 * n_gy], refs[2 * n_gy :]
    me = lax.axis_index("gy")
    parity = lax.axis_index("gz") % 2
    half, channels = conv.shape[3:]
    count, deep_channels = down.shape[2:]
    for index, block in enumerate(blocks):
        side = jnp.bitwise_xor(parity, index // n_gy)
        column = jnp.bitwise_xor(me, index % n_gy)
        for k in range(27):
            conv[k, column, side] = block[pl.ds(k * half, half)]
        for wide in range(deep_channels // channels):
            down[side, column, :, pl.ds(wide * channels, channels)] = block[
                pl.ds(27 * half + wide * count, count)
            ]


def swapped(value, axis, code):
    return lax.ppermute(value, axis, [(i, i ^ code) for i in range(lax.axis_size(axis))])


def crossed(value, code_gz, code_gy):
    count = lax.axis_size("gy")
    pairs = [
        (i * count + j, (i ^ code_gz) * count + (j ^ code_gy))
        for i in range(lax.axis_size("gz"))
        for j in range(count)
    ]
    return lax.ppermute(value, ("gz", "gy"), pairs)


def even_pairs(value):
    return swapped(value, "gz", 1)


def odd_pairs(value):
    last = lax.axis_size("gz") - 1
    pairs = [(i + d, i + 1 - d) for i in range(1, last, 2) for d in range(2)]
    return lax.ppermute(value, "gz", pairs)


def exchanged(value, axis):
    return lax.all_to_all(value, axis, split_axis=0, concat_axis=0, tiled=True)


def per_device(
    level_input, pre_activation, conv_weight, down_weight, skip_cotangent, deep_cotangent
):
    n_gz = lax.axis_size("gz")
    n_gy = lax.axis_size("gy")
    _, rows, cols, channels = level_input.shape
    planes, deep_rows, deep_cols, share = deep_cotangent.shape
    deep_channels = down_weight.shape[4]
    parity = lax.axis_index("gz") % 2
    devices = n_gz * n_gy
    part = channels // n_gy
    cells = rows * cols
    deep_cells = deep_rows * deep_cols
    half = part // 2
    down_count = 4 * deep_channels // n_gy
    wire = BF16 if n_gz <= 8 else F32
    shape = jax.ShapeDtypeStruct

    level = level_input.reshape(cells, channels)
    deep = deep_cotangent.reshape(planes, deep_cells, share)
    if share % 16 == 0:
        keep, send = call(
            deep_kernel,
            [shape((planes // 2, share, deep_cells), BF16)] * 2,
            deep,
            scratch=[pltpu.VMEM((planes, share, deep_cells), BF16)],
        )
        code = planes
        held = jnp.stack([keep, swapped(send, "gz", code)], axis=1)
        while code > 2:
            code //= 2
            count = code // 2
            upper = lax.axis_index("gz") // code % 2
            keep = lax.dynamic_slice_in_dim(held, upper * count, count, axis=0)
            send = lax.dynamic_slice_in_dim(held, (1 - upper) * count, count, axis=0)
            held = jnp.concatenate([keep, swapped(send, "gz", code)], axis=1)
        deep_t = [held[0], swapped(held[0], "gz", 1)]
    else:
        deep_t = jnp.repeat(jnp.swapaxes(deep, 1, 2), 2, axis=0)
        deep_t = [exchanged(deep_t, "gz").reshape(deep_channels, deep_cells)]
    level_t = call(
        level_kernel,
        [shape((part, cells), BF16)] * n_gy,
        level,
        scratch=[pltpu.VMEM((n_gy, part, cells), BF16)],
    )
    level_t = [swapped(value, "gy", code) if code else value for code, value in enumerate(level_t)]
    level_t = jnp.stack(level_t)
    even = even_pairs(level_t)
    *deep_t, level_t = lax.optimization_barrier((*deep_t, level_t))
    down_slice = lax.dynamic_index_in_dim(down_weight, parity, 0, keepdims=False)
    grad, down, *others = call(
        lambda *refs: mask_kernel(n_gy, *refs),
        [shape((cells, channels), BF16), shape((down_count, channels), F32)]
        + [shape((down_count, channels), BF16)] * (n_gy - 1),
        pre_activation[0],
        skip_cotangent[0],
        down_slice,
        *deep_t,
        scratch=[
            pltpu.VMEM((deep_channels, deep_cells), BF16),
            pltpu.VMEM((n_gy, 4 * channels // n_gy, deep_channels), F32),
        ],
    )
    shared = [swapped(grad, "gy", code) if code else grad for code in range(n_gy)]
    shared[1], level_t = lax.optimization_barrier((shared[1], level_t))
    odd = odd_pairs(level_t)
    even, *others = lax.optimization_barrier((even, *others))
    for code, value in enumerate(others):
        down = down + swapped(value, "gy", code + 1).astype(F32)
    keep, send, near = call(
        lambda *refs: weight_kernel(n_gy, (rows, cols, channels), *refs),
        (
            shape((27 * half, channels), F32),
            shape((27 * half, channels), wire),
            shape((rows + 2, cols, channels), BF16),
        ),
        even,
        level_t,
        odd,
        *shared,
        scratch=[
            pltpu.VMEM((n_gy * rows + 2, cols, 3 * channels), BF16),
            pltpu.VMEM((n_gy, 3 * part, cells), BF16),
            pltpu.VMEM((2, 27 * half, channels), F32),
        ],
    )
    near_odd, near_even = odd_pairs(near), even_pairs(near)
    def rounded(value):
        return lax.optimization_barrier(value.astype(wire))

    def added(value, other):
        return value.astype(F32) + other.astype(F32)

    cell_total = devices * cells
    down = rounded(down)
    codes = []
    code = n_gz // 2
    while code > 1:
        codes.append(code)
        code //= 2
    send = swapped(send, "gz", 1)
    for index, code in enumerate(codes):
        down_other = swapped(down, "gz", code)
        if index == 0:
            conv = rounded(keep + send.astype(F32))
        else:
            conv_other = swapped(conv, "gz", codes[index - 1])
            if index == 1:
                tied = (conv_other, down_other, near_odd, near_even)
                conv_other, down_other, near_odd, near_even = lax.optimization_barrier(tied)
            conv = rounded(added(conv, conv_other))
        down = added(down, down_other)
        if index < len(codes) - 1:
            down = rounded(down)
    conv_other = swapped(conv, "gz", codes[-1])
    input_grad = call(
        input_kernel,
        shape((rows, cols, channels), BF16),
        near_even,
        near,
        near_odd,
        conv_weight,
    )
    conv_other, input_grad = lax.optimization_barrier((conv_other, input_grad))
    conv = added(conv, conv_other) * (1 / math.sqrt(cell_total))
    down = down * (1 / math.sqrt(cell_total // 8))
    total = jnp.concatenate([conv.astype(BF16), down.astype(BF16)], axis=0)
    if n_gy == 4:
        lines = [
            [total, swapped(total, "gy", 2)],
            [swapped(total, "gz", 1), crossed(total, 1, 2)],
        ]
        blocks = []
        for near_block, far_block in lines:
            blocks += [near_block, swapped(near_block, "gy", 1)]
            blocks += [far_block, swapped(far_block, "gy", 1)]
    else:
        blocks = [
            swapped(block, "gy", code) if code else block
            for block in (total, swapped(total, "gz", 1))
            for code in range(n_gy)
        ]
    conv_grad, down_grad = call(
        lambda *refs: place_kernel(n_gy, *refs),
        (
            shape((27, n_gy, 2, half, channels), BF16),
            shape((2, n_gy, 4 * channels // n_gy, deep_channels), BF16),
        ),
        *blocks,
    )
    return (
        input_grad[None],
        conv_grad.reshape(conv_weight.shape),
        down_grad.reshape(down_weight.shape),
    )


def solution(mesh):
    return jax.shard_map(
        per_device,
        mesh=mesh,
        in_specs=(
            P("gz", "gy", None, None),
            P("gz", "gy", None, None),
            P(),
            P(),
            P("gz", "gy", None, None),
            P(None, "gy", None, "gz"),
        ),
        out_specs=(P("gz", "gy", None, None), P(), P()),
        check_vma=False,
    )
```

```python
import math

import jax
import jax.numpy as jnp
from jax import lax
from jax.experimental import pallas as pl
from jax.experimental.pallas import tpu as pltpu
from jax.sharding import PartitionSpec as P

F32 = jnp.float32
BF16 = jnp.bfloat16
VMEM_LIMIT = 40 * 1024 * 1024


def call(kernel, out_shape, *operands, scratch=()):
    return pl.pallas_call(
        kernel,
        out_shape=out_shape,
        scratch_shapes=list(scratch),
        compiler_params=pltpu.CompilerParams(vmem_limit_bytes=VMEM_LIMIT),
    )(*operands)


def shifted(cells, step):
    if step == 0:
        return cells
    cols = cells.shape[1]
    moved = pltpu.roll(cells, step % cols, 1)
    col = lax.broadcasted_iota(jnp.int32, cells.shape, 1)
    keep = col >= step if step > 0 else col < cols + step
    return jnp.where(keep, moved, 0.0)


def deep_kernel(deep, keep, send, turned):
    planes = deep.shape[0]
    half = planes // 2
    for plane in range(planes):
        turned[plane] = deep[plane].astype(F32).T.astype(BF16)
    upper = lax.axis_index("gz") // planes
    keep[...] = turned[pl.ds(upper * half, half)]
    send[...] = turned[pl.ds((1 - upper) * half, half)]


def level_kernel(level, *rest):
    outs, level_t = rest[:-1], rest[-1]
    turned = level[...].astype(F32).T.astype(BF16)
    part = level_t.shape[1]
    for owner in range(len(outs)):
        level_t[owner] = turned[owner * part : (owner + 1) * part]
    me = lax.axis_index("gy")
    for code, out in enumerate(outs):
        out[...] = level_t[jnp.bitwise_xor(me, code)]


def mask_kernel(n_gy, pre, skip, weight, *rest):
    deeps, rest = rest[: -n_gy - 3], rest[-n_gy - 3 :]
    grad_out, kept, *outs, deep_t, down_all = rest
    if len(deeps) > 1:
        count, share = deeps[0].shape[:2]
        me = lax.axis_index("gz")
        for place in range(2 * count):
            owner = jnp.bitwise_xor(me, reversed_bits(place, 2 * count))
            first = pl.multiple_of(owner * share, share)
            deep_t[pl.ds(first, share)] = deeps[place // count][place % count]
    else:
        deep_t[...] = deeps[0][...]
    rows, cols, channels = pre.shape
    half = rows // 2
    deep_cols = cols // 2
    cells = half * cols
    deep_cells = half * deep_cols
    wide = lax.broadcasted_iota(jnp.int32, (deep_cells, cells), 1) // 2
    deep = lax.broadcasted_iota(jnp.int32, (deep_cells, cells), 0)
    repeat = (wide == deep).astype(BF16)
    spread = jnp.dot(deep_t[...], repeat, preferred_element_type=F32).astype(BF16)
    col = lax.broadcasted_iota(jnp.int32, (cells, channels), 0) % 2
    count = down_all.shape[1]
    for b in range(2):
        parts = [
            lax.dot_general(
                spread, weight[b, c], (((0,), (1,)), ((), ())), preferred_element_type=F32
            )
            for c in range(2)
        ]
        part = jnp.where(col == 0, parts[0], parts[1]).reshape(half, cols, channels)
        for y in range(half):
            row = 2 * y + b
            pre_row = pre[row].astype(F32)
            total = part[y] + skip[row].astype(F32)
            grad = jnp.where(pre_row > 0, total, 0.0).astype(BF16)
            grad_out[pl.ds(row * cols, cols)] = grad
        hidden = jnp.concatenate(
            [jnp.maximum(pre[2 * y + b].astype(F32), 0.0) for y in range(half)], axis=0
        )
        for c in range(2):
            one = jnp.where(col == c, hidden, 0.0).astype(BF16)
            down = lax.dot_general(
                one, spread, (((0,), (1,)), ((), ())), preferred_element_type=F32
            )
            for first, owner, inner, take in segments(channels, count, channels, (b * 2 + c) * channels):
                down_all[owner, pl.ds(inner, take)] = down[first : first + take]
    me = lax.axis_index("gy")
    for code, out in enumerate([kept, *outs]):
        owner = jnp.bitwise_xor(me, code)
        for side in range(down_all.shape[2] // channels):
            out[pl.ds(side * count, count)] = down_all[
                owner, :, pl.ds(side * channels, channels)
            ].astype(out.dtype)


def segments(rows, piece, unit, base=0):
    row = 0
    while row < rows:
        take = min(rows - row, unit - row % unit, piece - (base + row) % piece)
        yield row, (base + row) // piece, (base + row) % piece, take
        row += take


def sides(even, odd):
    upper = lax.axis_index("gz") % 2 == 0
    low = jnp.where(upper, odd[...].astype(F32), even[...].astype(F32)).astype(BF16)
    high = jnp.where(upper, even[...].astype(F32), odd[...].astype(F32)).astype(BF16)
    return low, high


def weight_kernel(n_gy, shape, *refs):
    even, own, odd = refs[:3]
    shared = refs[3 : 3 + n_gy]
    keep, send, near, wide, level, halves = refs[3 + n_gy :]
    rows, cols, channels = shape
    part = own.shape[1]
    cells = rows * cols
    half = part // 2
    rows_all = n_gy * rows
    me = lax.axis_index("gy")
    low, high = sides(even, odd)
    for edge in (0, rows_all + 1):
        wide[edge] = jnp.zeros(wide.shape[1:], BF16)
    for code in range(n_gy):
        owner = jnp.bitwise_xor(me, code)
        grads = shared[code][pl.ds(0, cells)].reshape(rows, cols, channels).astype(F32)
        for kx in range(3):
            wide[pl.ds(1 + owner * rows, rows), :, pl.ds(kx * channels, channels)] = shifted(
                grads, kx - 1
            ).astype(BF16)
        for kz, plane in enumerate((low[code], own[code], high[code])):
            level[owner, pl.ds(kz * part, part)] = plane
    near[...] = wide[pl.ds(me * rows, rows + 2), :, pl.ds(channels, channels)]
    for ky in range(3):
        total = None
        for owner in range(n_gy):
            slab = wide[pl.ds(2 - ky + owner * rows, rows)].reshape(cells, 3 * channels)
            term = jnp.dot(level[owner], slab, preferred_element_type=F32)
            total = term if total is None else total + term
        for kz in range(3):
            for kx in range(3):
                value = total[kz * part : (kz + 1) * part, kx * channels : (kx + 1) * channels]
                index = (kz * 3 + ky) * 3 + kx
                for side in range(2):
                    halves[side, pl.ds(index * half, half)] = value[side * half : (side + 1) * half]
    side = lax.axis_index("gz") % 2
    keep[...] = halves[side]
    send[...] = halves[1 - side].astype(send.dtype)


def input_kernel(even, own, odd, weight, out):
    rows, cols, channels = out.shape
    low, high = sides(even, odd)
    planes = (low, own, high)
    total = None
    for kz in range(3):
        for ky in range(3):
            slab = planes[2 - kz][2 - ky : 2 - ky + rows].reshape(rows * cols, channels)
            term = lax.dot_general(
                slab,
                weight[kz, ky].reshape(3 * channels, channels),
                (((1,), (1,)), ((), ())),
                preferred_element_type=F32,
            )
            total = term if total is None else total + term
    answer = None
    for kx in range(3):
        part = total[:, kx * channels : (kx + 1) * channels].reshape(rows, cols, channels)
        part = shifted(part, kx - 1)
        answer = part if answer is None else answer + part
    out[...] = answer.astype(BF16)


def reversed_bits(code, count):
    place, bit = 0, 1
    while bit < count:
        place = place * 2 + code // bit % 2
        bit *= 2
    return place


def place_kernel(n_gy, *refs):
    blocks, (conv, down) = refs[: 2 * n_gy], refs[2 * n_gy :]
    me = lax.axis_index("gy")
    parity = lax.axis_index("gz") % 2
    half, channels = conv.shape[3:]
    count, deep_channels = down.shape[2:]
    for index, block in enumerate(blocks):
        side = jnp.bitwise_xor(parity, index // n_gy)
        column = jnp.bitwise_xor(me, index % n_gy)
        for k in range(27):
            conv[k, column, side] = block[pl.ds(k * half, half)]
        for wide in range(deep_channels // channels):
            down[side, column, :, pl.ds(wide * channels, channels)] = block[
                pl.ds(27 * half + wide * count, count)
            ]


def swapped(value, axis, code):
    return lax.ppermute(value, axis, [(i, i ^ code) for i in range(lax.axis_size(axis))])


def crossed(value, code_gz, code_gy):
    count = lax.axis_size("gy")
    pairs = [
        (i * count + j, (i ^ code_gz) * count + (j ^ code_gy))
        for i in range(lax.axis_size("gz"))
        for j in range(count)
    ]
    return lax.ppermute(value, ("gz", "gy"), pairs)


def even_pairs(value):
    return swapped(value, "gz", 1)


def odd_pairs(value):
    last = lax.axis_size("gz") - 1
    pairs = [(i + d, i + 1 - d) for i in range(1, last, 2) for d in range(2)]
    return lax.ppermute(value, "gz", pairs)


def exchanged(value, axis):
    return lax.all_to_all(value, axis, split_axis=0, concat_axis=0, tiled=True)


def per_device(
    level_input, pre_activation, conv_weight, down_weight, skip_cotangent, deep_cotangent
):
    n_gz = lax.axis_size("gz")
    n_gy = lax.axis_size("gy")
    _, rows, cols, channels = level_input.shape
    planes, deep_rows, deep_cols, share = deep_cotangent.shape
    deep_channels = down_weight.shape[4]
    parity = lax.axis_index("gz") % 2
    devices = n_gz * n_gy
    part = channels // n_gy
    cells = rows * cols
    deep_cells = deep_rows * deep_cols
    half = part // 2
    down_count = 4 * deep_channels // n_gy
    wire = BF16 if n_gz <= 8 else F32
    shape = jax.ShapeDtypeStruct

    level = level_input.reshape(cells, channels)
    deep = deep_cotangent.reshape(planes, deep_cells, share)
    if share % 16 == 0:
        keep, send = call(
            deep_kernel,
            [shape((planes // 2, share, deep_cells), BF16)] * 2,
            deep,
            scratch=[pltpu.VMEM((planes, share, deep_cells), BF16)],
        )
        code = planes
        held = jnp.stack([keep, swapped(send, "gz", code)], axis=1)
        while code > 2:
            code //= 2
            count = code // 2
            upper = lax.axis_index("gz") // code % 2
            keep = lax.dynamic_slice_in_dim(held, upper * count, count, axis=0)
            send = lax.dynamic_slice_in_dim(held, (1 - upper) * count, count, axis=0)
            held = jnp.concatenate([keep, swapped(send, "gz", code)], axis=1)
        deep_t = [held[0], swapped(held[0], "gz", 1)]
    else:
        deep_t = jnp.repeat(jnp.swapaxes(deep, 1, 2), 2, axis=0)
        deep_t = [exchanged(deep_t, "gz").reshape(deep_channels, deep_cells)]
    level_t = call(
        level_kernel,
        [shape((part, cells), BF16)] * n_gy,
        level,
        scratch=[pltpu.VMEM((n_gy, part, cells), BF16)],
    )
    level_t = [swapped(value, "gy", code) if code else value for code, value in enumerate(level_t)]
    level_t = jnp.stack(level_t)
    even = even_pairs(level_t)
    *deep_t, level_t = lax.optimization_barrier((*deep_t, level_t))
    down_slice = lax.dynamic_index_in_dim(down_weight, parity, 0, keepdims=False)
    grad, down, *others = call(
        lambda *refs: mask_kernel(n_gy, *refs),
        [shape((cells, channels), BF16), shape((down_count, channels), F32)]
        + [shape((down_count, channels), BF16)] * (n_gy - 1),
        pre_activation[0],
        skip_cotangent[0],
        down_slice,
        *deep_t,
        scratch=[
            pltpu.VMEM((deep_channels, deep_cells), BF16),
            pltpu.VMEM((n_gy, 4 * channels // n_gy, deep_channels), F32),
        ],
    )
    shared = [swapped(grad, "gy", code) if code else grad for code in range(n_gy)]
    shared[1], level_t = lax.optimization_barrier((shared[1], level_t))
    odd = odd_pairs(level_t)
    even, *others = lax.optimization_barrier((even, *others))
    for code, value in enumerate(others):
        down = down + swapped(value, "gy", code + 1).astype(F32)
    keep, send, near = call(
        lambda *refs: weight_kernel(n_gy, (rows, cols, channels), *refs),
        (
            shape((27 * half, channels), F32),
            shape((27 * half, channels), wire),
            shape((rows + 2, cols, channels), BF16),
        ),
        even,
        level_t,
        odd,
        *shared,
        scratch=[
            pltpu.VMEM((n_gy * rows + 2, cols, 3 * channels), BF16),
            pltpu.VMEM((n_gy, 3 * part, cells), BF16),
            pltpu.VMEM((2, 27 * half, channels), F32),
        ],
    )
    near_even, near_odd = even_pairs(near), odd_pairs(near)
    def rounded(value):
        return lax.optimization_barrier(value.astype(wire))

    def added(value, other):
        return value.astype(F32) + other.astype(F32)

    cell_total = devices * cells
    down = rounded(down)
    codes = []
    code = n_gz // 2
    while code > 1:
        codes.append(code)
        code //= 2
    send = swapped(send, "gz", 1)
    for index, code in enumerate(codes):
        down_other = swapped(down, "gz", code)
        if index == 0:
            send, down_other = lax.optimization_barrier((send, down_other))
            conv = rounded(keep + send.astype(F32))
        else:
            conv_other = swapped(conv, "gz", codes[index - 1])
            if index == 1:
                tied = (conv_other, down_other, near_even, near_odd)
                conv_other, down_other, near_even, near_odd = lax.optimization_barrier(tied)
            conv = rounded(added(conv, conv_other))
        down = added(down, down_other)
        if index < len(codes) - 1:
            down = rounded(down)
    conv_other = swapped(conv, "gz", codes[-1])
    input_grad = call(
        input_kernel,
        shape((rows, cols, channels), BF16),
        near_even,
        near,
        near_odd,
        conv_weight,
    )
    conv_other, input_grad = lax.optimization_barrier((conv_other, input_grad))
    conv = added(conv, conv_other) * (1 / math.sqrt(cell_total))
    down = down * (1 / math.sqrt(cell_total // 8))
    total = jnp.concatenate([conv.astype(BF16), down.astype(BF16)], axis=0)
    if n_gy == 4:
        lines = [
            [total, swapped(total, "gy", 2)],
            [swapped(total, "gz", 1), crossed(total, 1, 2)],
        ]
        blocks = []
        for near_block, far_block in lines:
            blocks += [near_block, swapped(near_block, "gy", 1)]
            blocks += [far_block, swapped(far_block, "gy", 1)]
    else:
        blocks = [
            swapped(block, "gy", code) if code else block
            for block in (total, swapped(total, "gz", 1))
            for code in range(n_gy)
        ]
    conv_grad, down_grad = call(
        lambda *refs: place_kernel(n_gy, *refs),
        (
            shape((27, n_gy, 2, half, channels), BF16),
            shape((2, n_gy, 4 * channels // n_gy, deep_channels), BF16),
        ),
        *blocks,
    )
    return (
        input_grad[None],
        conv_grad.reshape(conv_weight.shape),
        down_grad.reshape(down_weight.shape),
    )


def solution(mesh):
    return jax.shard_map(
        per_device,
        mesh=mesh,
        in_specs=(
            P("gz", "gy", None, None),
            P("gz", "gy", None, None),
            P(),
            P(),
            P("gz", "gy", None, None),
            P(None, "gy", None, "gz"),
        ),
        out_specs=(P("gz", "gy", None, None), P(), P()),
        check_vma=False,
    )
```

```python
import math

import jax
import jax.numpy as jnp
from jax import lax
from jax.experimental import pallas as pl
from jax.experimental.pallas import tpu as pltpu
from jax.sharding import PartitionSpec as P

F32 = jnp.float32
BF16 = jnp.bfloat16
VMEM_LIMIT = 40 * 1024 * 1024


def call(kernel, out_shape, *operands, scratch=()):
    return pl.pallas_call(
        kernel,
        out_shape=out_shape,
        scratch_shapes=list(scratch),
        compiler_params=pltpu.CompilerParams(vmem_limit_bytes=VMEM_LIMIT),
    )(*operands)


def shifted(cells, step):
    if step == 0:
        return cells
    cols = cells.shape[1]
    moved = pltpu.roll(cells, step % cols, 1)
    col = lax.broadcasted_iota(jnp.int32, cells.shape, 1)
    keep = col >= step if step > 0 else col < cols + step
    return jnp.where(keep, moved, 0.0)


def deep_kernel(deep, keep, send, turned):
    planes = deep.shape[0]
    half = planes // 2
    for plane in range(planes):
        turned[plane] = deep[plane].astype(F32).T.astype(BF16)
    upper = lax.axis_index("gz") // planes
    keep[...] = turned[pl.ds(upper * half, half)]
    send[...] = turned[pl.ds((1 - upper) * half, half)]


def level_kernel(level, *rest):
    outs, level_t = rest[:-1], rest[-1]
    turned = level[...].astype(F32).T.astype(BF16)
    part = level_t.shape[1]
    for owner in range(len(outs)):
        level_t[owner] = turned[owner * part : (owner + 1) * part]
    me = lax.axis_index("gy")
    for code, out in enumerate(outs):
        out[...] = level_t[jnp.bitwise_xor(me, code)]


def mask_kernel(n_gy, pre, skip, weight, *rest):
    deeps, rest = rest[: -n_gy - 3], rest[-n_gy - 3 :]
    grad_out, kept, *outs, deep_t, down_all = rest
    if len(deeps) > 1:
        count, share = deeps[0].shape[:2]
        me = lax.axis_index("gz")
        for place in range(2 * count):
            owner = jnp.bitwise_xor(me, reversed_bits(place, 2 * count))
            first = pl.multiple_of(owner * share, share)
            deep_t[pl.ds(first, share)] = deeps[place // count][place % count]
    else:
        deep_t[...] = deeps[0][...]
    rows, cols, channels = pre.shape
    half = rows // 2
    deep_cols = cols // 2
    cells = half * cols
    deep_cells = half * deep_cols
    wide = lax.broadcasted_iota(jnp.int32, (deep_cells, cells), 1) // 2
    deep = lax.broadcasted_iota(jnp.int32, (deep_cells, cells), 0)
    repeat = (wide == deep).astype(BF16)
    spread = jnp.dot(deep_t[...], repeat, preferred_element_type=F32).astype(BF16)
    col = lax.broadcasted_iota(jnp.int32, (cells, channels), 0) % 2
    count = down_all.shape[1]
    for b in range(2):
        parts = [
            lax.dot_general(
                spread, weight[b, c], (((0,), (1,)), ((), ())), preferred_element_type=F32
            )
            for c in range(2)
        ]
        part = jnp.where(col == 0, parts[0], parts[1]).reshape(half, cols, channels)
        for y in range(half):
            row = 2 * y + b
            pre_row = pre[row].astype(F32)
            total = part[y] + skip[row].astype(F32)
            grad = jnp.where(pre_row > 0, total, 0.0).astype(BF16)
            grad_out[pl.ds(row * cols, cols)] = grad
        hidden = jnp.concatenate(
            [jnp.maximum(pre[2 * y + b].astype(F32), 0.0) for y in range(half)], axis=0
        )
        for c in range(2):
            one = jnp.where(col == c, hidden, 0.0).astype(BF16)
            down = lax.dot_general(
                one, spread, (((0,), (1,)), ((), ())), preferred_element_type=F32
            )
            for first, owner, inner, take in segments(channels, count, channels, (b * 2 + c) * channels):
                down_all[owner, pl.ds(inner, take)] = down[first : first + take]
    me = lax.axis_index("gy")
    for code, out in enumerate([kept, *outs]):
        owner = jnp.bitwise_xor(me, code)
        for side in range(down_all.shape[2] // channels):
            out[pl.ds(side * count, count)] = down_all[
                owner, :, pl.ds(side * channels, channels)
            ].astype(out.dtype)


def segments(rows, piece, unit, base=0):
    row = 0
    while row < rows:
        take = min(rows - row, unit - row % unit, piece - (base + row) % piece)
        yield row, (base + row) // piece, (base + row) % piece, take
        row += take


def sides(even, odd):
    upper = lax.axis_index("gz") % 2 == 0
    low = jnp.where(upper, odd[...].astype(F32), even[...].astype(F32)).astype(BF16)
    high = jnp.where(upper, even[...].astype(F32), odd[...].astype(F32)).astype(BF16)
    return low, high


def weight_kernel(n_gy, shape, *refs):
    even, own, odd = refs[:3]
    shared = refs[3 : 3 + n_gy]
    keep, send, near, wide, level, halves = refs[3 + n_gy :]
    rows, cols, channels = shape
    part = own.shape[1]
    cells = rows * cols
    half = part // 2
    rows_all = n_gy * rows
    me = lax.axis_index("gy")
    low, high = sides(even, odd)
    for edge in (0, rows_all + 1):
        wide[edge] = jnp.zeros(wide.shape[1:], BF16)
    for code in range(n_gy):
        owner = jnp.bitwise_xor(me, code)
        grads = shared[code][pl.ds(0, cells)].reshape(rows, cols, channels).astype(F32)
        for kx in range(3):
            wide[pl.ds(1 + owner * rows, rows), :, pl.ds(kx * channels, channels)] = shifted(
                grads, kx - 1
            ).astype(BF16)
        for kz, plane in enumerate((low[code], own[code], high[code])):
            level[owner, pl.ds(kz * part, part)] = plane
    near[...] = wide[pl.ds(me * rows, rows + 2), :, pl.ds(channels, channels)]
    for ky in range(3):
        total = None
        for owner in range(n_gy):
            slab = wide[pl.ds(2 - ky + owner * rows, rows)].reshape(cells, 3 * channels)
            term = jnp.dot(level[owner], slab, preferred_element_type=F32)
            total = term if total is None else total + term
        for kz in range(3):
            for kx in range(3):
                value = total[kz * part : (kz + 1) * part, kx * channels : (kx + 1) * channels]
                index = (kz * 3 + ky) * 3 + kx
                for side in range(2):
                    halves[side, pl.ds(index * half, half)] = value[side * half : (side + 1) * half]
    side = lax.axis_index("gz") % 2
    keep[...] = halves[side]
    send[...] = halves[1 - side].astype(send.dtype)


def input_kernel(even, own, odd, weight, out):
    rows, cols, channels = out.shape
    low, high = sides(even, odd)
    planes = (low, own, high)
    total = None
    for kz in range(3):
        for ky in range(3):
            slab = planes[2 - kz][2 - ky : 2 - ky + rows].reshape(rows * cols, channels)
            term = lax.dot_general(
                slab,
                weight[kz, ky].reshape(3 * channels, channels),
                (((1,), (1,)), ((), ())),
                preferred_element_type=F32,
            )
            total = term if total is None else total + term
    answer = None
    for kx in range(3):
        part = total[:, kx * channels : (kx + 1) * channels].reshape(rows, cols, channels)
        part = shifted(part, kx - 1)
        answer = part if answer is None else answer + part
    out[...] = answer.astype(BF16)


def reversed_bits(code, count):
    place, bit = 0, 1
    while bit < count:
        place = place * 2 + code // bit % 2
        bit *= 2
    return place


def place_kernel(n_gy, *refs):
    blocks, (conv, down) = refs[: 2 * n_gy], refs[2 * n_gy :]
    me = lax.axis_index("gy")
    parity = lax.axis_index("gz") % 2
    half, channels = conv.shape[3:]
    count, deep_channels = down.shape[2:]
    for index, block in enumerate(blocks):
        side = jnp.bitwise_xor(parity, index // n_gy)
        column = jnp.bitwise_xor(me, index % n_gy)
        for k in range(27):
            conv[k, column, side] = block[pl.ds(k * half, half)]
        for wide in range(deep_channels // channels):
            down[side, column, :, pl.ds(wide * channels, channels)] = block[
                pl.ds(27 * half + wide * count, count)
            ]


def swapped(value, axis, code):
    return lax.ppermute(value, axis, [(i, i ^ code) for i in range(lax.axis_size(axis))])


def crossed(value, code_gz, code_gy):
    count = lax.axis_size("gy")
    pairs = [
        (i * count + j, (i ^ code_gz) * count + (j ^ code_gy))
        for i in range(lax.axis_size("gz"))
        for j in range(count)
    ]
    return lax.ppermute(value, ("gz", "gy"), pairs)


def even_pairs(value):
    return swapped(value, "gz", 1)


def odd_pairs(value):
    last = lax.axis_size("gz") - 1
    pairs = [(i + d, i + 1 - d) for i in range(1, last, 2) for d in range(2)]
    return lax.ppermute(value, "gz", pairs)


def exchanged(value, axis):
    return lax.all_to_all(value, axis, split_axis=0, concat_axis=0, tiled=True)


def per_device(
    level_input, pre_activation, conv_weight, down_weight, skip_cotangent, deep_cotangent
):
    n_gz = lax.axis_size("gz")
    n_gy = lax.axis_size("gy")
    _, rows, cols, channels = level_input.shape
    planes, deep_rows, deep_cols, share = deep_cotangent.shape
    deep_channels = down_weight.shape[4]
    parity = lax.axis_index("gz") % 2
    devices = n_gz * n_gy
    part = channels // n_gy
    cells = rows * cols
    deep_cells = deep_rows * deep_cols
    half = part // 2
    down_count = 4 * deep_channels // n_gy
    wire = BF16 if n_gz <= 8 else F32
    shape = jax.ShapeDtypeStruct

    level = level_input.reshape(cells, channels)
    deep = deep_cotangent.reshape(planes, deep_cells, share)
    if share % 16 == 0:
        keep, send = call(
            deep_kernel,
            [shape((planes // 2, share, deep_cells), BF16)] * 2,
            deep,
            scratch=[pltpu.VMEM((planes, share, deep_cells), BF16)],
        )
        code = planes
        held = jnp.stack([keep, swapped(send, "gz", code)], axis=1)
        while code > 2:
            code //= 2
            count = code // 2
            upper = lax.axis_index("gz") // code % 2
            keep = lax.dynamic_slice_in_dim(held, upper * count, count, axis=0)
            send = lax.dynamic_slice_in_dim(held, (1 - upper) * count, count, axis=0)
            held = jnp.concatenate([keep, swapped(send, "gz", code)], axis=1)
        deep_t = [held[0], swapped(held[0], "gz", 1)]
    else:
        deep_t = jnp.repeat(jnp.swapaxes(deep, 1, 2), 2, axis=0)
        deep_t = [exchanged(deep_t, "gz").reshape(deep_channels, deep_cells)]
    level_t = call(
        level_kernel,
        [shape((part, cells), BF16)] * n_gy,
        level,
        scratch=[pltpu.VMEM((n_gy, part, cells), BF16)],
    )
    level_t = [swapped(value, "gy", code) if code else value for code, value in enumerate(level_t)]
    level_t = jnp.stack(level_t)
    even = even_pairs(level_t)
    *deep_t, level_t = lax.optimization_barrier((*deep_t, level_t))
    down_slice = lax.dynamic_index_in_dim(down_weight, parity, 0, keepdims=False)
    grad, down, *others = call(
        lambda *refs: mask_kernel(n_gy, *refs),
        [shape((cells, channels), BF16), shape((down_count, channels), F32)]
        + [shape((down_count, channels), BF16)] * (n_gy - 1),
        pre_activation[0],
        skip_cotangent[0],
        down_slice,
        *deep_t,
        scratch=[
            pltpu.VMEM((deep_channels, deep_cells), BF16),
            pltpu.VMEM((n_gy, 4 * channels // n_gy, deep_channels), F32),
        ],
    )
    shared = [swapped(grad, "gy", code) if code else grad for code in range(n_gy)]
    shared[1], level_t = lax.optimization_barrier((shared[1], level_t))
    odd = odd_pairs(level_t)
    even, *others = lax.optimization_barrier((even, *others))
    for code, value in enumerate(others):
        down = down + swapped(value, "gy", code + 1).astype(F32)
    keep, send, near = call(
        lambda *refs: weight_kernel(n_gy, (rows, cols, channels), *refs),
        (
            shape((27 * half, channels), F32),
            shape((27 * half, channels), wire),
            shape((rows + 2, cols, channels), BF16),
        ),
        even,
        level_t,
        odd,
        *shared,
        scratch=[
            pltpu.VMEM((n_gy * rows + 2, cols, 3 * channels), BF16),
            pltpu.VMEM((n_gy, 3 * part, cells), BF16),
            pltpu.VMEM((2, 27 * half, channels), F32),
        ],
    )
    near_even, near_odd = even_pairs(near), odd_pairs(near)
    def rounded(value):
        return lax.optimization_barrier(value.astype(wire))

    def added(value, other):
        return value.astype(F32) + other.astype(F32)

    cell_total = devices * cells
    down = rounded(down)
    codes = []
    code = n_gz // 2
    while code > 1:
        codes.append(code)
        code //= 2
    send = swapped(send, "gz", 1)
    for index, code in enumerate(codes):
        down_other = swapped(down, "gz", code)
        if index == 0:
            conv = rounded(keep + send.astype(F32))
        else:
            conv_other = swapped(conv, "gz", codes[index - 1])
            if index == 1:
                tied = (conv_other, down_other, near_even, near_odd)
                conv_other, down_other, near_even, near_odd = lax.optimization_barrier(tied)
            conv = rounded(added(conv, conv_other))
        down = added(down, down_other)
        if index < len(codes) - 1:
            down = rounded(down)
    conv_other = swapped(conv, "gz", codes[-1])
    input_grad = call(
        input_kernel,
        shape((rows, cols, channels), BF16),
        near_even,
        near,
        near_odd,
        conv_weight,
    )
    conv_other, input_grad = lax.optimization_barrier((conv_other, input_grad))
    conv = added(conv, conv_other) * (1 / math.sqrt(cell_total))
    down = down * (1 / math.sqrt(cell_total // 8))
    total = jnp.concatenate([conv.astype(BF16), down.astype(BF16)], axis=0)
    if n_gy == 4:
        lines = [
            [total, swapped(total, "gy", 2)],
            [swapped(total, "gz", 1), crossed(total, 1, 2)],
        ]
        blocks = []
        for near_block, far_block in lines:
            blocks += [near_block, swapped(near_block, "gy", 1)]
            blocks += [far_block, swapped(far_block, "gy", 1)]
    else:
        blocks = [
            swapped(block, "gy", code) if code else block
            for block in (total, swapped(total, "gz", 1))
            for code in range(n_gy)
        ]
    conv_grad, down_grad = call(
        lambda *refs: place_kernel(n_gy, *refs),
        (
            shape((27, n_gy, 2, half, channels), BF16),
            shape((2, n_gy, 4 * channels // n_gy, deep_channels), BF16),
        ),
        *blocks,
    )
    return (
        input_grad[None],
        conv_grad.reshape(conv_weight.shape),
        down_grad.reshape(down_weight.shape),
    )


def solution(mesh):
    return jax.shard_map(
        per_device,
        mesh=mesh,
        in_specs=(
            P("gz", "gy", None, None),
            P("gz", "gy", None, None),
            P(),
            P(),
            P("gz", "gy", None, None),
            P(None, "gy", None, "gz"),
        ),
        out_specs=(P("gz", "gy", None, None), P(), P()),
        check_vma=False,
    )
```
